32 devices in a mesh: col: 16 (over z, x, core), row: 2 (over y).
Axes of the slice: x: 2, y: 2, z: 4, core: 2. Of those that a mesh axis runs over, the one named last changes fastest.
Arguments:
- inputs: bfloat16 [512, 8192], P('col', 'row'), may hold values from -6 to 6
- weight: bfloat16 [8192, 28672], P('row', 'col'), may hold values from -0.0625 to 0.0625
- adapter_down_factors: bfloat16 [16, 16, 8192], P(None, None, 'row'), may hold values from -0.06629126 to 0.06629126
- adapter_up_factors: bfloat16 [16, 16, 28672], P(None, None, 'col'), may hold values from -1.5 to 1.5
- magnitude: float32 [16, 28672], P(None, 'col'), may hold values from 0.5 to 2
- cotangent: bfloat16 [512, 28672], P('row', 'col'), may hold values from -6 to 6
- tenant: int32 [512], replicated, may hold values from 0 to 15, as said below
Outputs:
- output: bfloat16 [512, 28672], P('row', 'col')
- grad_inputs: bfloat16 [512, 8192], P('col', 'row')
- grad_b: float32 [16, 16, 28672], P(None, None, 'col')
- grad_m: float32 [16, 28672], P(None, 'col')
The draws below stay inside these ranges and needn't reach their ends.
Inputs may be any that keep to these rules, and one draw needn't show every extreme that they name: `tenant`: constant on each aligned block of 128 tokens; both 0 and 15 occur in every draw.
All inputs are finite; a program needn't handle non-finite values.
Results may differ from the reference program's by a relative error of at most 0.0051.
Values may be sent and summed in bfloat16 or wider, within the bound.
No kernel may reach another device: no remote copies, remote signals or barrier semaphores. Data moves between devices by JAX's collectives and lax.ppermute only.
A program may use at most 192 MiB of HBM per device.

```python
import math
import jax
import jax.numpy as jnp
from jax import lax

MODEL_WIDTH = 8192
HIDDEN_UNITS = 28672
TENANT_COUNT = 16
ADAPTER_RANK = 16
BLOCK = 128
TOKENS = 512


def draw_tenant(key, part):
    key = jax.random.fold_in(key, 7)
    nblocks = TOKENS // BLOCK
    first, second = jax.random.split(key)
    block_tenant_index = jax.random.randint(first, (nblocks,), 0, TENANT_COUNT)
    where_top = jax.random.randint(second, (), 0, nblocks)
    places = jnp.arange(nblocks)
    block_tenant_index = jnp.where(places == where_top, TENANT_COUNT - 1, block_tenant_index)
    block_tenant_index = jnp.where(places == (where_top + 1) % nblocks, 0, block_tenant_index)
    return jnp.repeat(block_tenant_index, BLOCK).astype(jnp.int32)


def combine_factors(common, own, strength, sign_key):
    signs = jax.random.randint(sign_key, (TENANT_COUNT, ADAPTER_RANK, 1), 0, 2).astype(jnp.float32) * 2.0 - 1.0
    loading = strength * signs
    mixed = loading * common + jnp.sqrt(1.0 - loading * loading) * own
    return mixed * float(MODEL_WIDTH) ** (-0.5)


def draw_adapter_down_factors(key, part):
    key = jax.random.fold_in(key, 11)
    first, second, third, fourth = jax.random.split(key, 4)
    common = jnp.clip(jax.random.normal(first, (TENANT_COUNT, 1, MODEL_WIDTH), jnp.float32), -4.0, 4.0)
    own = jnp.clip(jax.random.normal(second, (TENANT_COUNT, ADAPTER_RANK, MODEL_WIDTH), jnp.float32), -4.0, 4.0)
    strength = jax.random.uniform(third, (TENANT_COUNT, 1, 1), jnp.float32, 0.5, 0.8)
    return combine_factors(common, own, strength, fourth).astype(jnp.bfloat16)


def spiked(array, rng, source, target, shards_of, factor):
    owner, partner = [(jnp.arange(array.shape[axis_at]) // (array.shape[axis_at] // shards_of)).reshape([-1 if axis == axis_at else 1 for axis in range(array.ndim)]) for axis_at in (source, target)]
    chosen = jax.random.permutation(rng, shards_of)[partner]
    strong = (owner == chosen) | (owner == (partner + shards_of // 2) % shards_of)
    return jnp.where(strong, factor * array, array)


def shard_levels(stream_key, extent, pieces, least, high):
    level, own = 1.0, jax.random.fold_in(stream_key, 6)
    for position, parts in pieces:
        draws = jnp.exp(jax.random.uniform(jax.random.fold_in(own, position), (parts,), jnp.float32, least / len(pieces), high / len(pieces)))
        level = level * jnp.repeat(draws, extent[position] // parts).reshape([-1 if axis == position else 1 for axis in range(len(extent))])
    return level


def centred(stream_key, dims, spread, most, cuts=(), kind=jnp.bfloat16):
    values = jax.random.normal(stream_key, dims, jnp.float32) * spread
    if len(cuts) > 0:
        values = shard_levels(stream_key, dims, cuts, -0.22, 0.18) * values
    return jnp.clip(values, min=-most, max=most).astype(kind)


def gaussian_with(stream_key, extent, spread, reach, cuts, heavy, held_as=jnp.bfloat16):
    entries = spread * jax.random.normal(stream_key, extent, jnp.float32)
    if cuts:
        entries = entries * shard_levels(stream_key, extent, cuts, -0.22, 0.18)
    return jnp.clip(spiked(entries, jax.random.fold_in(stream_key, 3), *heavy), -reach, reach).astype(held_as)


def setup_inputs(seed: int = 0) -> dict:
    arg_keys = jax.random.split(jax.random.key(seed), 8)
    inputs = centred(arg_keys[0], (TOKENS, MODEL_WIDTH), 1.0, 6.0, ((0, 16), (1, 2)))
    weight = centred(arg_keys[1], (MODEL_WIDTH, HIDDEN_UNITS), MODEL_WIDTH ** -0.5, 0.0625, ((0, 2), (1, 16)))
    adapter_down_factors = draw_adapter_down_factors(jax.random.fold_in(arg_keys[7], 71), 0)
    adapter_up_factors = centred(arg_keys[3], (TENANT_COUNT, ADAPTER_RANK, HIDDEN_UNITS), ADAPTER_RANK ** -0.5, 1.5, ((2, 16),))
    magnitude = jnp.clip(jnp.exp(math.log(2.0) - 1.3862944 * jax.random.uniform(arg_keys[4], (TENANT_COUNT, HIDDEN_UNITS), jnp.float32) ** shard_levels(arg_keys[4], (TENANT_COUNT, HIDDEN_UNITS), ((1, 16),), -0.2, 0.2)), 0.5, 2.0)
    cotangent = gaussian_with(arg_keys[5], (TOKENS, HIDDEN_UNITS), 1.0, 6.0, ((0, 2), (1, 16)), (1, 0, 16, 2.0))
    tenant = draw_tenant(jax.random.fold_in(arg_keys[7], 71), 0)
    return {"inputs": inputs, "weight": weight, "adapter_down_factors": adapter_down_factors, "adapter_up_factors": adapter_up_factors, "magnitude": magnitude, "cotangent": cotangent, "tenant": tenant}


HIGH = lax.Precision.HIGHEST
EPS = 1e-06

def squared_column_norms(weight, adapter_down_factors, adapter_up_factors):
    tenant_number, rank_dimension, width_dimension = adapter_down_factors.shape
    wf = weight.astype(jnp.float32)
    wsq = lax.optimization_barrier(jnp.sum(wf * wf, axis=0))
    cross_product_term = jnp.dot(adapter_down_factors.reshape(tenant_number * rank_dimension, width_dimension), weight, preferred_element_type=jnp.float32).reshape(tenant_number, rank_dimension, -1)
    down_flat_view = adapter_down_factors.astype(jnp.float32)
    up_flat_view = adapter_up_factors.astype(jnp.float32)
    gram = jnp.einsum('trd,tsd->trs', down_flat_view, down_flat_view, precision=HIGH)
    quad = jnp.einsum('trj,trs,tsj->tj', up_flat_view, gram, up_flat_view, precision=HIGH)
    return wsq[None, :] + 2.0 * lax.optimization_barrier(jnp.sum(cross_product_term * up_flat_view, axis=1)) + quad

def reference(inputs, weight, adapter_down_factors, adapter_up_factors, magnitude, cotangent, tenant):
    tenant_number, rank_dimension, width_dimension = adapter_down_factors.shape
    onehot = (tenant[:, None] == jnp.arange(tenant_number, dtype=jnp.int32)[None, :]).astype(jnp.float32)
    mask = jnp.repeat(onehot, rank_dimension, axis=1)
    down_factor_flat = adapter_down_factors.reshape(tenant_number * rank_dimension, width_dimension)
    up_factor_flat = adapter_up_factors.reshape(tenant_number * rank_dimension, -1)
    contract = (((1,), (1,)), ((), ()))
    low_all = lax.dot_general(inputs, down_factor_flat, contract, preferred_element_type=jnp.float32)
    low_wide = (low_all * mask).astype(jnp.bfloat16)
    pre = jnp.dot(inputs, weight, preferred_element_type=jnp.float32) + jnp.dot(low_wide, up_factor_flat, preferred_element_type=jnp.float32)
    norm_squared_total = squared_column_norms(weight, adapter_down_factors, adapter_up_factors)
    scale = magnitude / jnp.sqrt(norm_squared_total + EPS)
    token_scale = jnp.dot(onehot, scale, precision=HIGH)
    output = (token_scale * pre).astype(jnp.bfloat16)
    gradient_scaled = (cotangent.astype(jnp.float32) * token_scale).astype(jnp.bfloat16)
    grad_b = jnp.dot(low_wide.T, gradient_scaled, preferred_element_type=jnp.float32).reshape(tenant_number, rank_dimension, -1)
    back_wide = lax.dot_general(gradient_scaled, up_factor_flat, contract, preferred_element_type=jnp.float32) * mask
    grad_inputs = lax.dot_general(gradient_scaled, weight, contract, preferred_element_type=jnp.float32)
    grad_inputs = grad_inputs + jnp.dot(back_wide, down_factor_flat.astype(jnp.float32), precision=HIGH)
    grad_inputs = grad_inputs.astype(jnp.bfloat16)
    product = cotangent.astype(jnp.float32) * output.astype(jnp.float32)
    grad_m = jnp.dot(onehot.T, product, precision=HIGH) / magnitude
    return (output, grad_inputs, grad_b, grad_m)
```

```python
import functools

import jax
import jax.numpy as jnp
from jax import lax
from jax.experimental import pallas as pl
from jax.experimental.pallas import tpu as pltpu
from jax.sharding import PartitionSpec as P

BLOCK = 128
EPS = 1e-06
HIGH = lax.Precision.HIGHEST
CHUNKS = 4
F32 = jnp.float32
BF16 = jnp.bfloat16
COST = pl.CostEstimate(flops=1000, bytes_accessed=1000, transcendentals=0)
LAST = (((1,), (1,)), ((), ()))
PARAMS = pltpu.CompilerParams(vmem_limit_bytes=40 * 1024 * 1024)


def cat_blocks(refs):
    return jnp.concatenate([ref[0] for ref in refs], axis=0)


def order_specs(deps):
    return [pl.BlockSpec(memory_space=pl.ANY)] * len(deps)


def column_block(cols):
    return 256 if cols % 256 == 0 else 128


def hi_lo(value, axis):
    hi = value.astype(BF16)
    lo = (value - hi.astype(F32)).astype(BF16)
    return jnp.concatenate([hi, lo], axis=axis)


def norm_body(nblk, rank, tenant_ref, w_ref, *refs):
    a_refs, up_refs = refs[:nblk], refs[nblk : 2 * nblk]
    nsq_ref, gram_ref = refs[2 * nblk :]
    depth, jb = w_ref.shape
    rows = nblk * rank

    @pl.when(pl.program_id(0) == 0)
    def _():
        a_all = cat_blocks(a_refs)
        gram = lax.dot_general(a_all, a_all, LAST, preferred_element_type=F32)
        row = lax.broadcasted_iota(jnp.int32, (rows, rows), 0) // rank
        col = lax.broadcasted_iota(jnp.int32, (rows, rows), 1) // rank
        gram_ref[...] = jnp.where(row == col, gram, 0.0)

    step = min(depth, 256)
    cross = jnp.zeros((rows, jb), F32)
    squares = jnp.zeros((8, jb), F32)
    for start in range(0, depth, step):
        w = w_ref[start : start + step, :]
        a_part = jnp.concatenate([ref[0, :, start : start + step] for ref in a_refs], axis=0)
        cross = cross + jnp.dot(a_part, w, preferred_element_type=F32)
        wf = w.astype(F32)
        squares = squares + jnp.sum((wf * wf).reshape(step // 8, 8, jb), axis=0)
    up = cat_blocks(up_refs).astype(F32)
    quad = jnp.dot(gram_ref[...], up, preferred_element_type=F32, precision=HIGH)
    mixed = jnp.sum((up * (2.0 * cross + quad)).reshape(nblk, rank, jb), axis=1)
    nsq_ref[...] = mixed + jnp.sum(squares, axis=0, keepdims=True)


def partial_norms(tenant, weight, down, up):
    depth, cols = weight.shape
    rank = down.shape[1]
    nblk = tenant.shape[0] // BLOCK
    jb = column_block(cols)

    def down_spec(b):
        return pl.BlockSpec((1, rank, depth), lambda j, t: (t[b * BLOCK], 0, 0))

    def up_spec(b):
        return pl.BlockSpec((1, rank, jb), lambda j, t: (t[b * BLOCK], 0, j))

    return pl.pallas_call(
        functools.partial(norm_body, nblk, rank),
        out_shape=jax.ShapeDtypeStruct((nblk, cols), F32),
        grid_spec=pltpu.PrefetchScalarGridSpec(
            num_scalar_prefetch=1,
            grid=(cols // jb,),
            in_specs=[pl.BlockSpec((depth, jb), lambda j, t: (0, j))]
            + [down_spec(b) for b in range(nblk)]
            + [up_spec(b) for b in range(nblk)],
            out_specs=pl.BlockSpec((nblk, jb), lambda j, t: (0, j)),
            scratch_shapes=[pltpu.VMEM((nblk * rank, nblk * rank), F32)],
        ),
        compiler_params=PARAMS,
        cost_estimate=COST,
        name="partial_norms",
    )(tenant, weight, *([down] * nblk), *([up] * nblk))


def scaled_body(nblk, rank, groups, tenant_ref, base_ref, *refs):
    cot_refs, refs = refs[:groups], refs[groups:]
    nsq_a, nsq_b, mag_ref = refs[:3]
    up_refs = refs[3 : 3 + nblk]
    scale_ref, sg_ref, back_ref = refs[-3:]
    for b in range(nblk):
        total = nsq_a[b : b + 1, :] + nsq_b[b : b + 1, :]
        mag = mag_ref[pl.ds(tenant_ref[b * BLOCK], 1), :]
        scale_ref[b : b + 1, :] = mag / jnp.sqrt(total + EPS)
    up_all = cat_blocks(up_refs)
    owner = lax.broadcasted_iota(jnp.int32, (BLOCK, nblk * rank), 1) // rank
    for g in range(groups):
        for i in range(cot_refs[g].shape[0] // BLOCK):
            b = base_ref[g] + i
            rows = pl.ds(pl.multiple_of(b * BLOCK, BLOCK), BLOCK)
            grad = cot_refs[g][i * BLOCK : (i + 1) * BLOCK, :].astype(F32)
            sg = (grad * scale_ref[pl.ds(b, 1), :]).astype(BF16)
            sg_ref[rows, :] = sg
            back = lax.dot_general(sg, up_all, LAST, preferred_element_type=F32)
            back_ref[rows, :] = hi_lo(jnp.where(owner == b, back, 0.0), 1)


def scaled_gradient(tenant, bases, cots, nsq_a, nsq_b, magnitude, up, deps):
    tokens = tenant.shape[0]
    nblk = tokens // BLOCK
    tenants, cols = magnitude.shape
    rank = up.shape[1]

    def whole(array):
        return pl.BlockSpec(array.shape, lambda i, t, s: (0,) * array.ndim)

    def up_spec(b):
        return pl.BlockSpec((1, rank, cols), lambda i, t, s: (t[b * BLOCK], 0, 0))

    shapes = (
        jax.ShapeDtypeStruct((nblk, cols), F32),
        jax.ShapeDtypeStruct((tokens, cols), BF16),
        jax.ShapeDtypeStruct((tokens, 2 * nblk * rank), BF16),
    )
    return pl.pallas_call(
        functools.partial(scaled_body, nblk, rank, len(cots)),
        out_shape=shapes,
        grid_spec=pltpu.PrefetchScalarGridSpec(
            num_scalar_prefetch=2,
            grid=(1,),
            in_specs=[whole(c) for c in cots]
            + [whole(nsq_a), whole(nsq_b), whole(magnitude)]
            + [up_spec(b) for b in range(nblk)]
            + order_specs(deps),
            out_specs=[whole(s) for s in shapes],
        ),
        compiler_params=PARAMS,
        cost_estimate=COST,
        name="scaled_gradient",
    )(tenant, bases, *cots, nsq_a, nsq_b, magnitude, *([up] * nblk), *deps)


def grad_body(nblk, rank, nz, tenant_ref, place_ref, sg_ref, back_ref, w_ref, *refs):
    a_refs = refs[:nblk]
    keep_ref, send_ref, sgp_ref, backp_ref = refs[-4:]
    tokens = sg_ref.shape[0]
    piece = tokens // (4 * nz)
    half = tokens // 2

    @pl.when(pl.program_id(0) == 0)
    def _():
        z, x, core = place_ref[0], place_ref[1], place_ref[2]
        for fc in range(2):
            for fx in range(2):
                for k in range(nz):
                    c = lax.rem(z + k, nz) * 4 + (x ^ fx) * 2 + (core ^ fc)
                    src = pl.ds(pl.multiple_of(c * piece, piece), piece)
                    at = ((fc * 2 + fx) * nz + k) * piece
                    sgp_ref[at : at + piece, :] = sg_ref[src, :]
                    backp_ref[at : at + piece, :] = back_ref[src, :]

    down = cat_blocks(a_refs)
    down = jnp.concatenate([down, down], axis=0)
    w = w_ref[...]
    for h, out in ((1, send_ref), (0, keep_ref)):
        rows = slice(h * half, (h + 1) * half)
        part = lax.dot_general(sgp_ref[rows, :], w, LAST, preferred_element_type=F32)
        part = part + jnp.dot(backp_ref[rows, :], down, preferred_element_type=F32)
        out[...] = part.astype(out.dtype)


def grad_chunk(tenant, place, sg, back, weight, down, nz, chunk, deps):
    depth, cols = weight.shape
    tokens = sg.shape[0]
    nblk = tokens // BLOCK
    rank = down.shape[1]
    size = depth // CHUNKS
    db = min(size, 512)
    steps = size // db

    def down_spec(b):
        return pl.BlockSpec((1, rank, db), lambda i, t, p: (t[b * BLOCK], 0, chunk * steps + i))

    return pl.pallas_call(
        functools.partial(grad_body, nblk, rank, nz),
        out_shape=(
            jax.ShapeDtypeStruct((tokens // 2, size), F32),
            jax.ShapeDtypeStruct((tokens // 2, size), BF16),
        ),
        grid_spec=pltpu.PrefetchScalarGridSpec(
            num_scalar_prefetch=2,
            grid=(steps,),
            in_specs=[
                pl.BlockSpec(sg.shape, lambda i, t, p: (0, 0)),
                pl.BlockSpec(back.shape, lambda i, t, p: (0, 0)),
                pl.BlockSpec((db, cols), lambda i, t, p: (chunk * steps + i, 0)),
            ]
            + [down_spec(b) for b in range(nblk)]
            + order_specs(deps),
            out_specs=[pl.BlockSpec((tokens // 2, db), lambda i, t, p: (0, i))] * 2,
            scratch_shapes=[pltpu.VMEM(sg.shape, BF16), pltpu.VMEM(back.shape, BF16)],
        ),
        compiler_params=PARAMS,
        cost_estimate=COST,
        name="grad_chunk",
    )(tenant, place, sg, back, weight, *([down] * nblk), *deps)


def add_core_body(keep_ref, recv_ref, *refs):
    mine_ref, send_ref = refs[-2:]
    half = mine_ref.shape[0]
    mine_ref[...] = keep_ref[:half, :] + recv_ref[:half, :].astype(F32)
    send_ref[...] = (keep_ref[half:, :] + recv_ref[half:, :].astype(F32)).astype(BF16)


def add_core(keep, recv, deps):
    rows, size = keep.shape
    return pl.pallas_call(
        add_core_body,
        out_shape=(
            jax.ShapeDtypeStruct((rows // 2, size), F32),
            jax.ShapeDtypeStruct((rows // 2, size), BF16),
        ),
        in_specs=[pl.BlockSpec(memory_space=pltpu.VMEM)] * 2 + order_specs(deps),
        compiler_params=PARAMS,
        cost_estimate=COST,
        name="add_core",
    )(keep, recv, *deps)


def add_x_body(keep_ref, recv_ref, *refs):
    nz = keep_ref.shape[0] // refs[-1].shape[0]
    outs = refs[-nz:]
    piece = outs[0].shape[0]
    for k in range(nz):
        rows = slice(k * piece, (k + 1) * piece)
        total = keep_ref[rows, :] + recv_ref[rows, :].astype(F32)
        outs[k][...] = total.astype(outs[k].dtype)


def add_x(keep, recv, nz, deps):
    rows, size = keep.shape
    return pl.pallas_call(
        add_x_body,
        out_shape=tuple(
            jax.ShapeDtypeStruct((rows // nz, size), BF16 if k else F32) for k in range(nz)
        ),
        in_specs=[pl.BlockSpec(memory_space=pltpu.VMEM)] * 2 + order_specs(deps),
        compiler_params=PARAMS,
        cost_estimate=COST,
        name="add_x",
    )(keep, recv, *deps)


def add_z_body(nz, *refs):
    out_ref = refs[-1]
    size = refs[0].shape[1]
    for chunk in range((len(refs) - 1) // nz):
        total = refs[chunk * nz][...]
        for k in range(1, nz):
            total = total + refs[chunk * nz + k][...].astype(F32)
        out_ref[:, chunk * size : (chunk + 1) * size] = total.astype(BF16)


def add_z(parts, nz):
    piece, size = parts[0].shape
    return pl.pallas_call(
        functools.partial(add_z_body, nz),
        out_shape=jax.ShapeDtypeStruct((piece, size * (len(parts) // nz)), BF16),
        in_specs=[pl.BlockSpec(memory_space=pltpu.VMEM)] * len(parts),
        compiler_params=PARAMS,
        cost_estimate=COST,
        name="add_z",
    )(*parts)


def forward_body(nb, rank, nz, tenant_ref, place_ref, w_ref, cot_ref, *refs):
    a_refs, up_refs = refs[:nb], refs[nb : 2 * nb]
    pieces = refs[2 * nb : 2 * nb + 4 * nz]
    part_ref, dot_ref, low_ref, x_ref, lowcat_ref, sem = refs[-6:]
    piece = pieces[0].shape[0]

    @pl.when(pl.program_id(0) == 0)
    def _():
        z, x, core, first = place_ref[0], place_ref[1], place_ref[2], place_ref[3]

        def each(act):
            for n in range(4 * nz):
                k, fx, fc = n // 4, (n // 2) % 2, n % 2
                b = lax.rem(z + (nz - k), nz) - first

                @pl.when(jnp.logical_and(b >= 0, b < nb))
                def _():
                    row = (b * 4 + (x ^ fx) * 2 + (core ^ fc)) * piece
                    rows = pl.ds(pl.multiple_of(row, piece), piece)
                    act(pltpu.make_async_copy(pieces[n], x_ref.at[rows, :], sem.at[n]))

        each(lambda copy: copy.start())
        each(lambda copy: copy.wait())
        low = lax.dot_general(cat_blocks(a_refs), x_ref[...], LAST, preferred_element_type=F32)
        owner = lax.broadcasted_iota(jnp.int32, low.shape, 0) // rank
        block = lax.broadcasted_iota(jnp.int32, low.shape, 1) // BLOCK
        low = jnp.where(owner == block, low, 0.0)
        low_ref[...] = jnp.sum(low.reshape(nb, rank, low.shape[1]), axis=0)
        hi = low.astype(BF16).astype(F32)
        lowcat_ref[...] = jnp.concatenate([hi, low - hi], axis=0).T.astype(BF16)

    up = cat_blocks(up_refs)
    up = jnp.concatenate([up, up], axis=0)
    part = jnp.dot(x_ref[...], w_ref[...], preferred_element_type=F32)
    part = part + jnp.dot(lowcat_ref[...], up, preferred_element_type=F32)
    part_ref[...] = part.astype(part_ref.dtype)
    product = part * cot_ref[...].astype(F32)
    dot_ref[...] = jnp.sum(product.reshape(nb, BLOCK, product.shape[1]), axis=1)


def forward_group(tenant, place, weight, cot, down, up, pieces, nz, out_dtype, deps):
    depth, cols = weight.shape
    rows = cot.shape[0]
    nb = rows // BLOCK
    rank = down.shape[1]
    jb = column_block(cols)

    def down_spec(b):
        return pl.BlockSpec((1, rank, depth), lambda j, t, p: (t[(p[3] + b) * BLOCK], 0, 0))

    def up_spec(b):
        return pl.BlockSpec((1, rank, jb), lambda j, t, p: (t[(p[3] + b) * BLOCK], 0, j))

    return pl.pallas_call(
        functools.partial(forward_body, nb, rank, nz),
        out_shape=(
            jax.ShapeDtypeStruct((rows, cols), out_dtype),
            jax.ShapeDtypeStruct((nb, cols), F32),
            jax.ShapeDtypeStruct((rank, rows), F32),
        ),
        grid_spec=pltpu.PrefetchScalarGridSpec(
            num_scalar_prefetch=2,
            grid=(cols // jb,),
            in_specs=[
                pl.BlockSpec((depth, jb), lambda j, t, p: (0, j)),
                pl.BlockSpec((rows, jb), lambda j, t, p: (0, j)),
            ]
            + [down_spec(b) for b in range(nb)]
            + [up_spec(b) for b in range(nb)]
            + [pl.BlockSpec(memory_space=pl.ANY)] * len(pieces)
            + order_specs(deps),
            out_specs=[
                pl.BlockSpec((rows, jb), lambda j, t, p: (0, j)),
                pl.BlockSpec((nb, jb), lambda j, t, p: (0, j)),
                pl.BlockSpec((rank, rows), lambda j, t, p: (0, 0)),
            ],
            scratch_shapes=[
                pltpu.VMEM((rows, depth), BF16),
                pltpu.VMEM((rows, 2 * nb * rank), BF16),
                pltpu.SemaphoreType.DMA((len(pieces),)),
            ],
        ),
        compiler_params=PARAMS,
        cost_estimate=COST,
        name="forward_group",
    )(tenant, place, weight, cot, *([down] * nb), *([up] * nb), *pieces, *deps)


def shards(inputs, weight, adapter_down_factors, adapter_up_factors, magnitude, cotangent, tenant):
    col_count, row_count = lax.axis_size("col"), lax.axis_size("row")
    nz = col_count // 4
    down, up = adapter_down_factors, adapter_up_factors
    tenant_number, rank, depth = down.shape
    cols = weight.shape[1]
    tokens = tenant.shape[0]
    nblk = tokens // BLOCK
    rows_row = tokens // row_count
    blocks_mine = rows_row // BLOCK
    col, row = lax.axis_index("col"), lax.axis_index("row")
    z, x, core = col >> 2, (col >> 1) & 1, col & 1

    def move(value, dz, fx, fc):
        perm = []
        for source in range(col_count):
            sz, sx, sc = source // 4, (source // 2) % 2, source % 2
            perm.append((source, ((sz + dz) % nz) * 4 + (sx ^ fx) * 2 + (sc ^ fc)))
        return lax.ppermute(value, "col", perm)

    def swap(value):
        return lax.ppermute(value, "row", [(0, 1), (1, 0)])

    pair = row_count == 2

    pieces = []
    for k in range(nz):
        base = inputs if k == 0 else move(inputs, k, 0, 0)
        flip = move(base, 0, 1, 0)
        pieces += [base, move(base, 0, 0, 1), flip, move(flip, 0, 0, 1)]

    if pair:
        cots = [cotangent, swap(cotangent)]
        bases = jnp.stack([row, 1 - row]).astype(jnp.int32) * blocks_mine
    else:
        cots = [lax.all_gather(cotangent, "row", axis=0, tiled=True)]
        bases = jnp.zeros((1,), jnp.int32)

    nsq = partial_norms(tenant, weight, down, up)
    if pair:
        nsq_a, nsq_b = nsq, swap(nsq)
    else:
        nsq_a = lax.psum(nsq, "row")
        nsq_b = jnp.zeros_like(nsq)
    scale, sg, back = scaled_gradient(tenant, bases, cots, nsq_a, nsq_b, magnitude, up, pieces[:3] + pieces[4::4])

    place = jnp.stack([z, x, core, 0 * z]).astype(jnp.int32)

    def grad(chunk, deps):
        return grad_chunk(tenant, place, sg, back, weight, down, nz, chunk, deps)

    def cross_core(made, deps):
        return add_core(made[0], move(made[1], 0, 0, 1), deps)

    def cross_x(made, deps):
        mine, *away = add_x(made[0], move(made[1], 0, 1, 0), nz, deps)
        return [mine] + [move(a, k + 1, 0, 0) for k, a in enumerate(away)], mine

    made, summed = [grad(0, pieces[5::4])], []
    for chunk in range(1, CHUNKS):
        last = [summed[-1][0]] if summed else [made[-1][0]] + pieces[6::4]
        made.append(grad(chunk, last))
        summed.append(cross_core(made[chunk - 1], [made[chunk][0]]))

    if pair:
        theirs, ours = [
            jnp.stack([z, x, core, first]).astype(jnp.int32)
            for first in ((1 - row) * blocks_mine, row * blocks_mine)
        ]
        away, dots_away, low_away = forward_group(
            tenant, theirs, weight, cots[1], down, up, pieces, nz, BF16, [summed[-1][0]]
        )
        arrived = swap(away)
        after = dots_away
    else:
        after = summed[-1][0]
    summed.append(cross_core(made[-1], [after]))
    finals, after = cross_x(summed[0], [summed[-1][0]])
    if pair:
        part, dots_here, low_here = forward_group(
            tenant, ours, weight, cots[0], down, up, pieces, nz, F32, [after]
        )
        pre = part + arrived.astype(F32)

        def ordered(here, there, axis):
            return jnp.where(
                row == 0,
                jnp.concatenate([here, there], axis=axis),
                jnp.concatenate([there, here], axis=axis),
            )

        dots = ordered(dots_here, dots_away, 0)
        low = ordered(low_here, low_away, 1)
        dots = dots + swap(dots)
        low = low + swap(low)
        after = dots_here
    else:
        part, dots, low = forward_group(
            tenant, place, weight, cots[0], down, up, pieces, nz, F32, [after]
        )
        pre = lax.psum_scatter(part, "row", scatter_dimension=0, tiled=True)
        dots, low = lax.psum((dots, low), "row")
        after = part
    for chunk in range(1, CHUNKS):
        more, after = cross_x(summed[chunk], [after])
        finals += more
    grad_inputs = add_z(finals, nz)

    scale_mine = lax.dynamic_slice_in_dim(scale, row * blocks_mine, blocks_mine, 0)
    output = (pre.reshape(blocks_mine, BLOCK, cols) * scale_mine[:, None, :]).astype(BF16)
    output = output.reshape(rows_row, cols)

    block_tenant = tenant.reshape(nblk, BLOCK)[:, 0]
    tenants = jnp.arange(tenant_number, dtype=jnp.int32)
    wide = jnp.where(
        (tenants[:, None] == tenant[None, :])[:, None, :], low.astype(BF16)[None], 0
    ).reshape(tenant_number * rank, tokens)
    grad_b = jnp.dot(wide, sg, preferred_element_type=F32)
    grad_b = grad_b.reshape(tenant_number, rank, cols)
    hit = (tenants[:, None] == block_tenant[None, :])[:, :, None]
    grad_m = jnp.sum(jnp.where(hit, (dots * scale)[None], 0.0), axis=1) / magnitude
    return (output, grad_inputs, grad_b, grad_m)


def solution(mesh):
    return jax.shard_map(
        shards,
        mesh=mesh,
        in_specs=(
            P("col", "row"),
            P("row", "col"),
            P(None, None, "row"),
            P(None, None, "col"),
            P(None, "col"),
            P("row", "col"),
            P(),
        ),
        out_specs=(P("row", "col"), P("col", "row"), P(None, None, "col"), P(None, "col")),
        check_vma=False,
    )
```

```python
import functools

import jax
import jax.numpy as jnp
from jax import lax
from jax.experimental import pallas as pl
from jax.experimental.pallas import tpu as pltpu
from jax.sharding import PartitionSpec as P

BLOCK = 128
EPS = 1e-06
HIGH = lax.Precision.HIGHEST
CHUNKS = 2
STEPS = 8
F32 = jnp.float32
BF16 = jnp.bfloat16
COST = pl.CostEstimate(flops=1000, bytes_accessed=1000, transcendentals=0)
LAST = (((1,), (1,)), ((), ()))
PARAMS = pltpu.CompilerParams(vmem_limit_bytes=24 * 1024 * 1024)


def cat_blocks(refs):
    return jnp.concatenate([ref[0] for ref in refs], axis=0)


def order_specs(deps):
    return [pl.BlockSpec(memory_space=pl.ANY)] * len(deps)


def same_block(array):
    return pl.BlockSpec(array.shape, lambda *args: (0,) * array.ndim)


def hi_lo(value, axis):
    hi = value.astype(BF16)
    lo = (value - hi.astype(F32)).astype(BF16)
    return jnp.concatenate([hi, lo], axis=axis)


def norm_body(nblk, rank, tenant_ref, w_ref, *refs):
    a_refs, up_refs = refs[:nblk], refs[nblk : 2 * nblk]
    nsq_ref, gram_ref, cross_ref, square_ref = refs[2 * nblk :]
    depth, cols = w_ref.shape

    @pl.when(pl.program_id(0) == 0)
    def _():
        gram_ref[...] = jnp.zeros_like(gram_ref)
        cross_ref[...] = jnp.zeros_like(cross_ref)
        square_ref[...] = jnp.zeros_like(square_ref)

    a_all = cat_blocks(a_refs)
    gram_ref[...] += lax.dot_general(a_all, a_all, LAST, preferred_element_type=F32)
    step = min(depth, 256)
    for start in range(0, depth, step):
        w = w_ref[start : start + step, :]
        cross_ref[...] += jnp.dot(a_all[:, start : start + step], w, preferred_element_type=F32)
        wf = w.astype(F32)
        square_ref[...] += jnp.sum((wf * wf).reshape(step // 8, 8, cols), axis=0)

    @pl.when(pl.program_id(0) == pl.num_programs(0) - 1)
    def _():
        gram = gram_ref[...]
        row = lax.broadcasted_iota(jnp.int32, gram.shape, 0) // rank
        col = lax.broadcasted_iota(jnp.int32, gram.shape, 1) // rank
        gram = jnp.where(row == col, gram, 0.0)
        up = cat_blocks(up_refs).astype(F32)
        quad = jnp.dot(gram, up, preferred_element_type=F32, precision=HIGH)
        mixed = (up * (2.0 * cross_ref[...] + quad)).reshape(nblk, rank, cols)
        nsq_ref[...] = jnp.sum(mixed, axis=1) + jnp.sum(square_ref[...], axis=0, keepdims=True)


def partial_norms(tenant, weight, down, up):
    depth, cols = weight.shape
    rank = down.shape[1]
    nblk = tenant.shape[0] // BLOCK
    db = depth // STEPS

    def down_spec(b):
        return pl.BlockSpec((1, rank, db), lambda i, t: (t[b * BLOCK], 0, i))

    def up_spec(b):
        return pl.BlockSpec((1, rank, cols), lambda i, t: (t[b * BLOCK], 0, 0))

    return pl.pallas_call(
        functools.partial(norm_body, nblk, rank),
        out_shape=jax.ShapeDtypeStruct((nblk, cols), F32),
        grid_spec=pltpu.PrefetchScalarGridSpec(
            num_scalar_prefetch=1,
            grid=(STEPS,),
            in_specs=[pl.BlockSpec((db, cols), lambda i, t: (i, 0))]
            + [down_spec(b) for b in range(nblk)]
            + [up_spec(b) for b in range(nblk)],
            out_specs=pl.BlockSpec((nblk, cols), lambda i, t: (0, 0)),
            scratch_shapes=[
                pltpu.VMEM((nblk * rank, nblk * rank), F32),
                pltpu.VMEM((nblk * rank, cols), F32),
                pltpu.VMEM((8, cols), F32),
            ],
        ),
        compiler_params=PARAMS,
        cost_estimate=COST,
        name="partial_norms",
    )(tenant, weight, *([down] * nblk), *([up] * nblk))


def scaled_body(nb, rank, tenant_ref, place_ref, cot_ref, nsq_a, nsq_b, mag_ref, *refs):
    up_refs = refs[:nb]
    scale_ref, sg_ref, back_ref = refs[-3:]
    first = place_ref[3]
    up_all = cat_blocks(up_refs)
    owner = lax.broadcasted_iota(jnp.int32, (BLOCK, nb * rank), 1) // rank
    for i in range(nb):
        b = first + i
        total = nsq_a[pl.ds(b, 1), :] + nsq_b[pl.ds(b, 1), :]
        scale = mag_ref[pl.ds(tenant_ref[b * BLOCK], 1), :] / jnp.sqrt(total + EPS)
        scale_ref[i : i + 1, :] = scale
        rows = slice(i * BLOCK, (i + 1) * BLOCK)
        sg = (cot_ref[rows, :].astype(F32) * scale).astype(BF16)
        sg_ref[rows, :] = sg
        back = lax.dot_general(sg, up_all, LAST, preferred_element_type=F32)
        back_ref[rows, :] = hi_lo(jnp.where(owner == i, back, 0.0), 1)


def scaled_gradient(tenant, place, cot, nsq_a, nsq_b, magnitude, up, deps):
    rows, cols = cot.shape
    nb = rows // BLOCK
    rank = up.shape[1]

    def up_spec(b):
        return pl.BlockSpec((1, rank, cols), lambda i, t, p: (t[(p[3] + b) * BLOCK], 0, 0))

    shapes = (
        jax.ShapeDtypeStruct((nb, cols), F32),
        jax.ShapeDtypeStruct((rows, cols), BF16),
        jax.ShapeDtypeStruct((rows, 2 * nb * rank), BF16),
    )
    return pl.pallas_call(
        functools.partial(scaled_body, nb, rank),
        out_shape=shapes,
        grid_spec=pltpu.PrefetchScalarGridSpec(
            num_scalar_prefetch=2,
            grid=(1,),
            in_specs=[same_block(a) for a in (cot, nsq_a, nsq_b, magnitude)]
            + [up_spec(b) for b in range(nb)]
            + order_specs(deps),
            out_specs=[same_block(s) for s in shapes],
        ),
        compiler_params=PARAMS,
        cost_estimate=COST,
        name="scaled_gradient",
    )(tenant, place, cot, nsq_a, nsq_b, magnitude, *([up] * nb), *deps)


def grad_body(nb, rank, tenant_ref, place_ref, sg_ref, back_ref, w_ref, *refs):
    a_refs = refs[:nb]
    keep_ref, send_ref, sgp_ref, backp_ref = refs[-4:]
    rows = sg_ref.shape[0]
    piece = BLOCK // 4
    half = rows // 2

    @pl.when(pl.program_id(0) == 0)
    def _():
        x, core = place_ref[1], place_ref[2]
        for fc in range(2):
            for fx in range(2):
                for b in range(nb):
                    c = b * 4 + (x ^ fx) * 2 + (core ^ fc)
                    src = pl.ds(pl.multiple_of(c * piece, piece), piece)
                    at = ((fc * 2 + fx) * nb + b) * piece
                    sgp_ref[at : at + piece, :] = sg_ref[src, :]
                    backp_ref[at : at + piece, :] = back_ref[src, :]

    down = cat_blocks(a_refs)
    down = jnp.concatenate([down, down], axis=0)
    part = lax.dot_general(sgp_ref[...], w_ref[...], LAST, preferred_element_type=F32)
    part = part + jnp.dot(backp_ref[...], down, preferred_element_type=F32)
    keep_ref[...] = part[:half, :]
    send_ref[...] = part[half:, :].astype(BF16)


def grad_chunk(tenant, place, sg, back, weight, down, chunk, deps):
    depth, cols = weight.shape
    rows = sg.shape[0]
    nb = rows // BLOCK
    rank = down.shape[1]
    size = depth // CHUNKS
    db = depth // STEPS
    steps = size // db

    def down_spec(b):
        return pl.BlockSpec(
            (1, rank, db), lambda i, t, p: (t[(p[3] + b) * BLOCK], 0, chunk * steps + i)
        )

    return pl.pallas_call(
        functools.partial(grad_body, nb, rank),
        out_shape=(
            jax.ShapeDtypeStruct((rows // 2, size), F32),
            jax.ShapeDtypeStruct((rows // 2, size), BF16),
        ),
        grid_spec=pltpu.PrefetchScalarGridSpec(
            num_scalar_prefetch=2,
            grid=(steps,),
            in_specs=[
                same_block(sg),
                same_block(back),
                pl.BlockSpec((db, cols), lambda i, t, p: (chunk * steps + i, 0)),
            ]
            + [down_spec(b) for b in range(nb)]
            + order_specs(deps),
            out_specs=[pl.BlockSpec((rows // 2, db), lambda i, t, p: (0, i))] * 2,
            scratch_shapes=[pltpu.VMEM(sg.shape, BF16), pltpu.VMEM(back.shape, BF16)],
        ),
        compiler_params=PARAMS,
        cost_estimate=COST,
        name="grad_chunk",
    )(tenant, place, sg, back, weight, *([down] * nb), *deps)


def add_core_body(keep_ref, recv_ref, *refs):
    mine_ref, send_ref = refs[-2:]
    half = mine_ref.shape[0]
    mine_ref[...] = keep_ref[:half, :] + recv_ref[:half, :].astype(F32)
    send_ref[...] = (keep_ref[half:, :] + recv_ref[half:, :].astype(F32)).astype(BF16)


def add_core(keep, recv, deps):
    rows, size = keep.shape
    return pl.pallas_call(
        add_core_body,
        out_shape=(
            jax.ShapeDtypeStruct((rows // 2, size), F32),
            jax.ShapeDtypeStruct((rows // 2, size), BF16),
        ),
        in_specs=[pl.BlockSpec(memory_space=pltpu.VMEM)] * 2 + order_specs(deps),
        compiler_params=PARAMS,
        cost_estimate=COST,
        name="add_core",
    )(keep, recv, *deps)


def add_x_body(groups, nz, place_ref, *refs):
    outs, total_ref = refs[-nz - 1 : -1], refs[-1]
    piece = outs[0].shape[0]
    z = place_ref[0]
    for g in range(groups):
        keep_ref, recv_ref = refs[2 * g : 2 * g + 2]
        rows = keep_ref.shape[0]
        first = pl.multiple_of(place_ref[3 + g] * piece, piece)
        total_ref[pl.ds(first, rows), :] = keep_ref[...] + recv_ref[...].astype(F32)
    for k in range(nz):
        at = pl.multiple_of(lax.rem(z + k, nz) * piece, piece)
        outs[k][...] = total_ref[pl.ds(at, piece), :].astype(outs[k].dtype)


def add_x(place, pairs, nz, deps):
    size = pairs[0][0].shape[1]
    piece = BLOCK // 4
    operands = [array for pair in pairs for array in pair]
    shapes = tuple(jax.ShapeDtypeStruct((piece, size), BF16 if k else F32) for k in range(nz))
    return pl.pallas_call(
        functools.partial(add_x_body, len(pairs), nz),
        out_shape=shapes,
        grid_spec=pltpu.PrefetchScalarGridSpec(
            num_scalar_prefetch=1,
            grid=(1,),
            in_specs=[same_block(a) for a in operands] + order_specs(deps),
            out_specs=[same_block(s) for s in shapes],
            scratch_shapes=[pltpu.VMEM((nz * piece, size), F32)],
        ),
        compiler_params=PARAMS,
        cost_estimate=COST,
        name="add_x",
    )(place, *operands, *deps)


def add_z_body(nz, *refs):
    out_ref = refs[-1]
    size = refs[0].shape[1]
    for chunk in range((len(refs) - 1) // nz):
        total = refs[chunk * nz][...]
        for k in range(1, nz):
            total = total + refs[chunk * nz + k][...].astype(F32)
        out_ref[:, chunk * size : (chunk + 1) * size] = total.astype(BF16)


def add_z(parts, nz):
    piece, size = parts[0].shape
    return pl.pallas_call(
        functools.partial(add_z_body, nz),
        out_shape=jax.ShapeDtypeStruct((piece, size * (len(parts) // nz)), BF16),
        in_specs=[pl.BlockSpec(memory_space=pltpu.VMEM)] * len(parts),
        compiler_params=PARAMS,
        cost_estimate=COST,
        name="add_z",
    )(*parts)


def forward_body(nb, rank, nz, tenant_ref, place_ref, w_ref, cot_ref, *refs):
    a_refs, up_refs = refs[:nb], refs[nb : 2 * nb]
    pieces = refs[2 * nb : 2 * nb + 2 * nz + 2]
    part_ref, dot_ref, low_ref, x_ref, acc_ref, lowacc_ref, sem = refs[-7:]
    piece = BLOCK // 4
    db = w_ref.shape[0]
    step = pl.program_id(0)

    @pl.when(step == 0)
    def _():
        z, x, core, first = place_ref[0], place_ref[1], place_ref[2], place_ref[3]

        def each(act):
            for n in range(4 * nz):
                k, fx, fc = n // 4, (n // 2) % 2, n % 2
                src = pieces[2 * nz + fx].at[pl.ds(k * piece, piece), :] if fc else pieces[2 * k + fx]
                b = lax.rem(z + (nz - k), nz) - first

                @pl.when(jnp.logical_and(b >= 0, b < nb))
                def _():
                    row = (b * 4 + (x ^ fx) * 2 + (core ^ fc)) * piece
                    rows = pl.ds(pl.multiple_of(row, piece), piece)
                    act(pltpu.make_async_copy(src, x_ref.at[rows, :], sem.at[n]))

        each(lambda copy: copy.start())
        acc_ref[...] = jnp.zeros_like(acc_ref)
        lowacc_ref[...] = jnp.zeros_like(lowacc_ref)
        each(lambda copy: copy.wait())

    xs = x_ref[:, pl.ds(pl.multiple_of(step * db, db), db)]
    acc_ref[...] += jnp.dot(xs, w_ref[...], preferred_element_type=F32)
    lowacc_ref[...] += lax.dot_general(cat_blocks(a_refs), xs, LAST, preferred_element_type=F32)

    @pl.when(step == pl.num_programs(0) - 1)
    def _():
        low = lowacc_ref[...]
        owner = lax.broadcasted_iota(jnp.int32, low.shape, 0) // rank
        block = lax.broadcasted_iota(jnp.int32, low.shape, 1) // BLOCK
        low = jnp.where(owner == block, low, 0.0)
        low_ref[...] = jnp.sum(low.reshape(nb, rank, low.shape[1]), axis=0)
        hi = low.astype(BF16).astype(F32)
        lowcat = jnp.concatenate([hi, low - hi], axis=0).T.astype(BF16)
        up = cat_blocks(up_refs)
        up = jnp.concatenate([up, up], axis=0)
        for i in range(nb):
            rows = slice(i * BLOCK, (i + 1) * BLOCK)
            part = acc_ref[rows, :] + jnp.dot(lowcat[rows, :], up, preferred_element_type=F32)
            part_ref[rows, :] = part.astype(part_ref.dtype)
            product = part * cot_ref[rows, :].astype(F32)
            dot_ref[i : i + 1, :] = jnp.sum(product, axis=0, keepdims=True)


def forward_group(tenant, place, weight, cot, down, up, pieces, nz, out_dtype, deps):
    depth, cols = weight.shape
    rows = cot.shape[0]
    nb = rows // BLOCK
    rank = down.shape[1]
    db = depth // STEPS

    def down_spec(b):
        return pl.BlockSpec((1, rank, db), lambda i, t, p: (t[(p[3] + b) * BLOCK], 0, i))

    def up_spec(b):
        return pl.BlockSpec((1, rank, cols), lambda i, t, p: (t[(p[3] + b) * BLOCK], 0, 0))

    shapes = (
        jax.ShapeDtypeStruct((rows, cols), out_dtype),
        jax.ShapeDtypeStruct((nb, cols), F32),
        jax.ShapeDtypeStruct((rank, rows), F32),
    )
    return pl.pallas_call(
        functools.partial(forward_body, nb, rank, nz),
        out_shape=shapes,
        grid_spec=pltpu.PrefetchScalarGridSpec(
            num_scalar_prefetch=2,
            grid=(STEPS,),
            in_specs=[pl.BlockSpec((db, cols), lambda i, t, p: (i, 0)), same_block(cot)]
            + [down_spec(b) for b in range(nb)]
            + [up_spec(b) for b in range(nb)]
            + [pl.BlockSpec(memory_space=pl.ANY)] * len(pieces)
            + order_specs(deps),
            out_specs=[same_block(s) for s in shapes],
            scratch_shapes=[
                pltpu.VMEM((rows, depth), BF16),
                pltpu.VMEM((rows, cols), F32),
                pltpu.VMEM((nb * rank, rows), F32),
                pltpu.SemaphoreType.DMA((4 * nz,)),
            ],
        ),
        compiler_params=PARAMS,
        cost_estimate=COST,
        name="forward_group",
    )(tenant, place, weight, cot, *([down] * nb), *([up] * nb), *pieces, *deps)


def shards(inputs, weight, adapter_down_factors, adapter_up_factors, magnitude, cotangent, tenant):
    col_count, row_count = lax.axis_size("col"), lax.axis_size("row")
    nz = col_count // 4
    down, up = adapter_down_factors, adapter_up_factors
    tenant_number, rank, depth = down.shape
    cols = weight.shape[1]
    tokens = tenant.shape[0]
    nblk = tokens // BLOCK
    rows_row = tokens // row_count
    blocks_mine = rows_row // BLOCK
    col, row = lax.axis_index("col"), lax.axis_index("row")
    z, x, core = col >> 2, (col >> 1) & 1, col & 1

    def move(value, dz, fx, fc):
        perm = []
        for source in range(col_count):
            sz, sx, sc = source // 4, (source // 2) % 2, source % 2
            perm.append((source, ((sz + dz) % nz) * 4 + (sx ^ fx) * 2 + (sc ^ fc)))
        return lax.ppermute(value, "col", perm)

    def swap(value):
        return lax.ppermute(value, "row", [(0, 1), (1, 0)])

    def place(*firsts):
        return jnp.stack([z, x, core, *firsts]).astype(jnp.int32)

    pair = row_count == 2

    along_z = [inputs] + [move(inputs, k, 0, 0) for k in range(1, nz)]
    own, _ = lax.optimization_barrier((inputs, along_z[-1]))
    along_x = [move(piece, 0, 1, 0) for piece in [own] + along_z[1:]]
    pieces = [piece for both in zip(along_z, along_x) for piece in both]
    pieces += [move(jnp.concatenate(part, axis=0), 0, 0, 1) for part in (along_z, along_x)]

    nsq = partial_norms(tenant, weight, down, up)
    if pair:
        nsq_a, nsq_b = nsq, swap(nsq)
        firsts = [row * blocks_mine, (1 - row) * blocks_mine]
        cots = [cotangent, swap(cotangent)]
    else:
        nsq_a, nsq_b = lax.psum(nsq, "row"), jnp.zeros_like(nsq)
        firsts = [0 * row]
        cots = [lax.all_gather(cotangent, "row", axis=0, tiled=True)]
    places = [place(first) for first in firsts]

    def scaled(g, deps):
        return scaled_gradient(tenant, places[g], cots[g], nsq_a, nsq_b, magnitude, up, deps)

    def grad(g, part, chunk, deps):
        return grad_chunk(tenant, places[g], part[1], part[2], weight, down, chunk, deps)

    def cross_core(made, deps):
        return add_core(made[0], move(made[1], 0, 0, 1), deps)

    def cross_x(made, deps):
        pairs = [(mine, move(away, 0, 1, 0)) for mine, away in made]
        mine, *away = add_x(place(*firsts), pairs, nz, deps)
        return [mine] + [move(a, k + 1, 0, 0) for k, a in enumerate(away)], mine

    def forward(g, out_dtype, deps):
        return forward_group(
            tenant, places[g], weight, cots[g], down, up, pieces, nz, out_dtype, deps
        )

    if pair:
        ours = scaled(0, [])
        made = [grad(0, ours, 0, along_z[3:])]
        made += [grad(0, ours, 1, [made[0][0], cots[1]] + along_z[1:2])]
        theirs = scaled(1, [made[1][0]] + along_z[2:3])
        near = [cross_core(made[0], [theirs[0]])]
        far = [grad(1, theirs, 0, [near[0][0]] + along_x[1:2] + along_x[3:])]
        near += [cross_core(made[1], [far[0][0]])]
        far += [grad(1, theirs, 1, [near[1][0]] + along_x[2:3])]
        done = [cross_core(far[0], [far[1][0]])]
        away, dots_away, low_away = forward(1, BF16, [done[0][0]])
        arrived = swap(away)
        done += [cross_core(far[1], [dots_away])]
        finals, after = cross_x([near[0], done[0]], [done[1][0]])
        part, dots_here, low_here = forward(0, F32, [after])
        more, after = cross_x([near[1], done[1]], [dots_here])
        finals += more
        pre = part + arrived.astype(F32)
        dots = [dots_here, dots_away]
        low = [low_here, low_away]
        dots_new = swap(jnp.concatenate(dots[::-1], axis=0))
        low_new = swap(jnp.concatenate(low[::-1], axis=1))
        dots = jnp.concatenate(dots, axis=0) + dots_new
        low = jnp.concatenate(low, axis=1) + low_new
        parts = [ours, theirs]
    else:
        ours = scaled(0, [])
        near = [cross_core(grad(0, ours, chunk, []), []) for chunk in range(CHUNKS)]
        part, dots, low = forward(0, F32, [])
        finals = []
        for chunk in range(CHUNKS):
            finals += cross_x([near[chunk]], [])[0]
        pre = lax.psum_scatter(part, "row", scatter_dimension=0, tiled=True)
        dots, low = lax.psum((dots, low), "row")
        parts = [ours]

    grad_inputs = add_z(finals, nz)
    scales = jnp.concatenate([part[0] for part in parts], axis=0)
    if pair:
        scale_mine = parts[0][0]
    else:
        scale_mine = lax.dynamic_slice_in_dim(scales, row * blocks_mine, blocks_mine, 0)
    output = (pre.reshape(blocks_mine, BLOCK, cols) * scale_mine[:, None, :]).astype(BF16)
    output = output.reshape(rows_row, cols)

    tenants = jnp.arange(tenant_number, dtype=jnp.int32)
    block_tenant = tenant.reshape(nblk, BLOCK)[:, 0]
    size = nblk // len(parts)
    owners = jnp.concatenate(
        [lax.dynamic_slice_in_dim(block_tenant, first, size, 0) for first in firsts]
    )
    low = low.astype(BF16)
    grad_b = 0.0
    for g, made in enumerate(parts):
        owner = jnp.repeat(owners[g * size : (g + 1) * size], BLOCK)
        mine = low[:, g * size * BLOCK : (g + 1) * size * BLOCK]
        wide = jnp.where((tenants[:, None] == owner[None, :])[:, None, :], mine[None], 0)
        wide = wide.reshape(tenant_number * rank, size * BLOCK)
        grad_b = grad_b + jnp.dot(wide, made[1], preferred_element_type=F32)
    grad_b = grad_b.reshape(tenant_number, rank, cols)
    hit = (tenants[:, None] == owners[None, :])[:, :, None]
    terms = jnp.where(hit, (dots * scales)[None], 0.0)
    grad_m = 0.0
    for g in range(len(parts)):
        group = terms[:, g * size : (g + 1) * size]
        grad_m = grad_m + functools.reduce(jnp.add, [group[:, i] for i in range(size)])
    return (output, grad_inputs, grad_b, grad_m / magnitude)


def solution(mesh):
    return jax.shard_map(
        shards,
        mesh=mesh,
        in_specs=(
            P("col", "row"),
            P("row", "col"),
            P(None, None, "row"),
            P(None, None, "col"),
            P(None, "col"),
            P("row", "col"),
            P(),
        ),
        out_specs=(P("row", "col"), P("col", "row"), P(None, None, "col"), P(None, "col")),
        check_vma=False,
    )
```

```python
import functools

import jax
import jax.numpy as jnp
from jax import lax
from jax.experimental import pallas as pl
from jax.experimental.pallas import tpu as pltpu
from jax.sharding import PartitionSpec as P

BLOCK = 128
EPS = 1e-06
HIGH = lax.Precision.HIGHEST
CHUNKS = 2
STEPS = 8
F32 = jnp.float32
BF16 = jnp.bfloat16
COST = pl.CostEstimate(flops=1000, bytes_accessed=1000, transcendentals=0)
LAST = (((1,), (1,)), ((), ()))
PARAMS = pltpu.CompilerParams(vmem_limit_bytes=52 * 1024 * 1024)
IN_HBM = pl.BlockSpec(memory_space=pltpu.HBM)


def order_specs(deps):
    return [pl.BlockSpec(memory_space=pl.ANY)] * len(deps)


def same_block(array):
    return pl.BlockSpec(array.shape, lambda *args: (0,) * array.ndim)


def hi_lo(value, axis):
    hi = value.astype(BF16)
    lo = (value - hi.astype(F32)).astype(BF16)
    return jnp.concatenate([hi, lo], axis=axis)


def weight_copy(w_hbm, w_ref, sem, i, first=0):
    db = w_ref.shape[0] // sem.shape[0]
    src = pl.ds(pl.multiple_of((first + i) * db, db), db)
    dst = pl.ds(pl.multiple_of(i * db, db), db)
    return pltpu.make_async_copy(w_hbm.at[src, :], w_ref.at[dst, :], sem.at[i])


def factor_copies(tenant_ref, first, hbm, ref, sem, at, columns=None):
    rank, nblk = hbm.shape[1], tenant_ref.shape[0] // BLOCK
    copies = []
    for b in range(ref.shape[0] // rank):
        src = hbm.at[tenant_ref[lax.rem(first + b, nblk) * BLOCK]]
        if columns is not None:
            src = src.at[:, columns]
        dst = ref.at[pl.ds(b * rank, rank), :]
        copies.append(pltpu.make_async_copy(src, dst, sem.at[at + b]))
    return copies


def norm_body(nblk, rank, tenant_ref, w_hbm, a_hbm, up_hbm, nsq_ref, *refs):
    w_ref, a_ref, up_ref, cross_ref, square_ref, w_sem, sem = refs
    cols = w_ref.shape[1]
    db = w_ref.shape[0] // STEPS
    copies = factor_copies(tenant_ref, 0, a_hbm, a_ref, sem, 0)
    late = factor_copies(tenant_ref, 0, up_hbm, up_ref, sem, nblk)
    for copy in copies:
        copy.start()
    for i in range(STEPS):
        weight_copy(w_hbm, w_ref, w_sem, i).start()
    for copy in late:
        copy.start()
    cross_ref[...] = jnp.zeros_like(cross_ref)
    square_ref[...] = jnp.zeros_like(square_ref)
    for copy in copies:
        copy.wait()
    step = min(db, 256)

    def block(i, carry):
        weight_copy(w_hbm, w_ref, w_sem, i).wait()
        for start in range(0, db, step):
            rows = pl.ds(pl.multiple_of(i * db + start, step), step)
            w = w_ref[rows, :]
            cross_ref[...] += jnp.dot(a_ref[:, rows], w, preferred_element_type=F32)
            wf = w.astype(F32)
            square_ref[...] += jnp.sum((wf * wf).reshape(step // 8, 8, cols), axis=0)
        return carry

    lax.fori_loop(0, STEPS, block, 0)
    for copy in late:
        copy.wait()
    gram = lax.dot_general(a_ref[...], a_ref[...], LAST, preferred_element_type=F32)
    row = lax.broadcasted_iota(jnp.int32, gram.shape, 0) // rank
    col = lax.broadcasted_iota(jnp.int32, gram.shape, 1) // rank
    gram = jnp.where(row == col, gram, 0.0)
    up = up_ref[...].astype(F32)
    quad = jnp.dot(gram, up, preferred_element_type=F32, precision=HIGH)
    mixed = (up * (2.0 * cross_ref[...] + quad)).reshape(nblk, rank, cols)
    nsq_ref[...] = jnp.sum(mixed, axis=1) + jnp.sum(square_ref[...], axis=0, keepdims=True)


def partial_norms(tenant, weight, down, up):
    depth, cols = weight.shape
    rank = down.shape[1]
    nblk = tenant.shape[0] // BLOCK
    shape = jax.ShapeDtypeStruct((nblk, cols), F32)
    return pl.pallas_call(
        functools.partial(norm_body, nblk, rank),
        out_shape=shape,
        grid_spec=pltpu.PrefetchScalarGridSpec(
            num_scalar_prefetch=1,
            grid=(1,),
            in_specs=[IN_HBM] * 3,
            out_specs=same_block(shape),
            scratch_shapes=[
                pltpu.VMEM((depth, cols), BF16),
                pltpu.VMEM((nblk * rank, depth), BF16),
                pltpu.VMEM((nblk * rank, cols), BF16),
                pltpu.VMEM((nblk * rank, cols), F32),
                pltpu.VMEM((8, cols), F32),
                pltpu.SemaphoreType.DMA((STEPS,)),
                pltpu.SemaphoreType.DMA((2 * nblk,)),
            ],
        ),
        compiler_params=PARAMS,
        cost_estimate=COST,
        name="partial_norms",
    )(tenant, weight, down, up)


def scaled_body(nb, rank, tenant_ref, place_ref, cot_ref, nsq_a, nsq_b, mag_ref, up_hbm, *refs):
    scale_ref, sg_ref, back_ref, up_ref, sem = refs[-5:]
    first = place_ref[3]
    copies = factor_copies(tenant_ref, first, up_hbm, up_ref, sem, 0)
    for copy in copies:
        copy.start()
    for i in range(nb):
        b = first + i
        total = nsq_a[pl.ds(b, 1), :] + nsq_b[pl.ds(b, 1), :]
        scale = mag_ref[pl.ds(tenant_ref[b * BLOCK], 1), :] / jnp.sqrt(total + EPS)
        scale_ref[i : i + 1, :] = scale
        rows = slice(i * BLOCK, (i + 1) * BLOCK)
        sg_ref[rows, :] = (cot_ref[rows, :].astype(F32) * scale).astype(BF16)
    for copy in copies:
        copy.wait()
    back = lax.dot_general(sg_ref[...], up_ref[...], LAST, preferred_element_type=F32)
    block = lax.broadcasted_iota(jnp.int32, back.shape, 0) // BLOCK
    owner = lax.broadcasted_iota(jnp.int32, back.shape, 1) // rank
    back_ref[...] = hi_lo(jnp.where(owner == block, back, 0.0), 1)


def scaled_gradient(tenant, place, cot, nsq_a, nsq_b, magnitude, up, deps):
    rows, cols = cot.shape
    nb = rows // BLOCK
    rank = up.shape[1]
    shapes = (
        jax.ShapeDtypeStruct((nb, cols), F32),
        jax.ShapeDtypeStruct((rows, cols), BF16),
        jax.ShapeDtypeStruct((rows, 2 * nb * rank), BF16),
    )
    return pl.pallas_call(
        functools.partial(scaled_body, nb, rank),
        out_shape=shapes,
        grid_spec=pltpu.PrefetchScalarGridSpec(
            num_scalar_prefetch=2,
            grid=(1,),
            in_specs=[same_block(a) for a in (cot, nsq_a, nsq_b, magnitude)]
            + [IN_HBM]
            + order_specs(deps),
            out_specs=[same_block(s) for s in shapes],
            scratch_shapes=[
                pltpu.VMEM((nb * rank, cols), BF16),
                pltpu.SemaphoreType.DMA((nb,)),
            ],
        ),
        compiler_params=PARAMS,
        cost_estimate=COST,
        name="scaled_gradient",
    )(tenant, place, cot, nsq_a, nsq_b, magnitude, up, *deps)


def grad_body(nb, rank, chunk, tenant_ref, place_ref, sg_ref, back_ref, w_hbm, a_hbm, *refs):
    keep_ref, send_ref, w_ref, a_ref, sgp_ref, backp_ref, w_sem, sem = refs[-8:]
    rows, size = sg_ref.shape[0], w_ref.shape[0]
    steps = w_sem.shape[0]
    db = size // steps
    piece = BLOCK // 4
    half = rows // 2
    for i in range(steps):
        weight_copy(w_hbm, w_ref, w_sem, i, chunk * steps).start()
    columns = pl.ds(chunk * size, size)
    copies = factor_copies(tenant_ref, place_ref[3], a_hbm, a_ref, sem, 0, columns)
    for copy in copies:
        copy.start()
    x, core = place_ref[1], place_ref[2]
    for fc in range(2):
        for fx in range(2):
            for b in range(nb):
                c = b * 4 + (x ^ fx) * 2 + (core ^ fc)
                src = pl.ds(pl.multiple_of(c * piece, piece), piece)
                at = ((fc * 2 + fx) * nb + b) * piece
                sgp_ref[at : at + piece, :] = sg_ref[src, :]
                backp_ref[at : at + piece, :] = back_ref[src, :]
    for copy in copies:
        copy.wait()

    def block(i, carry):
        weight_copy(w_hbm, w_ref, w_sem, i, chunk * steps).wait()
        at = pl.ds(pl.multiple_of(i * db, db), db)
        down = a_ref[:, at]
        down = jnp.concatenate([down, down], axis=0)
        part = lax.dot_general(sgp_ref[...], w_ref[at, :], LAST, preferred_element_type=F32)
        part = part + jnp.dot(backp_ref[...], down, preferred_element_type=F32)
        keep_ref[:, at] = part[:half, :]
        send_ref[:, at] = part[half:, :].astype(BF16)
        return carry

    lax.fori_loop(0, steps, block, 0)


def grad_chunk(tenant, place, sg, back, weight, down, chunk, deps):
    depth, cols = weight.shape
    rows = sg.shape[0]
    nb = rows // BLOCK
    rank = down.shape[1]
    size = depth // CHUNKS
    shapes = (
        jax.ShapeDtypeStruct((rows // 2, size), F32),
        jax.ShapeDtypeStruct((rows // 2, size), BF16),
    )
    return pl.pallas_call(
        functools.partial(grad_body, nb, rank, chunk),
        out_shape=shapes,
        grid_spec=pltpu.PrefetchScalarGridSpec(
            num_scalar_prefetch=2,
            grid=(1,),
            in_specs=[same_block(sg), same_block(back), IN_HBM, IN_HBM] + order_specs(deps),
            out_specs=[same_block(s) for s in shapes],
            scratch_shapes=[
                pltpu.VMEM((size, cols), BF16),
                pltpu.VMEM((nb * rank, size), BF16),
                pltpu.VMEM(sg.shape, BF16),
                pltpu.VMEM(back.shape, BF16),
                pltpu.SemaphoreType.DMA((STEPS // CHUNKS,)),
                pltpu.SemaphoreType.DMA((nb,)),
            ],
        ),
        compiler_params=PARAMS,
        cost_estimate=COST,
        name="grad_chunk",
    )(tenant, place, sg, back, weight, down, *deps)


def add_core_body(chunks, *refs):
    mine_ref, send_ref = refs[-2:]
    half = mine_ref.shape[0]
    for c in range(chunks):
        keep_ref, recv_ref = refs[2 * c : 2 * c + 2]
        size = keep_ref.shape[1]
        at = slice(c * size, (c + 1) * size)
        mine_ref[:, at] = keep_ref[:half, :] + recv_ref[:half, :].astype(F32)
        send_ref[:, at] = (keep_ref[half:, :] + recv_ref[half:, :].astype(F32)).astype(BF16)


def add_core(pairs, deps):
    rows, size = pairs[0][0].shape
    operands = [array for pair in pairs for array in pair]
    shape = (rows // 2, size * len(pairs))
    return pl.pallas_call(
        functools.partial(add_core_body, len(pairs)),
        out_shape=(jax.ShapeDtypeStruct(shape, F32), jax.ShapeDtypeStruct(shape, BF16)),
        in_specs=[pl.BlockSpec(memory_space=pltpu.VMEM)] * len(operands) + order_specs(deps),
        compiler_params=PARAMS,
        cost_estimate=COST,
        name="add_core",
    )(*operands, *deps)


def add_x_body(counts, nz, place_ref, *refs):
    outs, total_ref = refs[-nz - 1 : -1], refs[-1]
    piece = outs[0].shape[0]
    z = place_ref[0]
    n = 0
    for g, count in enumerate(counts):
        for c in range(count):
            keep_ref, recv_ref = refs[2 * n : 2 * n + 2]
            n += 1
            rows, size = keep_ref.shape
            first = pl.multiple_of(place_ref[3 + g] * piece, piece)
            total = keep_ref[...] + recv_ref[...].astype(F32)
            total_ref[pl.ds(first, rows), c * size : (c + 1) * size] = total
    for k in range(nz):
        at = pl.multiple_of(lax.rem(z + k, nz) * piece, piece)
        outs[k][...] = total_ref[pl.ds(at, piece), :].astype(outs[k].dtype)


def add_x(place, groups, nz, deps):
    piece = BLOCK // 4
    size = sum(pair[0].shape[1] for pair in groups[0])
    operands = [array for group in groups for pair in group for array in pair]
    shapes = tuple(jax.ShapeDtypeStruct((piece, size), BF16 if k else F32) for k in range(nz))
    return pl.pallas_call(
        functools.partial(add_x_body, [len(group) for group in groups], nz),
        out_shape=shapes,
        grid_spec=pltpu.PrefetchScalarGridSpec(
            num_scalar_prefetch=1,
            grid=(1,),
            in_specs=[same_block(a) for a in operands] + order_specs(deps),
            out_specs=[same_block(s) for s in shapes],
            scratch_shapes=[pltpu.VMEM((nz * piece, size), F32)],
        ),
        compiler_params=PARAMS,
        cost_estimate=COST,
        name="add_x",
    )(place, *operands, *deps)


def add_z_body(nz, *refs):
    out_ref = refs[-1]
    size = refs[0].shape[1]
    for chunk in range((len(refs) - 1) // nz):
        total = refs[chunk * nz][...]
        for k in range(1, nz):
            total = total + refs[chunk * nz + k][...].astype(F32)
        out_ref[:, chunk * size : (chunk + 1) * size] = total.astype(BF16)


def add_z(parts, nz):
    piece, size = parts[0].shape
    return pl.pallas_call(
        functools.partial(add_z_body, nz),
        out_shape=jax.ShapeDtypeStruct((piece, size * (len(parts) // nz)), BF16),
        in_specs=[pl.BlockSpec(memory_space=pltpu.VMEM)] * len(parts),
        compiler_params=PARAMS,
        cost_estimate=COST,
        name="add_z",
    )(*parts)


def forward_body(rank, nz, groups, tenant_ref, place_ref, *refs):
    cot_refs, refs = refs[:groups], refs[groups:]
    w_hbm, a_hbm, up_hbm = refs[:3]
    pieces = refs[3 : 2 * nz + 5]
    w_ref, a_ref, up_ref, x_ref, acc_ref, low_acc, w_sem, sem, x_sem = refs[-9:]
    tokens, cols = acc_ref.shape
    nblk = tokens // BLOCK
    outs = refs[-11 - (groups - 1) * (nblk // groups) : -9]
    part_refs, side_ref = outs[:-1], outs[-1]
    piece = BLOCK // 4
    db = w_ref.shape[0] // STEPS
    z, x, core, first = place_ref[0], place_ref[1], place_ref[2], place_ref[3]
    moves = []
    for n in range(4 * nz):
        k, fx, fc = n // 4, (n // 2) % 2, n % 2
        src = pieces[2 * nz + fx].at[pl.ds(k * piece, piece), :] if fc else pieces[2 * k + fx]
        b = lax.rem(z + (2 * nz - k) - first, nz)
        row = (b * 4 + (x ^ fx) * 2 + (core ^ fc)) * piece
        rows = pl.ds(pl.multiple_of(row, piece), piece)
        moves.append(pltpu.make_async_copy(src, x_ref.at[rows, :], x_sem.at[n]))
    moves += factor_copies(tenant_ref, first, a_hbm, a_ref, sem, 0)
    late = factor_copies(tenant_ref, first, up_hbm, up_ref, sem, nblk)
    for copy in moves:
        copy.start()
    for i in range(STEPS):
        weight_copy(w_hbm, w_ref, w_sem, i).start()
    for copy in late:
        copy.start()
    acc_ref[...] = jnp.zeros_like(acc_ref)
    low_acc[...] = jnp.zeros_like(low_acc)
    side_ref[...] = jnp.zeros_like(side_ref)
    for copy in moves:
        copy.wait()

    def block(i, carry):
        weight_copy(w_hbm, w_ref, w_sem, i).wait()
        at = pl.ds(pl.multiple_of(i * db, db), db)
        xs = x_ref[:, at]
        acc_ref[...] += jnp.dot(xs, w_ref[at, :], preferred_element_type=F32)
        low_acc[...] += lax.dot_general(a_ref[:, at], xs, LAST, preferred_element_type=F32)
        return carry

    lax.fori_loop(0, STEPS, block, 0)
    low = low_acc[...]
    owner = lax.broadcasted_iota(jnp.int32, low.shape, 0) // rank
    block_of = lax.broadcasted_iota(jnp.int32, low.shape, 1) // BLOCK
    low = jnp.where(owner == block_of, low, 0.0)
    side_ref[:rank, :tokens] = jnp.sum(low.reshape(nblk, rank, tokens), axis=0)
    hi = low.astype(BF16).astype(F32)
    lowcat = jnp.concatenate([hi, low - hi], axis=0).T.astype(BF16)
    for copy in late:
        copy.wait()
    up = up_ref[...]
    up = jnp.concatenate([up, up], axis=0)
    size = nblk // groups
    for i in range(nblk):
        rows = slice(i * BLOCK, (i + 1) * BLOCK)
        here = slice(i % size * BLOCK, (i % size + 1) * BLOCK)
        part = acc_ref[rows, :] + jnp.dot(lowcat[rows, :], up, preferred_element_type=F32)
        if i < size:
            part_refs[0][here, :] = part
        else:
            part_refs[1 + i - size][...] = part.astype(BF16)
        product = part * cot_refs[i // size][here, :].astype(F32)
        side_ref[rank + i : rank + i + 1, :cols] = jnp.sum(product, axis=0, keepdims=True)


def forward(tenant, place, weight, cots, down, up, pieces, nz, deps):
    depth, cols = weight.shape
    tokens = tenant.shape[0]
    nblk = tokens // BLOCK
    rank = down.shape[1]
    groups = len(cots)
    size = nblk // groups
    shapes = [jax.ShapeDtypeStruct((size * BLOCK, cols), F32)]
    shapes += [jax.ShapeDtypeStruct((BLOCK, cols), BF16)] * (nblk - size)
    shapes += [jax.ShapeDtypeStruct((rank + nblk, max(cols, tokens)), F32)]
    return pl.pallas_call(
        functools.partial(forward_body, rank, nz, groups),
        out_shape=shapes,
        grid_spec=pltpu.PrefetchScalarGridSpec(
            num_scalar_prefetch=2,
            grid=(1,),
            in_specs=[same_block(cot) for cot in cots]
            + [IN_HBM] * (3 + len(pieces))
            + order_specs(deps),
            out_specs=[same_block(s) for s in shapes],
            scratch_shapes=[
                pltpu.VMEM((depth, cols), BF16),
                pltpu.VMEM((nblk * rank, depth), BF16),
                pltpu.VMEM((nblk * rank, cols), BF16),
                pltpu.VMEM((tokens, depth), BF16),
                pltpu.VMEM((tokens, cols), F32),
                pltpu.VMEM((nblk * rank, tokens), F32),
                pltpu.SemaphoreType.DMA((STEPS,)),
                pltpu.SemaphoreType.DMA((2 * nblk,)),
                pltpu.SemaphoreType.DMA((4 * nz,)),
            ],
        ),
        compiler_params=PARAMS,
        cost_estimate=COST,
        name="forward",
    )(tenant, place, *cots, weight, down, up, *pieces, *deps)


def shards(inputs, weight, adapter_down_factors, adapter_up_factors, magnitude, cotangent, tenant):
    col_count, row_count = lax.axis_size("col"), lax.axis_size("row")
    nz = col_count // 4
    down, up = adapter_down_factors, adapter_up_factors
    tenant_number, rank, depth = down.shape
    cols = weight.shape[1]
    tokens = tenant.shape[0]
    nblk = tokens // BLOCK
    rows_row = tokens // row_count
    blocks_mine = rows_row // BLOCK
    col, row = lax.axis_index("col"), lax.axis_index("row")
    z, x, core = col >> 2, (col >> 1) & 1, col & 1

    def move(value, dz, fx, fc):
        perm = []
        for source in range(col_count):
            sz, sx, sc = source // 4, (source // 2) % 2, source % 2
            perm.append((source, ((sz + dz) % nz) * 4 + (sx ^ fx) * 2 + (sc ^ fc)))
        return lax.ppermute(value, "col", perm)

    def swap(value):
        return lax.ppermute(value, "row", [(0, 1), (1, 0)])

    def place(*firsts):
        return jnp.stack([z, x, core, *firsts]).astype(jnp.int32)

    pair = row_count == 2

    def once(value, other):
        return lax.optimization_barrier((value, other))[0]

    along_z = [inputs] + [move(inputs, k, 0, 0) for k in range(1, nz)]
    along_x = {0: move(once(inputs, along_z[-1]), 0, 1, 0), nz - 1: move(along_z[-1], 0, 1, 0)}

    def other_x(k, after):
        along_z[k] = once(along_z[k], after)
        along_x[k] = move(along_z[k], 0, 1, 0)

    def other_core(part):
        return move(jnp.concatenate(part, axis=0), 0, 0, 1)

    nsq = partial_norms(tenant, weight, down, up)
    if pair:
        nsq_a, nsq_b = nsq, swap(nsq)
        firsts = [row * blocks_mine, (1 - row) * blocks_mine]
        cots = [cotangent, swap(cotangent)]
    else:
        nsq_a, nsq_b = lax.psum(nsq, "row"), jnp.zeros_like(nsq)
        firsts = [0 * row]
        cots = [lax.all_gather(cotangent, "row", axis=0, tiled=True)]
    places = [place(first) for first in firsts]

    def scaled(g, deps):
        return scaled_gradient(tenant, places[g], cots[g], nsq_a, nsq_b, magnitude, up, deps)

    def grad(g, part, chunk, deps):
        return grad_chunk(tenant, places[g], part[1], part[2], weight, down, chunk, deps)

    def cross_core(made, deps):
        return add_core([(keep, move(send, 0, 0, 1)) for keep, send in made], deps)

    def cross_x(groups, deps):
        mine, *away = add_x(place(*firsts), groups, nz, deps)
        return [mine] + [move(a, k + 1, 0, 0) for k, a in enumerate(away)]

    def across_x(made):
        return made[0], move(made[1], 0, 1, 0)

    if pair:
        ours = scaled(0, [])
        made = [grad(0, ours, 0, along_z[-1:])]
        for k in range(1, nz - 2):
            other_x(k, made[0][0])
        made += [grad(0, ours, 1, [made[0][0], cots[1]])]
        other_x(nz - 2, made[1][0])
        theirs = scaled(1, [made[1][0]])
        near = [across_x(cross_core(made[:1], [theirs[0]]))]
        mine, away = cross_core(made[1:], [near[0][0]])
        near += [across_x((mine, once(away, near[0][1])))]
        far = [grad(1, theirs, 0, [mine, along_x[0], along_x[nz - 1]])]
        core_z = other_core(along_z)
        far += [grad(1, theirs, 1, [far[0][0], core_z] + [along_x[k] for k in range(1, nz - 2)])]
        along_x = [along_x[k] for k in range(nz)]
        along_x[nz - 2] = once(along_x[nz - 2], far[0][0])
        core_x = other_core(along_x)
        far = cross_core(far, along_x)
        pieces = [piece for both in zip(along_z, along_x) for piece in both] + [core_z, core_x]
        part, *away, side = forward(
            tenant, places[0], weight, cots, down, up, pieces, nz, [far[0], near[1][1]]
        )
        arrived = [swap(away[0])]
        finals = cross_x([near, [across_x(far)]], [side])
        for block in away[1:]:
            arrived.append(swap(once(block, (arrived[-1], finals[0]))))
        new = swap(once(side, (arrived[0], finals[-1])))
        low = side[:rank, :tokens] + jnp.roll(new[:rank, :tokens], rows_row, axis=1)
        dots = side[rank:, :cols] + jnp.roll(new[rank:, :cols], blocks_mine, axis=0)
        parts = [ours, theirs]
    else:
        ours = scaled(0, [])
        near = [across_x(cross_core([grad(0, ours, c, [])], [])) for c in range(CHUNKS)]
        for k in range(1, nz - 1):
            other_x(k, inputs)
        along_x = [along_x[k] for k in range(nz)]
        pieces = [piece for both in zip(along_z, along_x) for piece in both]
        pieces += [other_core(along_z), other_core(along_x)]
        part, side = forward(tenant, places[0], weight, cots, down, up, pieces, nz, [])
        finals = cross_x([near], [])
        low, dots = lax.psum((side[:rank, :tokens], side[rank:, :cols]), "row")
        parts = [ours]

    scales = jnp.concatenate([group[0] for group in parts], axis=0)

    tenants = jnp.arange(tenant_number, dtype=jnp.int32)
    block_tenant = tenant.reshape(nblk, BLOCK)[:, 0]
    size = nblk // len(parts)
    owners = jnp.concatenate(
        [lax.dynamic_slice_in_dim(block_tenant, first, size, 0) for first in firsts]
    )
    low = low.astype(BF16)
    grad_b = 0.0
    for g, group in enumerate(parts):
        owner = jnp.repeat(owners[g * size : (g + 1) * size], BLOCK)
        mine = low[:, g * size * BLOCK : (g + 1) * size * BLOCK]
        wide = jnp.where((tenants[:, None] == owner[None, :])[:, None, :], mine[None], 0)
        wide = wide.reshape(tenant_number * rank, size * BLOCK)
        grad_b = grad_b + jnp.dot(wide, group[1], preferred_element_type=F32)
    grad_b = grad_b.reshape(tenant_number, rank, cols)
    hit = (tenants[:, None] == owners[None, :])[:, :, None]
    terms = jnp.where(hit, (dots * scales)[None], 0.0)
    grad_m = 0.0
    for g in range(len(parts)):
        group = terms[:, g * size : (g + 1) * size]
        grad_m = grad_m + functools.reduce(jnp.add, [group[:, i] for i in range(size)])
    grad_inputs = add_z([once(finals[0], grad_b)] + finals[1:], nz)
    if pair:
        pre = part + jnp.concatenate(arrived, axis=0).astype(F32)
        scale_mine = parts[0][0]
    else:
        pre = lax.psum_scatter(part, "row", scatter_dimension=0, tiled=True)
        scale_mine = lax.dynamic_slice_in_dim(scales, row * blocks_mine, blocks_mine, 0)
    output = (pre.reshape(blocks_mine, BLOCK, cols) * scale_mine[:, None, :]).astype(BF16)
    output = output.reshape(rows_row, cols)
    return (output, grad_inputs, grad_b, grad_m / magnitude)


def solution(mesh):
    return jax.shard_map(
        shards,
        mesh=mesh,
        in_specs=(
            P("col", "row"),
            P("row", "col"),
            P(None, None, "row"),
            P(None, None, "col"),
            P(None, "col"),
            P("row", "col"),
            P(),
        ),
        out_specs=(P("row", "col"), P("col", "row"), P(None, None, "col"), P(None, "col")),
        check_vma=False,
    )
```

```python
import functools

import jax
import jax.numpy as jnp
from jax import lax
from jax.experimental import pallas as pl
from jax.experimental.pallas import tpu as pltpu
from jax.sharding import PartitionSpec as P

BLOCK = 128
EPS = 1e-06
HIGH = lax.Precision.HIGHEST
STEPS = 8
PARTS = 16
AHEAD = 6
F32 = jnp.float32
BF16 = jnp.bfloat16
COST = pl.CostEstimate(flops=1000, bytes_accessed=1000, transcendentals=0)
LAST = (((1,), (1,)), ((), ()))
PARAMS = pltpu.CompilerParams(vmem_limit_bytes=52 * 1024 * 1024)
IN_HBM = pl.BlockSpec(memory_space=pltpu.HBM)


def order_specs(deps):
    return [pl.BlockSpec(memory_space=pl.ANY)] * len(deps)


def same_block(array):
    return pl.BlockSpec(array.shape, lambda *args: (0,) * array.ndim)


def hi_lo(value, axis):
    hi = value.astype(BF16)
    lo = (value - hi.astype(F32)).astype(BF16)
    return jnp.concatenate([hi, lo], axis=axis)


def weight_copy(w_hbm, w_ref, sem, i):
    size = w_ref.shape[0] // PARTS
    rows = pl.ds(pl.multiple_of(i * size, size), size)
    return pltpu.make_async_copy(w_hbm.at[rows, :], w_ref.at[rows, :], sem.at[i])


def weight_block(w_hbm, w_ref, sem, i, steps):
    count = PARTS // steps
    for n in range(count):
        weight_copy(w_hbm, w_ref, sem, i * count + n).wait()
    for n in range(count):
        later = i * count + n + AHEAD

        @pl.when(later < PARTS)
        def _():
            weight_copy(w_hbm, w_ref, sem, later).start()


def factor_copies(tenant_ref, first, hbm, ref, sem, at):
    rank, nblk = hbm.shape[1], tenant_ref.shape[0] // BLOCK
    copies = []
    for b in range(ref.shape[0] // rank):
        src = hbm.at[tenant_ref[lax.rem(first + b, nblk) * BLOCK]]
        dst = ref.at[pl.ds(b * rank, rank), :]
        copies.append(pltpu.make_async_copy(src, dst, sem.at[at + b]))
    return copies


def norm_body(nblk, rank, tenant_ref, w_hbm, a_hbm, up_hbm, nsq_ref, *refs):
    w_ref, a_ref, up_ref, cross_ref, square_ref, w_sem, sem = refs
    cols = w_ref.shape[1]
    db = w_ref.shape[0] // STEPS
    copies = factor_copies(tenant_ref, 0, a_hbm, a_ref, sem, 0)
    late = factor_copies(tenant_ref, 0, up_hbm, up_ref, sem, nblk)
    for copy in copies:
        copy.start()
    for i in range(AHEAD):
        weight_copy(w_hbm, w_ref, w_sem, i).start()
    for copy in late:
        copy.start()
    cross_ref[...] = jnp.zeros_like(cross_ref)
    square_ref[...] = jnp.zeros_like(square_ref)
    for copy in copies:
        copy.wait()
    step = min(db, 256)

    def block(i, carry):
        weight_block(w_hbm, w_ref, w_sem, i, STEPS)
        squares = square_ref[...]
        for start in range(0, db, step):
            rows = pl.ds(pl.multiple_of(i * db + start, step), step)
            w = w_ref[rows, :]
            cross_ref[...] += jnp.dot(a_ref[:, rows], w, preferred_element_type=F32)
            for at in range(0, step, 16):
                wf = w[at : at + 16, :].astype(F32)
                squares = squares + wf[:8] * wf[:8] + wf[8:] * wf[8:]
        square_ref[...] = squares
        return carry

    lax.fori_loop(0, STEPS, block, 0)
    for copy in late:
        copy.wait()
    gram = lax.dot_general(a_ref[...], a_ref[...], LAST, preferred_element_type=F32)
    row = lax.broadcasted_iota(jnp.int32, gram.shape, 0) // rank
    col = lax.broadcasted_iota(jnp.int32, gram.shape, 1) // rank
    gram = jnp.where(row == col, gram, 0.0)
    up = up_ref[...].astype(F32)
    quad = jnp.dot(gram, up, preferred_element_type=F32, precision=HIGH)
    mixed = (up * (2.0 * cross_ref[...] + quad)).reshape(nblk, rank, cols)
    nsq_ref[...] = jnp.sum(mixed, axis=1) + jnp.sum(square_ref[...], axis=0, keepdims=True)


def partial_norms(tenant, weight, down, up):
    depth, cols = weight.shape
    rank = down.shape[1]
    nblk = tenant.shape[0] // BLOCK
    shape = jax.ShapeDtypeStruct((nblk, cols), F32)
    return pl.pallas_call(
        functools.partial(norm_body, nblk, rank),
        out_shape=shape,
        grid_spec=pltpu.PrefetchScalarGridSpec(
            num_scalar_prefetch=1,
            grid=(1,),
            in_specs=[IN_HBM] * 3,
            out_specs=same_block(shape),
            scratch_shapes=[
                pltpu.VMEM((depth, cols), BF16),
                pltpu.VMEM((nblk * rank, depth), BF16),
                pltpu.VMEM((nblk * rank, cols), BF16),
                pltpu.VMEM((nblk * rank, cols), F32),
                pltpu.VMEM((8, cols), F32),
                pltpu.SemaphoreType.DMA((PARTS,)),
                pltpu.SemaphoreType.DMA((2 * nblk,)),
            ],
        ),
        compiler_params=PARAMS,
        cost_estimate=COST,
        name="partial_norms",
    )(tenant, weight, down, up)


def grad_body(nb, rank, tenant_ref, place_ref, cot_ref, nsq_a, nsq_b, mag_ref, *refs):
    w_hbm, a_hbm, up_hbm = refs[:3]
    scale_ref, sg_ref, keep_ref, send_ref = refs[-11:-7]
    w_ref, a_ref, up_ref, sgp_ref, backp_ref, w_sem, sem = refs[-7:]
    rows, db = sg_ref.shape[0], keep_ref.shape[1]
    piece = BLOCK // 4
    half = rows // 2
    step = pl.program_id(0)
    x, core, first = place_ref[1], place_ref[2], place_ref[3]

    @pl.when(step == 0)
    def _():
        copies = factor_copies(tenant_ref, first, up_hbm, up_ref, sem, 0)
        copies += factor_copies(tenant_ref, first, a_hbm, a_ref, sem, nb)
        for copy in copies:
            copy.start()
        for i in range(AHEAD):
            weight_copy(w_hbm, w_ref, w_sem, i).start()
        for b in range(nb):
            at = first + b
            total = nsq_a[pl.ds(at, 1), :] + nsq_b[pl.ds(at, 1), :]
            scale = mag_ref[pl.ds(tenant_ref[at * BLOCK], 1), :] / jnp.sqrt(total + EPS)
            scale_ref[b : b + 1, :] = scale
            here = slice(b * BLOCK, (b + 1) * BLOCK)
            sg_ref[here, :] = (cot_ref[here, :].astype(F32) * scale).astype(BF16)
        for fc in range(2):
            for fx in range(2):
                for b in range(nb):
                    c = b * 4 + (x ^ fx) * 2 + (core ^ fc)
                    src = pl.ds(pl.multiple_of(c * piece, piece), piece)
                    at = ((fc * 2 + fx) * nb + b) * piece
                    sgp_ref[at : at + piece, :] = sg_ref[src, :]
        for copy in copies:
            copy.wait()
        back = lax.dot_general(sgp_ref[...], up_ref[...], LAST, preferred_element_type=F32)
        block = lax.broadcasted_iota(jnp.int32, back.shape, 0) // piece % nb
        owner = lax.broadcasted_iota(jnp.int32, back.shape, 1) // rank
        backp_ref[...] = hi_lo(jnp.where(owner == block, back, 0.0), 1)

    weight_block(w_hbm, w_ref, w_sem, step, STEPS)
    at = pl.ds(pl.multiple_of(step * db, db), db)
    down = a_ref[:, at]
    down = jnp.concatenate([down, down], axis=0)
    part = lax.dot_general(sgp_ref[...], w_ref[at, :], LAST, preferred_element_type=F32)
    part = part + jnp.dot(backp_ref[...], down, preferred_element_type=F32)
    keep_ref[...] = part[:half, :]
    send_ref[...] = part[half:, :].astype(BF16)


def input_gradient(tenant, place, cot, nsq_a, nsq_b, magnitude, weight, down, up, deps):
    depth, cols = weight.shape
    rows = cot.shape[0]
    nb = rows // BLOCK
    rank = down.shape[1]
    db = depth // STEPS
    shapes = (
        jax.ShapeDtypeStruct((nb, cols), F32),
        jax.ShapeDtypeStruct((rows, cols), BF16),
        jax.ShapeDtypeStruct((rows // 2, depth), F32),
        jax.ShapeDtypeStruct((rows // 2, depth), BF16),
    )
    return pl.pallas_call(
        functools.partial(grad_body, nb, rank),
        out_shape=shapes,
        grid_spec=pltpu.PrefetchScalarGridSpec(
            num_scalar_prefetch=2,
            grid=(STEPS,),
            in_specs=[same_block(a) for a in (cot, nsq_a, nsq_b, magnitude)]
            + [IN_HBM] * 3
            + order_specs(deps),
            out_specs=[same_block(s) for s in shapes[:2]]
            + [pl.BlockSpec((rows // 2, db), lambda i, t, p: (0, i))] * 2,
            scratch_shapes=[
                pltpu.VMEM((depth, cols), BF16),
                pltpu.VMEM((nb * rank, depth), BF16),
                pltpu.VMEM((nb * rank, cols), BF16),
                pltpu.VMEM((rows, cols), BF16),
                pltpu.VMEM((rows, 2 * nb * rank), BF16),
                pltpu.SemaphoreType.DMA((PARTS,)),
                pltpu.SemaphoreType.DMA((2 * nb,)),
            ],
        ),
        compiler_params=PARAMS,
        cost_estimate=COST,
        name="input_gradient",
    )(tenant, place, cot, nsq_a, nsq_b, magnitude, weight, down, up, *deps)


def add_core_body(keep_ref, recv_ref, *refs):
    mine_ref, send_ref = refs[-2:]
    half = mine_ref.shape[0]
    mine_ref[...] = keep_ref[:half, :] + recv_ref[:half, :].astype(F32)
    send_ref[...] = (keep_ref[half:, :] + recv_ref[half:, :].astype(F32)).astype(BF16)


def add_core(keep, recv, deps):
    rows, size = keep.shape
    block = size // 2
    return pl.pallas_call(
        add_core_body,
        out_shape=(
            jax.ShapeDtypeStruct((rows // 2, size), F32),
            jax.ShapeDtypeStruct((rows // 2, size), BF16),
        ),
        grid=(2,),
        in_specs=[pl.BlockSpec((rows, block), lambda i: (0, i))] * 2 + order_specs(deps),
        out_specs=[pl.BlockSpec((rows // 2, block), lambda i: (0, i))] * 2,
        compiler_params=PARAMS,
        cost_estimate=COST,
        name="add_core",
    )(keep, recv, *deps)


def add_x_body(groups, nz, place_ref, *refs):
    outs, total_ref = refs[-nz - 1 : -1], refs[-1]
    piece = outs[0].shape[0]
    z = place_ref[0]
    for g in range(groups):
        keep_ref, recv_ref = refs[2 * g : 2 * g + 2]
        first = pl.multiple_of(place_ref[3 + g] * piece, piece)
        total = keep_ref[...] + recv_ref[...].astype(F32)
        total_ref[pl.ds(first, keep_ref.shape[0]), :] = total
    for k in range(nz):
        at = pl.multiple_of(lax.rem(z + k, nz) * piece, piece)
        outs[k][...] = total_ref[pl.ds(at, piece), :].astype(outs[k].dtype)


def add_x(place, pairs, nz, deps):
    piece = BLOCK // 4
    size = pairs[0][0].shape[1]
    block = size // 2
    operands = [array for pair in pairs for array in pair]

    def spec(array):
        return pl.BlockSpec((array.shape[0], block), lambda i, p: (0, i))

    shapes = tuple(jax.ShapeDtypeStruct((piece, size), BF16 if k else F32) for k in range(nz))
    return pl.pallas_call(
        functools.partial(add_x_body, len(pairs), nz),
        out_shape=shapes,
        grid_spec=pltpu.PrefetchScalarGridSpec(
            num_scalar_prefetch=1,
            grid=(2,),
            in_specs=[spec(a) for a in operands] + order_specs(deps),
            out_specs=[spec(s) for s in shapes],
            scratch_shapes=[pltpu.VMEM((nz * piece, block), F32)],
        ),
        compiler_params=PARAMS,
        cost_estimate=COST,
        name="add_x",
    )(place, *operands, *deps)


def add_z_body(*refs):
    total = refs[0][...]
    for ref in refs[1:-1]:
        total = total + ref[...].astype(F32)
    refs[-1][...] = total.astype(BF16)


def add_z(parts):
    return pl.pallas_call(
        add_z_body,
        out_shape=jax.ShapeDtypeStruct(parts[0].shape, BF16),
        in_specs=[pl.BlockSpec(memory_space=pltpu.VMEM)] * len(parts),
        compiler_params=PARAMS,
        cost_estimate=COST,
        name="add_z",
    )(*parts)


def forward_body(rank, nz, groups, tenant_ref, place_ref, *refs):
    cot_refs, refs = refs[:groups], refs[groups:]
    w_hbm, a_hbm, up_hbm = refs[:3]
    pieces = refs[3 : 2 * nz + 5]
    w_ref, a_ref, up_ref, x_ref, acc_ref, low_acc, w_sem, sem, x_sem = refs[-9:]
    tokens, cols = acc_ref.shape
    nblk = tokens // BLOCK
    outs = refs[-11 - (groups - 1) * (nblk // groups) : -9]
    part_refs, side_ref = outs[:-1], outs[-1]
    piece = BLOCK // 4
    depth = w_ref.shape[0]
    steps = STEPS // 2
    db = depth // steps
    z, x, core, first = place_ref[0], place_ref[1], place_ref[2], place_ref[3]
    moves = [[], []]
    for n in range(4 * nz):
        k, fx, fc = n // 4, (n // 2) % 2, n % 2
        src = pieces[2 * nz + fx].at[pl.ds(k * piece, piece), :] if fc else pieces[2 * k + fx].at[:, :]
        b = lax.rem(z + (2 * nz - k) - first, nz)
        row = (b * 4 + (x ^ fx) * 2 + (core ^ fc)) * piece
        rows = pl.ds(pl.multiple_of(row, piece), piece)
        for h in range(2):
            at = pl.ds(h * depth // 2, depth // 2)
            copy = pltpu.make_async_copy(src.at[:, at], x_ref.at[rows, at], x_sem.at[h, n])
            moves[h].append(copy)
    moves[0] += factor_copies(tenant_ref, first, a_hbm, a_ref, sem, 0)
    late = factor_copies(tenant_ref, first, up_hbm, up_ref, sem, nblk)
    for copy in moves[0]:
        copy.start()
    for i in range(AHEAD):
        weight_copy(w_hbm, w_ref, w_sem, i).start()
    for copy in moves[1] + late:
        copy.start()
    acc_ref[...] = jnp.zeros_like(acc_ref)
    low_acc[...] = jnp.zeros_like(low_acc)
    side_ref[...] = jnp.zeros_like(side_ref)

    def block(i, carry):
        for h in range(2):

            @pl.when(i == h * (steps // 2))
            def _():
                for copy in moves[h]:
                    copy.wait()

        weight_block(w_hbm, w_ref, w_sem, i, steps)
        at = pl.ds(pl.multiple_of(i * db, db), db)
        xs = x_ref[:, at]
        acc_ref[...] += jnp.dot(xs, w_ref[at, :], preferred_element_type=F32)
        low_acc[...] += lax.dot_general(a_ref[:, at], xs, LAST, preferred_element_type=F32)
        return carry

    lax.fori_loop(0, steps, block, 0)
    low = low_acc[...]
    owner = lax.broadcasted_iota(jnp.int32, low.shape, 0) // rank
    block_of = lax.broadcasted_iota(jnp.int32, low.shape, 1) // BLOCK
    low = jnp.where(owner == block_of, low, 0.0)
    side_ref[:rank, :tokens] = jnp.sum(low.reshape(nblk, rank, tokens), axis=0)
    hi = low.astype(BF16).astype(F32)
    lowcat = jnp.concatenate([hi, low - hi], axis=0).T.astype(BF16)
    for copy in late:
        copy.wait()
    up = up_ref[...]
    up = jnp.concatenate([up, up], axis=0)
    size = nblk // groups
    for i in range(nblk):
        rows = slice(i * BLOCK, (i + 1) * BLOCK)
        here = slice(i % size * BLOCK, (i % size + 1) * BLOCK)
        part = acc_ref[rows, :] + jnp.dot(lowcat[rows, :], up, preferred_element_type=F32)
        if i < size:
            part_refs[0][here, :] = part
        else:
            part_refs[1 + i - size][:BLOCK, :] = part.astype(BF16)
        product = part * cot_refs[i // size][here, :].astype(F32)
        side_ref[rank + i : rank + i + 1, :cols] = jnp.sum(product, axis=0, keepdims=True)
    if groups > 1:
        out = part_refs[1]
        out[BLOCK:, :] = jnp.zeros((out.shape[0] - BLOCK, cols), BF16)
        low, dots = side_ref[:rank, :tokens], side_ref[rank:, :cols]
        packed = []
        for n in range(3):
            out[BLOCK : BLOCK + rank, n * tokens : (n + 1) * tokens] = low.astype(BF16)
            low = low - low.astype(BF16).astype(F32)
            packed.append(dots.astype(BF16).astype(F32))
            dots = dots - packed[-1]
        packed.append(jnp.zeros((out.shape[0] - BLOCK - rank - 3 * nblk, cols), F32))
        out[BLOCK + rank :, :] = jnp.concatenate(packed, axis=0).astype(BF16)


def forward(tenant, place, weight, cots, down, up, pieces, nz, deps):
    depth, cols = weight.shape
    tokens = tenant.shape[0]
    nblk = tokens // BLOCK
    rank = down.shape[1]
    groups = len(cots)
    size = nblk // groups
    shapes = [jax.ShapeDtypeStruct((size * BLOCK, cols), F32)]
    for i in range(nblk - size):
        extra = 0 if i else -(-(rank + 3 * nblk) // 16) * 16
        shapes += [jax.ShapeDtypeStruct((BLOCK + extra, cols), BF16)]
    shapes += [jax.ShapeDtypeStruct((rank + nblk, max(cols, tokens)), F32)]
    return pl.pallas_call(
        functools.partial(forward_body, rank, nz, groups),
        out_shape=shapes,
        grid_spec=pltpu.PrefetchScalarGridSpec(
            num_scalar_prefetch=2,
            grid=(1,),
            in_specs=[same_block(cot) for cot in cots]
            + [IN_HBM] * (3 + len(pieces))
            + order_specs(deps),
            out_specs=[same_block(s) for s in shapes],
            scratch_shapes=[
                pltpu.VMEM((depth, cols), BF16),
                pltpu.VMEM((nblk * rank, depth), BF16),
                pltpu.VMEM((nblk * rank, cols), BF16),
                pltpu.VMEM((tokens, depth), BF16),
                pltpu.VMEM((tokens, cols), F32),
                pltpu.VMEM((nblk * rank, tokens), F32),
                pltpu.SemaphoreType.DMA((PARTS,)),
                pltpu.SemaphoreType.DMA((2 * nblk,)),
                pltpu.SemaphoreType.DMA((2, 4 * nz)),
            ],
        ),
        compiler_params=PARAMS,
        cost_estimate=COST,
        name="forward",
    )(tenant, place, *cots, weight, down, up, *pieces, *deps)


def shards(inputs, weight, adapter_down_factors, adapter_up_factors, magnitude, cotangent, tenant):
    col_count, row_count = lax.axis_size("col"), lax.axis_size("row")
    nz = col_count // 4
    down, up = adapter_down_factors, adapter_up_factors
    tenant_number, rank, depth = down.shape
    cols = weight.shape[1]
    tokens = tenant.shape[0]
    nblk = tokens // BLOCK
    rows_row = tokens // row_count
    blocks_mine = rows_row // BLOCK
    col, row = lax.axis_index("col"), lax.axis_index("row")
    z, x, core = col >> 2, (col >> 1) & 1, col & 1

    def move(value, dz, fx, fc):
        perm = []
        for source in range(col_count):
            sz, sx, sc = source // 4, (source // 2) % 2, source % 2
            perm.append((source, ((sz + dz) % nz) * 4 + (sx ^ fx) * 2 + (sc ^ fc)))
        return lax.ppermute(value, "col", perm)

    def swap(value):
        return lax.ppermute(value, "row", [(0, 1), (1, 0)])

    def place(*firsts):
        return jnp.stack([z, x, core, *firsts]).astype(jnp.int32)

    pair = row_count == 2 and 3 * tokens <= cols

    def once(value, other):
        return lax.optimization_barrier((value, other))[0]

    along_z = [inputs] + [move(inputs, k, 0, 0) for k in range(1, nz)]
    along_x = {0: move(inputs, 0, 1, 0)}

    def other_x(k, after):
        along_z[k] = once(along_z[k], after)
        along_x[k] = move(along_z[k], 0, 1, 0)

    def other_core(part):
        return move(jnp.concatenate(part, axis=0), 0, 0, 1)

    nsq = partial_norms(tenant, weight, down, up)
    if pair:
        nsq_a, nsq_b = nsq, swap(once(nsq, along_x[0]))
        firsts = [row * blocks_mine, (1 - row) * blocks_mine]
        cots = [cotangent, swap(cotangent)]
    else:
        nsq_a, nsq_b = lax.psum(nsq, "row"), jnp.zeros_like(nsq)
        firsts = [0 * row]
        cots = [lax.all_gather(cotangent, "row", axis=0, tiled=True)]
    places = [place(first) for first in firsts]

    def gradient(g, deps):
        return input_gradient(
            tenant, places[g], cots[g], nsq_a, nsq_b, magnitude, weight, down, up, deps
        )

    def cross_core(made, deps):
        return add_core(made[2], move(made[3], 0, 0, 1), deps)

    def cross_x(pairs, deps):
        mine, *away = add_x(place(*firsts), pairs, nz, deps)
        return [mine] + [move(block, k + 1, 0, 0) for k, block in enumerate(away)]

    def across_x(made):
        return made[0], move(made[1], 0, 1, 0)

    if pair:
        other_x(nz - 1, nsq)
        for k in range(1, nz - 2):
            other_x(k, nsq_b)
        ours = gradient(0, [cots[1]])
        other_x(nz - 2, ours[0])
        core_z = other_core(along_z)
        near = across_x(cross_core(ours, []))
        theirs = gradient(1, [near[0], core_z, along_x[nz - 2]])
        along_x = [along_x[k] for k in range(nz)]
        core_x = other_core(along_x)
        far = cross_core(theirs, [core_x])
        pieces = [piece for both in zip(along_z, along_x) for piece in both] + [core_z, core_x]
        part, first, *away, side = forward(
            tenant, places[0], weight, cots, down, up, pieces, nz, [far[0]]
        )
        first = swap(first)
        arrived = [first[:BLOCK]] + [swap(once(block, first)) for block in away]
        finals = cross_x([near, across_x(far)], [side])
        first = once(first, (finals[nz // 2], finals[nz - 1]))[BLOCK:].astype(F32)
        low = [first[:rank, i * tokens : (i + 1) * tokens] for i in range(3)]
        dots = [first[rank + i * nblk : rank + (i + 1) * nblk] for i in range(3)]
        low = side[:rank, :tokens] + jnp.roll(low[0] + low[1] + low[2], rows_row, axis=1)
        dots = side[rank:, :cols] + jnp.roll(dots[0] + dots[1] + dots[2], blocks_mine, axis=0)
        parts = [ours, theirs]
    else:
        ours = gradient(0, [])
        near = across_x(cross_core(ours, []))
        for k in range(1, nz):
            other_x(k, inputs)
        along_x = [along_x[k] for k in range(nz)]
        pieces = [piece for both in zip(along_z, along_x) for piece in both]
        pieces += [other_core(along_z), other_core(along_x)]
        part, side = forward(tenant, places[0], weight, cots, down, up, pieces, nz, [])
        finals = cross_x([near], [])
        low, dots = lax.psum((side[:rank, :tokens], side[rank:, :cols]), "row")
        parts = [ours]

    scales = jnp.concatenate([group[0] for group in parts], axis=0)

    tenants = jnp.arange(tenant_number, dtype=jnp.int32)
    block_tenant = tenant.reshape(nblk, BLOCK)[:, 0]
    size = nblk // len(parts)
    owners = jnp.concatenate(
        [lax.dynamic_slice_in_dim(block_tenant, first, size, 0) for first in firsts]
    )
    low = low.astype(BF16)
    grad_b = 0.0
    for g, group in enumerate(parts):
        owner = jnp.repeat(owners[g * size : (g + 1) * size], BLOCK)
        mine = low[:, g * size * BLOCK : (g + 1) * size * BLOCK]
        wide = jnp.where((tenants[:, None] == owner[None, :])[:, None, :], mine[None], 0)
        wide = wide.reshape(tenant_number * rank, size * BLOCK)
        grad_b = grad_b + jnp.dot(wide, group[1], preferred_element_type=F32)
    grad_b = grad_b.reshape(tenant_number, rank, cols)
    hit = (tenants[:, None] == owners[None, :])[:, :, None]
    terms = jnp.where(hit, (dots * scales)[None], 0.0)
    grad_m = 0.0
    for g in range(len(parts)):
        group = terms[:, g * size : (g + 1) * size]
        grad_m = grad_m + functools.reduce(jnp.add, [group[:, i] for i in range(size)])
    grad_inputs = add_z([once(finals[0], grad_b)] + finals[1:])
    if pair:
        pre = part + jnp.concatenate(arrived, axis=0).astype(F32)
        scale_mine = parts[0][0]
    else:
        pre = lax.psum_scatter(part, "row", scatter_dimension=0, tiled=True)
        scale_mine = lax.dynamic_slice_in_dim(scales, row * blocks_mine, blocks_mine, 0)
    output = (pre.reshape(blocks_mine, BLOCK, cols) * scale_mine[:, None, :]).astype(BF16)
    output = output.reshape(rows_row, cols)
    return (output, grad_inputs, grad_b, grad_m / magnitude)


def solution(mesh):
    return jax.shard_map(
        shards,
        mesh=mesh,
        in_specs=(
            P("col", "row"),
            P("row", "col"),
            P(None, None, "row"),
            P(None, None, "col"),
            P(None, "col"),
            P("row", "col"),
            P(),
        ),
        out_specs=(P("row", "col"), P("col", "row"), P(None, None, "col"), P(None, "col")),
        check_vma=False,
    )
```

```python
import functools

import jax
import jax.numpy as jnp
from jax import lax
from jax.experimental import pallas as pl
from jax.experimental.pallas import tpu as pltpu
from jax.sharding import PartitionSpec as P

BLOCK = 128
EPS = 1e-06
HIGH = lax.Precision.HIGHEST
STEPS = 8
PARTS = 16
AHEAD = 6
F32 = jnp.float32
BF16 = jnp.bfloat16
COST = pl.CostEstimate(flops=1000, bytes_accessed=1000, transcendentals=0)
LAST = (((1,), (1,)), ((), ()))
PARAMS = pltpu.CompilerParams(vmem_limit_bytes=52 * 1024 * 1024)
IN_HBM = pl.BlockSpec(memory_space=pltpu.HBM)


def order_specs(deps):
    return [pl.BlockSpec(memory_space=pl.ANY)] * len(deps)


def same_block(array):
    return pl.BlockSpec(array.shape, lambda *args: (0,) * array.ndim)


def hi_lo(value, axis):
    hi = value.astype(BF16)
    lo = (value - hi.astype(F32)).astype(BF16)
    return jnp.concatenate([hi, lo], axis=axis)


def weight_copy(w_hbm, w_ref, sem, i):
    size = w_ref.shape[0] // PARTS
    rows = pl.ds(pl.multiple_of(i * size, size), size)
    return pltpu.make_async_copy(w_hbm.at[rows, :], w_ref.at[rows, :], sem.at[i])


def weight_block(w_hbm, w_ref, sem, i, steps):
    count = PARTS // steps
    for n in range(count):
        weight_copy(w_hbm, w_ref, sem, i * count + n).wait()
    for n in range(count):
        later = i * count + n + AHEAD

        @pl.when(later < PARTS)
        def _():
            weight_copy(w_hbm, w_ref, sem, later).start()


def factor_copies(tenant_ref, first, hbm, ref, sem, at):
    rank, nblk = hbm.shape[1], tenant_ref.shape[0] // BLOCK
    copies = []
    for b in range(ref.shape[0] // rank):
        src = hbm.at[tenant_ref[lax.rem(first + b, nblk) * BLOCK]]
        dst = ref.at[pl.ds(b * rank, rank), :]
        copies.append(pltpu.make_async_copy(src, dst, sem.at[at + b]))
    return copies


def norm_body(nblk, rank, tenant_ref, w_hbm, a_hbm, up_hbm, nsq_ref, *refs):
    w_ref, a_ref, up_ref, cross_ref, square_ref, w_sem, sem = refs
    cols = w_ref.shape[1]
    db = w_ref.shape[0] // STEPS
    copies = factor_copies(tenant_ref, 0, a_hbm, a_ref, sem, 0)
    late = factor_copies(tenant_ref, 0, up_hbm, up_ref, sem, nblk)
    for copy in copies:
        copy.start()
    for i in range(AHEAD):
        weight_copy(w_hbm, w_ref, w_sem, i).start()
    for copy in late:
        copy.start()
    cross_ref[...] = jnp.zeros_like(cross_ref)
    square_ref[...] = jnp.zeros_like(square_ref)
    for copy in copies:
        copy.wait()
    step = min(db, 256)

    def block(i, carry):
        weight_block(w_hbm, w_ref, w_sem, i, STEPS)
        squares = square_ref[...]
        for start in range(0, db, step):
            rows = pl.ds(pl.multiple_of(i * db + start, step), step)
            w = w_ref[rows, :]
            cross_ref[...] += jnp.dot(a_ref[:, rows], w, preferred_element_type=F32)
            for at in range(0, step, 16):
                wf = w[at : at + 16, :].astype(F32)
                squares = squares + wf[:8] * wf[:8] + wf[8:] * wf[8:]
        square_ref[...] = squares
        return carry

    lax.fori_loop(0, STEPS, block, 0)
    for copy in late:
        copy.wait()
    gram = lax.dot_general(a_ref[...], a_ref[...], LAST, preferred_element_type=F32)
    row = lax.broadcasted_iota(jnp.int32, gram.shape, 0) // rank
    col = lax.broadcasted_iota(jnp.int32, gram.shape, 1) // rank
    gram = jnp.where(row == col, gram, 0.0)
    up = up_ref[...].astype(F32)
    quad = jnp.dot(gram, up, preferred_element_type=F32, precision=HIGH)
    mixed = (up * (2.0 * cross_ref[...] + quad)).reshape(nblk, rank, cols)
    nsq_ref[...] = jnp.sum(mixed, axis=1) + jnp.sum(square_ref[...], axis=0, keepdims=True)


def partial_norms(tenant, weight, down, up):
    depth, cols = weight.shape
    rank = down.shape[1]
    nblk = tenant.shape[0] // BLOCK
    shape = jax.ShapeDtypeStruct((nblk, cols), F32)
    return pl.pallas_call(
        functools.partial(norm_body, nblk, rank),
        out_shape=shape,
        grid_spec=pltpu.PrefetchScalarGridSpec(
            num_scalar_prefetch=1,
            grid=(1,),
            in_specs=[IN_HBM] * 3,
            out_specs=same_block(shape),
            scratch_shapes=[
                pltpu.VMEM((depth, cols), BF16),
                pltpu.VMEM((nblk * rank, depth), BF16),
                pltpu.VMEM((nblk * rank, cols), BF16),
                pltpu.VMEM((nblk * rank, cols), F32),
                pltpu.VMEM((8, cols), F32),
                pltpu.SemaphoreType.DMA((PARTS,)),
                pltpu.SemaphoreType.DMA((2 * nblk,)),
            ],
        ),
        compiler_params=PARAMS,
        cost_estimate=COST,
        name="partial_norms",
    )(tenant, weight, down, up)


def grad_body(nb, rank, tenant_ref, place_ref, cot_ref, nsq_a, nsq_b, mag_ref, *refs):
    w_hbm, a_hbm, up_hbm = refs[:3]
    scale_ref, sg_ref, keep_ref, send_ref = refs[-11:-7]
    w_ref, a_ref, up_ref, sgp_ref, backp_ref, w_sem, sem = refs[-7:]
    rows, db = sg_ref.shape[0], keep_ref.shape[1]
    piece = BLOCK // 4
    half = rows // 2
    step = pl.program_id(0)
    x, core, first = place_ref[1], place_ref[2], place_ref[3]

    @pl.when(step == 0)
    def _():
        copies = factor_copies(tenant_ref, first, up_hbm, up_ref, sem, 0)
        copies += factor_copies(tenant_ref, first, a_hbm, a_ref, sem, nb)
        for copy in copies:
            copy.start()
        for i in range(AHEAD):
            weight_copy(w_hbm, w_ref, w_sem, i).start()
        for b in range(nb):
            at = first + b
            total = nsq_a[pl.ds(at, 1), :] + nsq_b[pl.ds(at, 1), :]
            scale = mag_ref[pl.ds(tenant_ref[at * BLOCK], 1), :] / jnp.sqrt(total + EPS)
            scale_ref[b : b + 1, :] = scale
            here = slice(b * BLOCK, (b + 1) * BLOCK)
            sg_ref[here, :] = (cot_ref[here, :].astype(F32) * scale).astype(BF16)
        for fc in range(2):
            for fx in range(2):
                for b in range(nb):
                    c = b * 4 + (x ^ fx) * 2 + (core ^ fc)
                    src = pl.ds(pl.multiple_of(c * piece, piece), piece)
                    at = ((fc * 2 + fx) * nb + b) * piece
                    sgp_ref[at : at + piece, :] = sg_ref[src, :]
        for copy in copies:
            copy.wait()
        back = lax.dot_general(sgp_ref[...], up_ref[...], LAST, preferred_element_type=F32)
        block = lax.broadcasted_iota(jnp.int32, back.shape, 0) // piece % nb
        owner = lax.broadcasted_iota(jnp.int32, back.shape, 1) // rank
        backp_ref[...] = hi_lo(jnp.where(owner == block, back, 0.0), 1)

    weight_block(w_hbm, w_ref, w_sem, step, STEPS)
    at = pl.ds(pl.multiple_of(step * db, db), db)
    down = a_ref[:, at]
    down = jnp.concatenate([down, down], axis=0)
    part = lax.dot_general(sgp_ref[...], w_ref[at, :], LAST, preferred_element_type=F32)
    part = part + jnp.dot(backp_ref[...], down, preferred_element_type=F32)
    keep_ref[...] = part[:half, :]
    send_ref[...] = part[half:, :].astype(BF16)


def input_gradient(tenant, place, cot, nsq_a, nsq_b, magnitude, weight, down, up, deps):
    depth, cols = weight.shape
    rows = cot.shape[0]
    nb = rows // BLOCK
    rank = down.shape[1]
    db = depth // STEPS
    shapes = (
        jax.ShapeDtypeStruct((nb, cols), F32),
        jax.ShapeDtypeStruct((rows, cols), BF16),
        jax.ShapeDtypeStruct((rows // 2, depth), F32),
        jax.ShapeDtypeStruct((rows // 2, depth), BF16),
    )
    return pl.pallas_call(
        functools.partial(grad_body, nb, rank),
        out_shape=shapes,
        grid_spec=pltpu.PrefetchScalarGridSpec(
            num_scalar_prefetch=2,
            grid=(STEPS,),
            in_specs=[same_block(a) for a in (cot, nsq_a, nsq_b, magnitude)]
            + [IN_HBM] * 3
            + order_specs(deps),
            out_specs=[same_block(s) for s in shapes[:2]]
            + [pl.BlockSpec((rows // 2, db), lambda i, t, p: (0, i))] * 2,
            scratch_shapes=[
                pltpu.VMEM((depth, cols), BF16),
                pltpu.VMEM((nb * rank, depth), BF16),
                pltpu.VMEM((nb * rank, cols), BF16),
                pltpu.VMEM((rows, cols), BF16),
                pltpu.VMEM((rows, 2 * nb * rank), BF16),
                pltpu.SemaphoreType.DMA((PARTS,)),
                pltpu.SemaphoreType.DMA((2 * nb,)),
            ],
        ),
        compiler_params=PARAMS,
        cost_estimate=COST,
        name="input_gradient",
    )(tenant, place, cot, nsq_a, nsq_b, magnitude, weight, down, up, *deps)


def add_core_body(keep_ref, recv_ref, *refs):
    mine_ref, send_ref = refs[-2:]
    half = mine_ref.shape[0]
    mine_ref[...] = keep_ref[:half, :] + recv_ref[:half, :].astype(F32)
    send_ref[...] = (keep_ref[half:, :] + recv_ref[half:, :].astype(F32)).astype(BF16)


def add_core(keep, recv, deps):
    rows, size = keep.shape
    block = size // 2
    return pl.pallas_call(
        add_core_body,
        out_shape=(
            jax.ShapeDtypeStruct((rows // 2, size), F32),
            jax.ShapeDtypeStruct((rows // 2, size), BF16),
        ),
        grid=(2,),
        in_specs=[pl.BlockSpec((rows, block), lambda i: (0, i))] * 2 + order_specs(deps),
        out_specs=[pl.BlockSpec((rows // 2, block), lambda i: (0, i))] * 2,
        compiler_params=PARAMS,
        cost_estimate=COST,
        name="add_core",
    )(keep, recv, *deps)


def add_x_body(groups, nz, place_ref, *refs):
    outs, total_ref = refs[-nz - 1 : -1], refs[-1]
    piece = outs[0].shape[0]
    z = place_ref[0]
    for g in range(groups):
        keep_ref, recv_ref = refs[2 * g : 2 * g + 2]
        first = pl.multiple_of(place_ref[3 + g] * piece, piece)
        total = keep_ref[...] + recv_ref[...].astype(F32)
        total_ref[pl.ds(first, keep_ref.shape[0]), :] = total
    for k in range(nz):
        at = pl.multiple_of(lax.rem(z + k, nz) * piece, piece)
        outs[k][...] = total_ref[pl.ds(at, piece), :].astype(outs[k].dtype)


def add_x(place, pairs, nz, deps):
    piece = BLOCK // 4
    size = pairs[0][0].shape[1]
    block = size // 2
    operands = [array for pair in pairs for array in pair]

    def spec(array):
        return pl.BlockSpec((array.shape[0], block), lambda i, p: (0, i))

    shapes = tuple(jax.ShapeDtypeStruct((piece, size), BF16 if k else F32) for k in range(nz))
    return pl.pallas_call(
        functools.partial(add_x_body, len(pairs), nz),
        out_shape=shapes,
        grid_spec=pltpu.PrefetchScalarGridSpec(
            num_scalar_prefetch=1,
            grid=(2,),
            in_specs=[spec(a) for a in operands] + order_specs(deps),
            out_specs=[spec(s) for s in shapes],
            scratch_shapes=[pltpu.VMEM((nz * piece, block), F32)],
        ),
        compiler_params=PARAMS,
        cost_estimate=COST,
        name="add_x",
    )(place, *operands, *deps)


def add_z_body(*refs):
    total = refs[0][...]
    for ref in refs[1:-1]:
        total = total + ref[...].astype(F32)
    refs[-1][...] = total.astype(BF16)


def add_z(parts):
    return pl.pallas_call(
        add_z_body,
        out_shape=jax.ShapeDtypeStruct(parts[0].shape, BF16),
        in_specs=[pl.BlockSpec(memory_space=pltpu.VMEM)] * len(parts),
        compiler_params=PARAMS,
        cost_estimate=COST,
        name="add_z",
    )(*parts)


def forward_body(nb, rank, nz, tenant_ref, place_ref, cot_ref, w_hbm, a_hbm, up_hbm, *refs):
    pieces = refs[: 2 * nz + 2]
    part_ref, dot_ref, low_ref = refs[-12:-9]
    w_ref, a_ref, up_ref, x_ref, acc_ref, low_acc, w_sem, sem, x_sem = refs[-9:]
    rows, cols = acc_ref.shape
    piece = BLOCK // 4
    depth = w_ref.shape[0]
    steps = STEPS // 2
    db = depth // steps
    z, x, core, first = place_ref[0], place_ref[1], place_ref[2], place_ref[3]

    def each(h, act):
        at = pl.ds(h * depth // 2, depth // 2)
        for n in range(4 * nz):
            k, fx, fc = n // 4, (n // 2) % 2, n % 2
            src = pieces[2 * nz + fx] if fc else pieces[2 * k + fx]
            src = src.at[pl.ds(k * piece if fc else 0, piece), at]
            b = lax.rem(z + (nz - k), nz) - first

            @pl.when(jnp.logical_and(b >= 0, b < nb))
            def _():
                row = (b * 4 + (x ^ fx) * 2 + (core ^ fc)) * piece
                dst = pl.ds(pl.multiple_of(row, piece), piece)
                act(pltpu.make_async_copy(src, x_ref.at[dst, at], x_sem.at[h, n]))

    copies = factor_copies(tenant_ref, first, a_hbm, a_ref, sem, 0)
    late = factor_copies(tenant_ref, first, up_hbm, up_ref, sem, nb)
    each(0, lambda copy: copy.start())
    for copy in copies:
        copy.start()
    for i in range(AHEAD):
        weight_copy(w_hbm, w_ref, w_sem, i).start()
    each(1, lambda copy: copy.start())
    for copy in late:
        copy.start()
    acc_ref[...] = jnp.zeros_like(acc_ref)
    low_acc[...] = jnp.zeros_like(low_acc)
    for copy in copies:
        copy.wait()

    def block(i, carry):
        for h in range(2):

            @pl.when(i == h * (steps // 2))
            def _():
                each(h, lambda copy: copy.wait())

        weight_block(w_hbm, w_ref, w_sem, i, steps)
        at = pl.ds(pl.multiple_of(i * db, db), db)
        xs = x_ref[:, at]
        acc_ref[...] += jnp.dot(xs, w_ref[at, :], preferred_element_type=F32)
        low_acc[...] += lax.dot_general(a_ref[:, at], xs, LAST, preferred_element_type=F32)
        return carry

    lax.fori_loop(0, steps, block, 0)
    low = low_acc[...]
    owner = lax.broadcasted_iota(jnp.int32, low.shape, 0) // rank
    block_of = lax.broadcasted_iota(jnp.int32, low.shape, 1) // BLOCK
    low = jnp.where(owner == block_of, low, 0.0)
    low_ref[...] = jnp.sum(low.reshape(nb, rank, rows), axis=0)
    hi = low.astype(BF16).astype(F32)
    lowcat = jnp.concatenate([hi, low - hi], axis=0).T.astype(BF16)
    for copy in late:
        copy.wait()
    up = up_ref[...]
    up = jnp.concatenate([up, up], axis=0)
    for i in range(nb):
        here = slice(i * BLOCK, (i + 1) * BLOCK)
        part = acc_ref[here, :] + jnp.dot(lowcat[here, :], up, preferred_element_type=F32)
        part_ref[here, :] = part.astype(part_ref.dtype)
        product = part * cot_ref[here, :].astype(F32)
        dot_ref[i : i + 1, :] = jnp.sum(product, axis=0, keepdims=True)


def forward(tenant, place, weight, cot, down, up, pieces, nz, out_dtype, deps):
    depth, cols = weight.shape
    rows = cot.shape[0]
    nb = rows // BLOCK
    rank = down.shape[1]
    shapes = (
        jax.ShapeDtypeStruct((rows, cols), out_dtype),
        jax.ShapeDtypeStruct((nb, cols), F32),
        jax.ShapeDtypeStruct((rank, rows), F32),
    )
    return pl.pallas_call(
        functools.partial(forward_body, nb, rank, nz),
        out_shape=shapes,
        grid_spec=pltpu.PrefetchScalarGridSpec(
            num_scalar_prefetch=2,
            grid=(1,),
            in_specs=[same_block(cot)] + [IN_HBM] * (3 + len(pieces)) + order_specs(deps),
            out_specs=[same_block(s) for s in shapes],
            scratch_shapes=[
                pltpu.VMEM((depth, cols), BF16),
                pltpu.VMEM((nb * rank, depth), BF16),
                pltpu.VMEM((nb * rank, cols), BF16),
                pltpu.VMEM((rows, depth), BF16),
                pltpu.VMEM((rows, cols), F32),
                pltpu.VMEM((nb * rank, rows), F32),
                pltpu.SemaphoreType.DMA((PARTS,)),
                pltpu.SemaphoreType.DMA((2 * nb,)),
                pltpu.SemaphoreType.DMA((2, 4 * nz)),
            ],
        ),
        compiler_params=PARAMS,
        cost_estimate=COST,
        name="forward",
    )(tenant, place, cot, weight, down, up, *pieces, *deps)


def shards(inputs, weight, adapter_down_factors, adapter_up_factors, magnitude, cotangent, tenant):
    col_count, row_count = lax.axis_size("col"), lax.axis_size("row")
    nz = col_count // 4
    down, up = adapter_down_factors, adapter_up_factors
    tenant_number, rank, depth = down.shape
    cols = weight.shape[1]
    tokens = tenant.shape[0]
    nblk = tokens // BLOCK
    rows_row = tokens // row_count
    blocks_mine = rows_row // BLOCK
    col, row = lax.axis_index("col"), lax.axis_index("row")
    z, x, core = col >> 2, (col >> 1) & 1, col & 1

    def move(value, dz, fx, fc):
        perm = []
        for source in range(col_count):
            sz, sx, sc = source // 4, (source // 2) % 2, source % 2
            perm.append((source, ((sz + dz) % nz) * 4 + (sx ^ fx) * 2 + (sc ^ fc)))
        return lax.ppermute(value, "col", perm)

    def swap(value):
        return lax.ppermute(value, "row", [(0, 1), (1, 0)])

    def place(*firsts):
        return jnp.stack([z, x, core, *firsts]).astype(jnp.int32)

    pair = row_count == 2

    def once(value, other):
        return lax.optimization_barrier((value, other))[0]

    along_z = [inputs] + [move(inputs, k, 0, 0) for k in range(1, nz)]
    along_x = {0: move(inputs, 0, 1, 0)}

    def other_x(k, after):
        along_z[k] = once(along_z[k], after)
        along_x[k] = move(along_z[k], 0, 1, 0)

    def other_core(part):
        return move(jnp.concatenate(part, axis=0), 0, 0, 1)

    nsq = partial_norms(tenant, weight, down, up)
    if pair:
        nsq_a, nsq_b = nsq, swap(once(nsq, along_x[0]))
        firsts = [row * blocks_mine, (1 - row) * blocks_mine]
        cots = [cotangent, swap(cotangent)]
    else:
        nsq_a, nsq_b = lax.psum(nsq, "row"), jnp.zeros_like(nsq)
        firsts = [0 * row]
        cots = [lax.all_gather(cotangent, "row", axis=0, tiled=True)]
    places = [place(first) for first in firsts]

    def gradient(g, deps):
        return input_gradient(
            tenant, places[g], cots[g], nsq_a, nsq_b, magnitude, weight, down, up, deps
        )

    def cross_core(made, deps):
        return add_core(made[2], move(made[3], 0, 0, 1), deps)

    def cross_x(pairs, deps):
        mine, *away = add_x(place(*firsts), pairs, nz, deps)
        return [mine] + [move(block, k + 1, 0, 0) for k, block in enumerate(away)]

    def across_x(made):
        return made[0], move(made[1], 0, 1, 0)

    if pair:
        ours = gradient(0, [cots[1]])
        for k in [nz - 1] + list(range(1, nz - 1)):
            other_x(k, ours[0])
        core_z = other_core(along_z)
        near = across_x(cross_core(ours, []))
        theirs = gradient(1, [near[0], core_z])
        along_x = [along_x[k] for k in range(nz)]
        along_x[nz - 2] = once(along_x[nz - 2], theirs[0])
        core_x = other_core(along_x)
        far = cross_core(theirs, [core_x])
        pieces = [piece for both in zip(along_z, along_x) for piece in both] + [core_z, core_x]

        def project(g, out_dtype, deps):
            return forward(
                tenant, places[g], weight, cots[g], down, up, pieces, nz, out_dtype, deps
            )

        away, dots_away, low_away = project(1, BF16, [far[0]])
        arrived = swap(away)
        finals = cross_x([near, across_x(far)], [dots_away])
        part, dots_here, low_here = project(0, F32, [finals[0]])
        dots = jnp.concatenate([dots_here, dots_away], axis=0)
        low = jnp.concatenate([low_here, low_away], axis=1)
        late = (finals[nz // 2], finals[nz - 1])
        dots = dots + jnp.roll(swap(once(dots, late)), blocks_mine, axis=0)
        low = low + jnp.roll(swap(once(low, late)), rows_row, axis=1)
        parts = [ours, theirs]
    else:
        ours = gradient(0, [])
        near = across_x(cross_core(ours, []))
        for k in range(1, nz):
            other_x(k, inputs)
        along_x = [along_x[k] for k in range(nz)]
        pieces = [piece for both in zip(along_z, along_x) for piece in both]
        pieces += [other_core(along_z), other_core(along_x)]
        part, dots, low = forward(
            tenant, places[0], weight, cots[0], down, up, pieces, nz, F32, []
        )
        finals = cross_x([near], [])
        low, dots = lax.psum((low, dots), "row")
        parts = [ours]

    scales = jnp.concatenate([group[0] for group in parts], axis=0)

    tenants = jnp.arange(tenant_number, dtype=jnp.int32)
    block_tenant = tenant.reshape(nblk, BLOCK)[:, 0]
    size = nblk // len(parts)
    owners = jnp.concatenate(
        [lax.dynamic_slice_in_dim(block_tenant, first, size, 0) for first in firsts]
    )
    low = low.astype(BF16)
    grad_b = 0.0
    for g, group in enumerate(parts):
        owner = jnp.repeat(owners[g * size : (g + 1) * size], BLOCK)
        mine = low[:, g * size * BLOCK : (g + 1) * size * BLOCK]
        wide = jnp.where((tenants[:, None] == owner[None, :])[:, None, :], mine[None], 0)
        wide = wide.reshape(tenant_number * rank, size * BLOCK)
        grad_b = grad_b + jnp.dot(wide, group[1], preferred_element_type=F32)
    grad_b = grad_b.reshape(tenant_number, rank, cols)
    hit = (tenants[:, None] == owners[None, :])[:, :, None]
    terms = jnp.where(hit, (dots * scales)[None], 0.0)
    grad_m = 0.0
    for g in range(len(parts)):
        group = terms[:, g * size : (g + 1) * size]
        grad_m = grad_m + functools.reduce(jnp.add, [group[:, i] for i in range(size)])
    grad_inputs = add_z([once(finals[0], grad_b)] + finals[1:])
    if pair:
        pre = part + arrived.astype(F32)
        scale_mine = parts[0][0]
    else:
        pre = lax.psum_scatter(part, "row", scatter_dimension=0, tiled=True)
        scale_mine = lax.dynamic_slice_in_dim(scales, row * blocks_mine, blocks_mine, 0)
    output = (pre.reshape(blocks_mine, BLOCK, cols) * scale_mine[:, None, :]).astype(BF16)
    output = output.reshape(rows_row, cols)
    return (output, grad_inputs, grad_b, grad_m / magnitude)


def solution(mesh):
    return jax.shard_map(
        shards,
        mesh=mesh,
        in_specs=(
            P("col", "row"),
            P("row", "col"),
            P(None, None, "row"),
            P(None, None, "col"),
            P(None, "col"),
            P("row", "col"),
            P(),
        ),
        out_specs=(P("row", "col"), P("col", "row"), P(None, None, "col"), P(None, "col")),
        check_vma=False,
    )
```

```python
import functools

import jax
import jax.numpy as jnp
from jax import lax
from jax.experimental import pallas as pl
from jax.experimental.pallas import tpu as pltpu
from jax.sharding import PartitionSpec as P

BLOCK = 128
EPS = 1e-06
HIGH = lax.Precision.HIGHEST
STEPS = 8
PARTS = 16
AHEAD = 6
F32 = jnp.float32
BF16 = jnp.bfloat16
COST = pl.CostEstimate(flops=1000, bytes_accessed=1000, transcendentals=0)
LAST = (((1,), (1,)), ((), ()))
PARAMS = pltpu.CompilerParams(vmem_limit_bytes=52 * 1024 * 1024)
SMALL = pltpu.CompilerParams(vmem_limit_bytes=12 * 1024 * 1024)
IN_HBM = pl.BlockSpec(memory_space=pltpu.HBM)


def order_specs(deps):
    return [pl.BlockSpec(memory_space=pl.ANY)] * len(deps)


def same_block(array):
    return pl.BlockSpec(array.shape, lambda *args: (0,) * array.ndim)


def hi_lo(value, axis):
    hi = value.astype(BF16)
    lo = (value - hi.astype(F32)).astype(BF16)
    return jnp.concatenate([hi, lo], axis=axis)


def weight_copy(w_hbm, w_ref, sem, i):
    size = w_ref.shape[0] // PARTS
    rows = pl.ds(pl.multiple_of(i * size, size), size)
    return pltpu.make_async_copy(w_hbm.at[rows, :], w_ref.at[rows, :], sem.at[i])


def weight_block(w_hbm, w_ref, sem, i, steps):
    count = PARTS // steps
    for n in range(count):
        weight_copy(w_hbm, w_ref, sem, i * count + n).wait()
    for n in range(count):
        later = i * count + n + AHEAD

        @pl.when(later < PARTS)
        def _():
            weight_copy(w_hbm, w_ref, sem, later).start()


def factor_copies(tenant_ref, first, hbm, ref, sem, at):
    rank, nblk = hbm.shape[1], tenant_ref.shape[0] // BLOCK
    copies = []
    for b in range(ref.shape[0] // rank):
        src = hbm.at[tenant_ref[lax.rem(first + b, nblk) * BLOCK]]
        dst = ref.at[pl.ds(b * rank, rank), :]
        copies.append(pltpu.make_async_copy(src, dst, sem.at[at + b]))
    return copies


def norm_body(nblk, rank, tenant_ref, w_hbm, a_hbm, up_hbm, nsq_ref, *refs):
    w_ref, a_ref, up_ref, cross_ref, square_ref, w_sem, sem = refs
    cols = w_ref.shape[1]
    db = w_ref.shape[0] // STEPS
    copies = factor_copies(tenant_ref, 0, a_hbm, a_ref, sem, 0)
    late = factor_copies(tenant_ref, 0, up_hbm, up_ref, sem, nblk)
    for copy in copies:
        copy.start()
    for i in range(AHEAD):
        weight_copy(w_hbm, w_ref, w_sem, i).start()
    for copy in late:
        copy.start()
    cross_ref[...] = jnp.zeros_like(cross_ref)
    square_ref[...] = jnp.zeros_like(square_ref)
    for copy in copies:
        copy.wait()
    step = min(db, 256)

    def block(i, carry):
        weight_block(w_hbm, w_ref, w_sem, i, STEPS)
        squares = square_ref[...]
        for start in range(0, db, step):
            rows = pl.ds(pl.multiple_of(i * db + start, step), step)
            w = w_ref[rows, :]
            cross_ref[...] += jnp.dot(a_ref[:, rows], w, preferred_element_type=F32)
            for at in range(0, step, 16):
                wf = w[at : at + 16, :].astype(F32)
                squares = squares + wf[:8] * wf[:8] + wf[8:] * wf[8:]
        square_ref[...] = squares
        return carry

    lax.fori_loop(0, STEPS, block, 0)
    for copy in late:
        copy.wait()
    gram = lax.dot_general(a_ref[...], a_ref[...], LAST, preferred_element_type=F32)
    row = lax.broadcasted_iota(jnp.int32, gram.shape, 0) // rank
    col = lax.broadcasted_iota(jnp.int32, gram.shape, 1) // rank
    gram = jnp.where(row == col, gram, 0.0)
    up = up_ref[...].astype(F32)
    quad = jnp.dot(gram, up, preferred_element_type=F32, precision=HIGH)
    mixed = (up * (2.0 * cross_ref[...] + quad)).reshape(nblk, rank, cols)
    nsq_ref[...] = jnp.sum(mixed, axis=1) + jnp.sum(square_ref[...], axis=0, keepdims=True)


def partial_norms(tenant, weight, down, up):
    depth, cols = weight.shape
    rank = down.shape[1]
    nblk = tenant.shape[0] // BLOCK
    shape = jax.ShapeDtypeStruct((nblk, cols), F32)
    return pl.pallas_call(
        functools.partial(norm_body, nblk, rank),
        out_shape=shape,
        grid_spec=pltpu.PrefetchScalarGridSpec(
            num_scalar_prefetch=1,
            grid=(1,),
            in_specs=[IN_HBM] * 3,
            out_specs=same_block(shape),
            scratch_shapes=[
                pltpu.VMEM((depth, cols), BF16),
                pltpu.VMEM((nblk * rank, depth), BF16),
                pltpu.VMEM((nblk * rank, cols), BF16),
                pltpu.VMEM((nblk * rank, cols), F32),
                pltpu.VMEM((8, cols), F32),
                pltpu.SemaphoreType.DMA((PARTS,)),
                pltpu.SemaphoreType.DMA((2 * nblk,)),
            ],
        ),
        compiler_params=PARAMS,
        cost_estimate=COST,
        name="partial_norms",
    )(tenant, weight, down, up)


def grad_body(nb, rank, adds, tenant_ref, place_ref, cot_ref, nsq_a, nsq_b, mag_ref, *refs):
    w_hbm, a_hbm, up_hbm = refs[:3]
    if adds:
        add_core_body(*refs[3:5], *refs[-9:-7])
        refs = refs[:-9] + refs[-7:]
    scale_ref, sg_ref, keep_ref, send_ref = refs[-11:-7]
    w_ref, a_ref, up_ref, sgp_ref, backp_ref, w_sem, sem = refs[-7:]
    rows, db = sg_ref.shape[0], keep_ref.shape[1]
    piece = BLOCK // 4
    half = rows // 2
    step = pl.program_id(0)
    x, core, first = place_ref[1], place_ref[2], place_ref[3]

    @pl.when(step == 0)
    def _():
        copies = factor_copies(tenant_ref, first, up_hbm, up_ref, sem, 0)
        copies += factor_copies(tenant_ref, first, a_hbm, a_ref, sem, nb)
        for copy in copies:
            copy.start()
        for i in range(AHEAD):
            weight_copy(w_hbm, w_ref, w_sem, i).start()
        for b in range(nb):
            at = first + b
            total = nsq_a[pl.ds(at, 1), :] + nsq_b[pl.ds(at, 1), :]
            scale = mag_ref[pl.ds(tenant_ref[at * BLOCK], 1), :] / jnp.sqrt(total + EPS)
            scale_ref[b : b + 1, :] = scale
            here = slice(b * BLOCK, (b + 1) * BLOCK)
            sg_ref[here, :] = (cot_ref[here, :].astype(F32) * scale).astype(BF16)
        for fc in range(2):
            for fx in range(2):
                for b in range(nb):
                    c = b * 4 + (x ^ fx) * 2 + (core ^ fc)
                    src = pl.ds(pl.multiple_of(c * piece, piece), piece)
                    at = ((fc * 2 + fx) * nb + b) * piece
                    sgp_ref[at : at + piece, :] = sg_ref[src, :]
        for copy in copies:
            copy.wait()
        back = lax.dot_general(sgp_ref[...], up_ref[...], LAST, preferred_element_type=F32)
        block = lax.broadcasted_iota(jnp.int32, back.shape, 0) // piece % nb
        owner = lax.broadcasted_iota(jnp.int32, back.shape, 1) // rank
        backp_ref[...] = hi_lo(jnp.where(owner == block, back, 0.0), 1)

    weight_block(w_hbm, w_ref, w_sem, step, STEPS)
    at = pl.ds(pl.multiple_of(step * db, db), db)
    down = a_ref[:, at]
    down = jnp.concatenate([down, down], axis=0)
    part = lax.dot_general(sgp_ref[...], w_ref[at, :], LAST, preferred_element_type=F32)
    part = part + jnp.dot(backp_ref[...], down, preferred_element_type=F32)
    keep_ref[...] = part[:half, :]
    send_ref[...] = part[half:, :].astype(BF16)


def input_gradient(tenant, place, cot, nsq_a, nsq_b, magnitude, weight, down, up, add, deps):
    depth, cols = weight.shape
    rows = cot.shape[0]
    nb = rows // BLOCK
    rank = down.shape[1]
    db = depth // STEPS
    shapes = (
        jax.ShapeDtypeStruct((nb, cols), F32),
        jax.ShapeDtypeStruct((rows, cols), BF16),
        jax.ShapeDtypeStruct((rows // 2, depth), F32),
        jax.ShapeDtypeStruct((rows // 2, depth), BF16),
    )
    if add:
        shapes += tuple(jax.ShapeDtypeStruct((rows // 4, depth), t) for t in (F32, BF16))

    def columns(array):
        return pl.BlockSpec((array.shape[0], db), lambda i, t, p: (0, i))

    return pl.pallas_call(
        functools.partial(grad_body, nb, rank, len(add)),
        out_shape=shapes,
        grid_spec=pltpu.PrefetchScalarGridSpec(
            num_scalar_prefetch=2,
            grid=(STEPS,),
            in_specs=[same_block(a) for a in (cot, nsq_a, nsq_b, magnitude)]
            + [IN_HBM] * 3
            + [columns(a) for a in add]
            + order_specs(deps),
            out_specs=[same_block(s) for s in shapes[:2]] + [columns(s) for s in shapes[2:]],
            scratch_shapes=[
                pltpu.VMEM((depth, cols), BF16),
                pltpu.VMEM((nb * rank, depth), BF16),
                pltpu.VMEM((nb * rank, cols), BF16),
                pltpu.VMEM((rows, cols), BF16),
                pltpu.VMEM((rows, 2 * nb * rank), BF16),
                pltpu.SemaphoreType.DMA((PARTS,)),
                pltpu.SemaphoreType.DMA((2 * nb,)),
            ],
        ),
        compiler_params=PARAMS,
        cost_estimate=COST,
        name="input_gradient",
    )(tenant, place, cot, nsq_a, nsq_b, magnitude, weight, down, up, *add, *deps)


def add_core_body(keep_ref, recv_ref, *refs):
    mine_ref, send_ref = refs[-2:]
    half = mine_ref.shape[0]
    mine_ref[...] = keep_ref[:half, :] + recv_ref[:half, :].astype(F32)
    send_ref[...] = (keep_ref[half:, :] + recv_ref[half:, :].astype(F32)).astype(BF16)


def add_core(keep, recv, deps):
    rows, size = keep.shape
    block = size // 2
    return pl.pallas_call(
        add_core_body,
        out_shape=(
            jax.ShapeDtypeStruct((rows // 2, size), F32),
            jax.ShapeDtypeStruct((rows // 2, size), BF16),
        ),
        grid=(2,),
        in_specs=[pl.BlockSpec((rows, block), lambda i: (0, i))] * 2 + order_specs(deps),
        out_specs=[pl.BlockSpec((rows // 2, block), lambda i: (0, i))] * 2,
        compiler_params=SMALL,
        cost_estimate=COST,
        name="add_core",
    )(keep, recv, *deps)


def add_x_body(groups, nz, place_ref, *refs):
    outs, total_ref = refs[-nz - 1 : -1], refs[-1]
    piece = outs[0].shape[0]
    z = place_ref[0]
    for g in range(groups):
        keep_ref, recv_ref = refs[2 * g : 2 * g + 2]
        first = pl.multiple_of(place_ref[3 + g] * piece, piece)
        total = keep_ref[...] + recv_ref[...].astype(F32)
        total_ref[pl.ds(first, keep_ref.shape[0]), :] = total
    for k in range(nz):
        at = pl.multiple_of(lax.rem(z + k, nz) * piece, piece)
        outs[k][...] = total_ref[pl.ds(at, piece), :].astype(outs[k].dtype)


def add_x(place, pairs, nz, deps):
    piece = BLOCK // 4
    size = pairs[0][0].shape[1]
    block = size // 2
    operands = [array for pair in pairs for array in pair]

    def spec(array):
        return pl.BlockSpec((array.shape[0], block), lambda i, p: (0, i))

    shapes = tuple(jax.ShapeDtypeStruct((piece, size), BF16 if k else F32) for k in range(nz))
    return pl.pallas_call(
        functools.partial(add_x_body, len(pairs), nz),
        out_shape=shapes,
        grid_spec=pltpu.PrefetchScalarGridSpec(
            num_scalar_prefetch=1,
            grid=(2,),
            in_specs=[spec(a) for a in operands] + order_specs(deps),
            out_specs=[spec(s) for s in shapes],
            scratch_shapes=[pltpu.VMEM((nz * piece, block), F32)],
        ),
        compiler_params=SMALL,
        cost_estimate=COST,
        name="add_x",
    )(place, *operands, *deps)


def add_z_body(*refs):
    total = refs[0][...]
    for ref in refs[1:-1]:
        total = total + ref[...].astype(F32)
    refs[-1][...] = total.astype(BF16)


def add_z(parts):
    return pl.pallas_call(
        add_z_body,
        out_shape=jax.ShapeDtypeStruct(parts[0].shape, BF16),
        in_specs=[pl.BlockSpec(memory_space=pltpu.VMEM)] * len(parts),
        compiler_params=SMALL,
        cost_estimate=COST,
        name="add_z",
    )(*parts)


def forward_body(nb, rank, nz, tenant_ref, place_ref, cot_ref, w_hbm, a_hbm, up_hbm, *refs):
    pieces = refs[: 2 * nz + 2]
    part_ref, dot_ref, low_ref = refs[-12:-9]
    w_ref, a_ref, up_ref, x_ref, acc_ref, low_acc, w_sem, sem, x_sem = refs[-9:]
    rows, cols = acc_ref.shape
    piece = BLOCK // 4
    depth = w_ref.shape[0]
    steps = STEPS
    db = depth // steps
    z, x, core, first = place_ref[0], place_ref[1], place_ref[2], place_ref[3]

    def each(h, act):
        at = pl.ds(h * depth // 2, depth // 2)
        for n in range(4 * nz):
            k, fx, fc = n // 4, (n // 2) % 2, n % 2
            src = pieces[2 * nz + fx] if fc else pieces[2 * k + fx]
            src = src.at[pl.ds(k * piece if fc else 0, piece), at]
            b = lax.rem(z + (nz - k), nz) - first

            @pl.when(jnp.logical_and(b >= 0, b < nb))
            def _():
                row = (b * 4 + (x ^ fx) * 2 + (core ^ fc)) * piece
                dst = pl.ds(pl.multiple_of(row, piece), piece)
                act(pltpu.make_async_copy(src, x_ref.at[dst, at], x_sem.at[h, n]))

    copies = factor_copies(tenant_ref, first, a_hbm, a_ref, sem, 0)
    late = factor_copies(tenant_ref, first, up_hbm, up_ref, sem, nb)
    each(0, lambda copy: copy.start())
    for copy in copies:
        copy.start()
    for i in range(AHEAD):
        weight_copy(w_hbm, w_ref, w_sem, i).start()
    each(1, lambda copy: copy.start())
    for copy in late:
        copy.start()
    acc_ref[...] = jnp.zeros_like(acc_ref)
    low_acc[...] = jnp.zeros_like(low_acc)
    for copy in copies:
        copy.wait()

    def block(i, carry):
        for h in range(2):

            @pl.when(i == h * (steps // 2))
            def _():
                each(h, lambda copy: copy.wait())

        weight_block(w_hbm, w_ref, w_sem, i, steps)
        at = pl.ds(pl.multiple_of(i * db, db), db)
        xs = x_ref[:, at]
        acc_ref[...] += jnp.dot(xs, w_ref[at, :], preferred_element_type=F32)
        low_acc[...] += lax.dot_general(a_ref[:, at], xs, LAST, preferred_element_type=F32)
        return carry

    lax.fori_loop(0, steps, block, 0)
    low = low_acc[...]
    owner = lax.broadcasted_iota(jnp.int32, low.shape, 0) // rank
    block_of = lax.broadcasted_iota(jnp.int32, low.shape, 1) // BLOCK
    low = jnp.where(owner == block_of, low, 0.0)
    low_ref[...] = jnp.sum(low.reshape(nb, rank, rows), axis=0)
    hi = low.astype(BF16).astype(F32)
    lowcat = jnp.concatenate([hi, low - hi], axis=0).T.astype(BF16)
    for copy in late:
        copy.wait()
    up = up_ref[...]
    up = jnp.concatenate([up, up], axis=0)
    for i in range(nb):
        here = slice(i * BLOCK, (i + 1) * BLOCK)
        part = acc_ref[here, :] + jnp.dot(lowcat[here, :], up, preferred_element_type=F32)
        part_ref[here, :] = part.astype(part_ref.dtype)
        product = part * cot_ref[here, :].astype(F32)
        dot_ref[i : i + 1, :] = jnp.sum(product, axis=0, keepdims=True)


def forward(tenant, place, weight, cot, down, up, pieces, nz, out_dtype, deps):
    depth, cols = weight.shape
    rows = cot.shape[0]
    nb = rows // BLOCK
    rank = down.shape[1]
    shapes = (
        jax.ShapeDtypeStruct((rows, cols), out_dtype),
        jax.ShapeDtypeStruct((nb, cols), F32),
        jax.ShapeDtypeStruct((rank, rows), F32),
    )
    return pl.pallas_call(
        functools.partial(forward_body, nb, rank, nz),
        out_shape=shapes,
        grid_spec=pltpu.PrefetchScalarGridSpec(
            num_scalar_prefetch=2,
            grid=(1,),
            in_specs=[same_block(cot)] + [IN_HBM] * (3 + len(pieces)) + order_specs(deps),
            out_specs=[same_block(s) for s in shapes],
            scratch_shapes=[
                pltpu.VMEM((depth, cols), BF16),
                pltpu.VMEM((nb * rank, depth), BF16),
                pltpu.VMEM((nb * rank, cols), BF16),
                pltpu.VMEM((rows, depth), BF16),
                pltpu.VMEM((rows, cols), F32),
                pltpu.VMEM((nb * rank, rows), F32),
                pltpu.SemaphoreType.DMA((PARTS,)),
                pltpu.SemaphoreType.DMA((2 * nb,)),
                pltpu.SemaphoreType.DMA((2, 4 * nz)),
            ],
        ),
        compiler_params=PARAMS,
        cost_estimate=COST,
        name="forward",
    )(tenant, place, cot, weight, down, up, *pieces, *deps)


def shards(inputs, weight, adapter_down_factors, adapter_up_factors, magnitude, cotangent, tenant):
    col_count, row_count = lax.axis_size("col"), lax.axis_size("row")
    nz = col_count // 4
    down, up = adapter_down_factors, adapter_up_factors
    tenant_number, rank, depth = down.shape
    cols = weight.shape[1]
    tokens = tenant.shape[0]
    nblk = tokens // BLOCK
    rows_row = tokens // row_count
    blocks_mine = rows_row // BLOCK
    col, row = lax.axis_index("col"), lax.axis_index("row")
    z, x, core = col >> 2, (col >> 1) & 1, col & 1

    def move(value, dz, fx, fc):
        perm = []
        for source in range(col_count):
            sz, sx, sc = source // 4, (source // 2) % 2, source % 2
            perm.append((source, ((sz + dz) % nz) * 4 + (sx ^ fx) * 2 + (sc ^ fc)))
        return lax.ppermute(value, "col", perm)

    def swap(value):
        return lax.ppermute(value, "row", [(0, 1), (1, 0)])

    def place(*firsts):
        return jnp.stack([z, x, core, *firsts]).astype(jnp.int32)

    pair = row_count == 2

    def once(value, other):
        return lax.optimization_barrier((value, other))[0]

    along_z = [inputs] + [move(inputs, k, 0, 0) for k in range(1, nz)]
    along_x = {0: move(inputs, 0, 1, 0)}

    def other_x(k, after):
        along_z[k] = once(along_z[k], after)
        along_x[k] = move(along_z[k], 0, 1, 0)

    def other_core(part):
        return move(jnp.concatenate(part, axis=0), 0, 0, 1)

    nsq = partial_norms(tenant, weight, down, up)
    if pair:
        nsq_a, nsq_b = nsq, swap(once(nsq, along_x[0]))
        firsts = [row * blocks_mine, (1 - row) * blocks_mine]
        cots = [cotangent, swap(cotangent)]
    else:
        nsq_a, nsq_b = lax.psum(nsq, "row"), jnp.zeros_like(nsq)
        firsts = [0 * row]
        cots = [lax.all_gather(cotangent, "row", axis=0, tiled=True)]
    places = [place(first) for first in firsts]

    def gradient(g, add, deps):
        return input_gradient(
            tenant, places[g], cots[g], nsq_a, nsq_b, magnitude, weight, down, up, add, deps
        )

    def cross_core(made, deps):
        return add_core(made[2], move(made[3], 0, 0, 1), deps)

    def cross_x(pairs, deps):
        mine, *away = add_x(place(*firsts), pairs, nz, deps)
        return [mine] + [move(block, k + 1, 0, 0) for k, block in enumerate(away)]

    def across_x(made):
        return made[0], move(made[1], 0, 1, 0)

    if pair:
        ours = gradient(0, [], [cots[1]])
        for k in [nz - 1] + list(range(1, nz - 1)):
            other_x(k, ours[0])
        core_z = other_core(along_z)
        theirs = gradient(1, [ours[2], move(ours[3], 0, 0, 1)], [core_z])
        near = across_x(theirs[4:])
        along_x = [along_x[k] for k in range(nz)]
        along_x[nz - 2] = once(along_x[nz - 2], theirs[0])
        core_x = other_core(along_x)
        far = cross_core(theirs, [core_x])
        pieces = [piece for both in zip(along_z, along_x) for piece in both] + [core_z, core_x]

        def project(g, out_dtype, deps):
            return forward(
                tenant, places[g], weight, cots[g], down, up, pieces, nz, out_dtype, deps
            )

        away, dots_away, low_away = project(1, BF16, [far[0]])
        arrived = swap(away)
        finals = cross_x([near, across_x(far)], [dots_away])
        part, dots_here, low_here = project(0, F32, [finals[0]])
        dots = jnp.concatenate([dots_here, dots_away], axis=0)
        low = jnp.concatenate([low_here, low_away], axis=1)
        late = (finals[nz // 2], finals[nz - 1])
        dots = dots + jnp.roll(swap(once(dots, late)), blocks_mine, axis=0)
        low = low + jnp.roll(swap(once(low, late)), rows_row, axis=1)
        parts = [ours, theirs]
    else:
        ours = gradient(0, [], [])
        near = across_x(cross_core(ours, []))
        for k in range(1, nz):
            other_x(k, inputs)
        along_x = [along_x[k] for k in range(nz)]
        pieces = [piece for both in zip(along_z, along_x) for piece in both]
        pieces += [other_core(along_z), other_core(along_x)]
        part, dots, low = forward(
            tenant, places[0], weight, cots[0], down, up, pieces, nz, F32, []
        )
        finals = cross_x([near], [])
        low, dots = lax.psum((low, dots), "row")
        parts = [ours]

    scales = jnp.concatenate([group[0] for group in parts], axis=0)

    tenants = jnp.arange(tenant_number, dtype=jnp.int32)
    block_tenant = tenant.reshape(nblk, BLOCK)[:, 0]
    size = nblk // len(parts)
    owners = jnp.concatenate(
        [lax.dynamic_slice_in_dim(block_tenant, first, size, 0) for first in firsts]
    )
    low = low.astype(BF16)
    grad_b = 0.0
    for g, group in enumerate(parts):
        owner = jnp.repeat(owners[g * size : (g + 1) * size], BLOCK)
        mine = low[:, g * size * BLOCK : (g + 1) * size * BLOCK]
        wide = jnp.where((tenants[:, None] == owner[None, :])[:, None, :], mine[None], 0)
        wide = wide.reshape(tenant_number * rank, size * BLOCK)
        grad_b = grad_b + jnp.dot(wide, group[1], preferred_element_type=F32)
    grad_b = grad_b.reshape(tenant_number, rank, cols)
    hit = (tenants[:, None] == owners[None, :])[:, :, None]
    terms = jnp.where(hit, (dots * scales)[None], 0.0)
    grad_m = 0.0
    for g in range(len(parts)):
        group = terms[:, g * size : (g + 1) * size]
        grad_m = grad_m + functools.reduce(jnp.add, [group[:, i] for i in range(size)])
    grad_inputs = add_z([once(finals[0], grad_b)] + finals[1:])
    if pair:
        pre = part + arrived.astype(F32)
        scale_mine = parts[0][0]
    else:
        pre = lax.psum_scatter(part, "row", scatter_dimension=0, tiled=True)
        scale_mine = lax.dynamic_slice_in_dim(scales, row * blocks_mine, blocks_mine, 0)
    output = (pre.reshape(blocks_mine, BLOCK, cols) * scale_mine[:, None, :]).astype(BF16)
    output = output.reshape(rows_row, cols)
    return (output, grad_inputs, grad_b, grad_m / magnitude)


def solution(mesh):
    return jax.shard_map(
        shards,
        mesh=mesh,
        in_specs=(
            P("col", "row"),
            P("row", "col"),
            P(None, None, "row"),
            P(None, None, "col"),
            P(None, "col"),
            P("row", "col"),
            P(),
        ),
        out_specs=(P("row", "col"), P("col", "row"), P(None, None, "col"), P(None, "col")),
        check_vma=False,
    )
```

```python
import functools

import jax
import jax.numpy as jnp
from jax import lax
from jax.experimental import pallas as pl
from jax.experimental.pallas import tpu as pltpu
from jax.sharding import PartitionSpec as P

BLOCK = 128
EPS = 1e-06
HIGH = lax.Precision.HIGHEST
STEPS = 8
PARTS = 16
AHEAD = 6
F32 = jnp.float32
BF16 = jnp.bfloat16
COST = pl.CostEstimate(flops=1000, bytes_accessed=1000, transcendentals=0)
LAST = (((1,), (1,)), ((), ()))
PARAMS = pltpu.CompilerParams(vmem_limit_bytes=52 * 1024 * 1024)
SMALL = pltpu.CompilerParams(vmem_limit_bytes=12 * 1024 * 1024)
IN_HBM = pl.BlockSpec(memory_space=pltpu.HBM)


def order_specs(deps):
    return [pl.BlockSpec(memory_space=pl.ANY)] * len(deps)


def same_block(array):
    return pl.BlockSpec(array.shape, lambda *args: (0,) * array.ndim)


def hi_lo(value, axis):
    hi = value.astype(BF16)
    lo = (value - hi.astype(F32)).astype(BF16)
    return jnp.concatenate([hi, lo], axis=axis)


def weight_copy(w_hbm, w_ref, sem, i):
    size = w_ref.shape[0] // PARTS
    rows = pl.ds(pl.multiple_of(i * size, size), size)
    return pltpu.make_async_copy(w_hbm.at[rows, :], w_ref.at[rows, :], sem.at[i])


def weight_block(w_hbm, w_ref, sem, i, steps):
    count = PARTS // steps
    for n in range(count):
        weight_copy(w_hbm, w_ref, sem, i * count + n).wait()
    for n in range(count):
        later = i * count + n + AHEAD

        @pl.when(later < PARTS)
        def _():
            weight_copy(w_hbm, w_ref, sem, later).start(priority=(n + AHEAD) % 2)


def factor_copies(tenant_ref, first, hbm, ref, sem, at):
    rank, nblk = hbm.shape[1], tenant_ref.shape[0] // BLOCK
    copies = []
    for b in range(ref.shape[0] // rank):
        src = hbm.at[tenant_ref[lax.rem(first + b, nblk) * BLOCK]]
        dst = ref.at[pl.ds(b * rank, rank), :]
        copies.append(pltpu.make_async_copy(src, dst, sem.at[at + b]))
    return copies


def norm_body(nblk, rank, tenant_ref, w_hbm, a_hbm, up_hbm, nsq_ref, *refs):
    w_ref, a_ref, up_ref, cross_ref, square_ref, w_sem, sem = refs
    cols = w_ref.shape[1]
    db = w_ref.shape[0] // STEPS
    copies = factor_copies(tenant_ref, 0, a_hbm, a_ref, sem, 0)
    late = factor_copies(tenant_ref, 0, up_hbm, up_ref, sem, nblk)
    for copy in copies:
        copy.start()
    for i in range(AHEAD):
        weight_copy(w_hbm, w_ref, w_sem, i).start(priority=i % 2)
    for copy in late:
        copy.start()
    cross_ref[...] = jnp.zeros_like(cross_ref)
    square_ref[...] = jnp.zeros_like(square_ref)
    for copy in copies:
        copy.wait()
    step = min(db, 256)

    def block(i, carry):
        weight_block(w_hbm, w_ref, w_sem, i, STEPS)
        squares = square_ref[...]
        for start in range(0, db, step):
            rows = pl.ds(pl.multiple_of(i * db + start, step), step)
            w = w_ref[rows, :]
            cross_ref[...] += jnp.dot(a_ref[:, rows], w, preferred_element_type=F32)
            for at in range(0, step, 16):
                wf = w[at : at + 16, :].astype(F32)
                squares = squares + wf[:8] * wf[:8] + wf[8:] * wf[8:]
        square_ref[...] = squares
        return carry

    lax.fori_loop(0, STEPS, block, 0)
    for copy in late:
        copy.wait()
    gram = lax.dot_general(a_ref[...], a_ref[...], LAST, preferred_element_type=F32)
    row = lax.broadcasted_iota(jnp.int32, gram.shape, 0) // rank
    col = lax.broadcasted_iota(jnp.int32, gram.shape, 1) // rank
    gram = jnp.where(row == col, gram, 0.0)
    up = up_ref[...].astype(F32)
    quad = jnp.dot(gram, up, preferred_element_type=F32, precision=HIGH)
    mixed = (up * (2.0 * cross_ref[...] + quad)).reshape(nblk, rank, cols)
    nsq_ref[...] = jnp.sum(mixed, axis=1) + jnp.sum(square_ref[...], axis=0, keepdims=True)


def partial_norms(tenant, weight, down, up):
    depth, cols = weight.shape
    rank = down.shape[1]
    nblk = tenant.shape[0] // BLOCK
    shape = jax.ShapeDtypeStruct((nblk, cols), F32)
    return pl.pallas_call(
        functools.partial(norm_body, nblk, rank),
        out_shape=shape,
        grid_spec=pltpu.PrefetchScalarGridSpec(
            num_scalar_prefetch=1,
            grid=(1,),
            in_specs=[IN_HBM] * 3,
            out_specs=same_block(shape),
            scratch_shapes=[
                pltpu.VMEM((depth, cols), BF16),
                pltpu.VMEM((nblk * rank, depth), BF16),
                pltpu.VMEM((nblk * rank, cols), BF16),
                pltpu.VMEM((nblk * rank, cols), F32),
                pltpu.VMEM((8, cols), F32),
                pltpu.SemaphoreType.DMA((PARTS,)),
                pltpu.SemaphoreType.DMA((2 * nblk,)),
            ],
        ),
        compiler_params=PARAMS,
        cost_estimate=COST,
        name="partial_norms",
    )(tenant, weight, down, up)


def grad_body(nb, rank, adds, tenant_ref, place_ref, cot_ref, nsq_a, nsq_b, mag_ref, *refs):
    w_hbm, a_hbm, up_hbm = refs[:3]
    if adds:
        add_core_body(*refs[3:5], *refs[-9:-7])
        refs = refs[:-9] + refs[-7:]
    scale_ref, sg_ref, keep_ref, send_ref = refs[-11:-7]
    w_ref, a_ref, up_ref, sgp_ref, backp_ref, w_sem, sem = refs[-7:]
    rows, db = sg_ref.shape[0], keep_ref.shape[1]
    piece = BLOCK // 4
    half = rows // 2
    step = pl.program_id(0)
    x, core, first = place_ref[1], place_ref[2], place_ref[3]

    @pl.when(step == 0)
    def _():
        copies = factor_copies(tenant_ref, first, up_hbm, up_ref, sem, 0)
        copies += factor_copies(tenant_ref, first, a_hbm, a_ref, sem, nb)
        for copy in copies:
            copy.start()
        for i in range(AHEAD):
            weight_copy(w_hbm, w_ref, w_sem, i).start(priority=i % 2)
        for b in range(nb):
            at = first + b
            total = nsq_a[pl.ds(at, 1), :] + nsq_b[pl.ds(at, 1), :]
            scale = mag_ref[pl.ds(tenant_ref[at * BLOCK], 1), :] / jnp.sqrt(total + EPS)
            scale_ref[b : b + 1, :] = scale
            here = slice(b * BLOCK, (b + 1) * BLOCK)
            sg_ref[here, :] = (cot_ref[here, :].astype(F32) * scale).astype(BF16)
        for fc in range(2):
            for fx in range(2):
                for b in range(nb):
                    c = b * 4 + (x ^ fx) * 2 + (core ^ fc)
                    src = pl.ds(pl.multiple_of(c * piece, piece), piece)
                    at = ((fc * 2 + fx) * nb + b) * piece
                    sgp_ref[at : at + piece, :] = sg_ref[src, :]
        for copy in copies:
            copy.wait()
        back = lax.dot_general(sgp_ref[...], up_ref[...], LAST, preferred_element_type=F32)
        block = lax.broadcasted_iota(jnp.int32, back.shape, 0) // piece % nb
        owner = lax.broadcasted_iota(jnp.int32, back.shape, 1) // rank
        backp_ref[...] = hi_lo(jnp.where(owner == block, back, 0.0), 1)

    weight_block(w_hbm, w_ref, w_sem, step, STEPS)
    at = pl.ds(pl.multiple_of(step * db, db), db)
    down = a_ref[:, at]
    down = jnp.concatenate([down, down], axis=0)
    part = lax.dot_general(sgp_ref[...], w_ref[at, :], LAST, preferred_element_type=F32)
    part = part + jnp.dot(backp_ref[...], down, preferred_element_type=F32)
    keep_ref[...] = part[:half, :]
    send_ref[...] = part[half:, :].astype(BF16)


def input_gradient(tenant, place, cot, nsq_a, nsq_b, magnitude, weight, down, up, add, deps):
    depth, cols = weight.shape
    rows = cot.shape[0]
    nb = rows // BLOCK
    rank = down.shape[1]
    db = depth // STEPS
    shapes = (
        jax.ShapeDtypeStruct((nb, cols), F32),
        jax.ShapeDtypeStruct((rows, cols), BF16),
        jax.ShapeDtypeStruct((rows // 2, depth), F32),
        jax.ShapeDtypeStruct((rows // 2, depth), BF16),
    )
    if add:
        shapes += tuple(jax.ShapeDtypeStruct((rows // 4, depth), t) for t in (F32, BF16))

    def columns(array):
        return pl.BlockSpec((array.shape[0], db), lambda i, t, p: (0, i))

    return pl.pallas_call(
        functools.partial(grad_body, nb, rank, len(add)),
        out_shape=shapes,
        grid_spec=pltpu.PrefetchScalarGridSpec(
            num_scalar_prefetch=2,
            grid=(STEPS,),
            in_specs=[same_block(a) for a in (cot, nsq_a, nsq_b, magnitude)]
            + [IN_HBM] * 3
            + [columns(a) for a in add]
            + order_specs(deps),
            out_specs=[same_block(s) for s in shapes[:2]] + [columns(s) for s in shapes[2:]],
            scratch_shapes=[
                pltpu.VMEM((depth, cols), BF16),
                pltpu.VMEM((nb * rank, depth), BF16),
                pltpu.VMEM((nb * rank, cols), BF16),
                pltpu.VMEM((rows, cols), BF16),
                pltpu.VMEM((rows, 2 * nb * rank), BF16),
                pltpu.SemaphoreType.DMA((PARTS,)),
                pltpu.SemaphoreType.DMA((2 * nb,)),
            ],
        ),
        compiler_params=PARAMS,
        cost_estimate=COST,
        name="input_gradient",
    )(tenant, place, cot, nsq_a, nsq_b, magnitude, weight, down, up, *add, *deps)


def add_core_body(keep_ref, recv_ref, *refs):
    mine_ref, send_ref = refs[-2:]
    half = mine_ref.shape[0]
    mine_ref[...] = keep_ref[:half, :] + recv_ref[:half, :].astype(F32)
    send_ref[...] = (keep_ref[half:, :] + recv_ref[half:, :].astype(F32)).astype(BF16)


def add_core(keep, recv, deps):
    rows, size = keep.shape
    block = size // 2
    return pl.pallas_call(
        add_core_body,
        out_shape=(
            jax.ShapeDtypeStruct((rows // 2, size), F32),
            jax.ShapeDtypeStruct((rows // 2, size), BF16),
        ),
        grid=(2,),
        in_specs=[pl.BlockSpec((rows, block), lambda i: (0, i))] * 2 + order_specs(deps),
        out_specs=[pl.BlockSpec((rows // 2, block), lambda i: (0, i))] * 2,
        compiler_params=SMALL,
        cost_estimate=COST,
        name="add_core",
    )(keep, recv, *deps)


def add_x_body(groups, nz, place_ref, *refs):
    outs, total_ref = refs[-nz - 1 : -1], refs[-1]
    piece = outs[0].shape[0]
    z = place_ref[0]
    for g in range(groups):
        keep_ref, recv_ref = refs[2 * g : 2 * g + 2]
        first = pl.multiple_of(place_ref[3 + g] * piece, piece)
        total = keep_ref[...] + recv_ref[...].astype(F32)
        total_ref[pl.ds(first, keep_ref.shape[0]), :] = total
    for k in range(nz):
        at = pl.multiple_of(lax.rem(z + k, nz) * piece, piece)
        outs[k][...] = total_ref[pl.ds(at, piece), :].astype(outs[k].dtype)


def add_x(place, pairs, nz, deps):
    piece = BLOCK // 4
    size = pairs[0][0].shape[1]
    block = size // 2
    operands = [array for pair in pairs for array in pair]

    def spec(array):
        return pl.BlockSpec((array.shape[0], block), lambda i, p: (0, i))

    shapes = tuple(jax.ShapeDtypeStruct((piece, size), BF16 if k else F32) for k in range(nz))
    return pl.pallas_call(
        functools.partial(add_x_body, len(pairs), nz),
        out_shape=shapes,
        grid_spec=pltpu.PrefetchScalarGridSpec(
            num_scalar_prefetch=1,
            grid=(2,),
            in_specs=[spec(a) for a in operands] + order_specs(deps),
            out_specs=[spec(s) for s in shapes],
            scratch_shapes=[pltpu.VMEM((nz * piece, block), F32)],
        ),
        compiler_params=SMALL,
        cost_estimate=COST,
        name="add_x",
    )(place, *operands, *deps)


def add_z_body(*refs):
    total = refs[0][...]
    for ref in refs[1:-1]:
        total = total + ref[...].astype(F32)
    refs[-1][...] = total.astype(BF16)


def add_z(parts):
    return pl.pallas_call(
        add_z_body,
        out_shape=jax.ShapeDtypeStruct(parts[0].shape, BF16),
        in_specs=[pl.BlockSpec(memory_space=pltpu.VMEM)] * len(parts),
        compiler_params=SMALL,
        cost_estimate=COST,
        name="add_z",
    )(*parts)


def forward_body(nb, rank, nz, tenant_ref, place_ref, cot_ref, w_hbm, a_hbm, up_hbm, *refs):
    pieces = refs[: 2 * nz + 2]
    part_ref, dot_ref, low_ref = refs[-12:-9]
    w_ref, a_ref, up_ref, x_ref, acc_ref, low_acc, w_sem, sem, x_sem = refs[-9:]
    rows, cols = acc_ref.shape
    piece = BLOCK // 4
    depth = w_ref.shape[0]
    steps = STEPS
    db = depth // steps
    z, x, core, first = place_ref[0], place_ref[1], place_ref[2], place_ref[3]

    def each(h, act):
        at = pl.ds(h * depth // 2, depth // 2)
        for n in range(4 * nz):
            k, fx, fc = n // 4, (n // 2) % 2, n % 2
            src = pieces[2 * nz + fx] if fc else pieces[2 * k + fx]
            src = src.at[pl.ds(k * piece if fc else 0, piece), at]
            b = lax.rem(z + (nz - k), nz) - first

            @pl.when(jnp.logical_and(b >= 0, b < nb))
            def _():
                row = (b * 4 + (x ^ fx) * 2 + (core ^ fc)) * piece
                dst = pl.ds(pl.multiple_of(row, piece), piece)
                act(pltpu.make_async_copy(src, x_ref.at[dst, at], x_sem.at[h, n]), n % 2)

    copies = factor_copies(tenant_ref, first, a_hbm, a_ref, sem, 0)
    late = factor_copies(tenant_ref, first, up_hbm, up_ref, sem, nb)
    each(0, lambda copy, queue: copy.start(priority=queue))
    for copy in copies:
        copy.start()
    for i in range(AHEAD):
        weight_copy(w_hbm, w_ref, w_sem, i).start(priority=i % 2)
    each(1, lambda copy, queue: copy.start(priority=queue))
    for copy in late:
        copy.start()
    acc_ref[...] = jnp.zeros_like(acc_ref)
    low_acc[...] = jnp.zeros_like(low_acc)
    for copy in copies:
        copy.wait()

    def block(i, carry):
        for h in range(2):

            @pl.when(i == h * (steps // 2))
            def _():
                each(h, lambda copy, queue: copy.wait())

        weight_block(w_hbm, w_ref, w_sem, i, steps)
        at = pl.ds(pl.multiple_of(i * db, db), db)
        xs = x_ref[:, at]
        acc_ref[...] += jnp.dot(xs, w_ref[at, :], preferred_element_type=F32)
        low_acc[...] += lax.dot_general(a_ref[:, at], xs, LAST, preferred_element_type=F32)
        return carry

    lax.fori_loop(0, steps, block, 0)
    low = low_acc[...]
    owner = lax.broadcasted_iota(jnp.int32, low.shape, 0) // rank
    block_of = lax.broadcasted_iota(jnp.int32, low.shape, 1) // BLOCK
    low = jnp.where(owner == block_of, low, 0.0)
    low_ref[...] = jnp.sum(low.reshape(nb, rank, rows), axis=0)
    hi = low.astype(BF16).astype(F32)
    lowcat = jnp.concatenate([hi, low - hi], axis=0).T.astype(BF16)
    for copy in late:
        copy.wait()
    up = up_ref[...]
    up = jnp.concatenate([up, up], axis=0)
    for i in range(nb):
        here = slice(i * BLOCK, (i + 1) * BLOCK)
        part = acc_ref[here, :] + jnp.dot(lowcat[here, :], up, preferred_element_type=F32)
        part_ref[here, :] = part.astype(part_ref.dtype)
        product = part * cot_ref[here, :].astype(F32)
        dot_ref[i : i + 1, :] = jnp.sum(product, axis=0, keepdims=True)


def forward(tenant, place, weight, cot, down, up, pieces, nz, out_dtype, deps):
    depth, cols = weight.shape
    rows = cot.shape[0]
    nb = rows // BLOCK
    rank = down.shape[1]
    shapes = (
        jax.ShapeDtypeStruct((rows, cols), out_dtype),
        jax.ShapeDtypeStruct((nb, cols), F32),
        jax.ShapeDtypeStruct((rank, rows), F32),
    )
    return pl.pallas_call(
        functools.partial(forward_body, nb, rank, nz),
        out_shape=shapes,
        grid_spec=pltpu.PrefetchScalarGridSpec(
            num_scalar_prefetch=2,
            grid=(1,),
            in_specs=[same_block(cot)] + [IN_HBM] * (3 + len(pieces)) + order_specs(deps),
            out_specs=[same_block(s) for s in shapes],
            scratch_shapes=[
                pltpu.VMEM((depth, cols), BF16),
                pltpu.VMEM((nb * rank, depth), BF16),
                pltpu.VMEM((nb * rank, cols), BF16),
                pltpu.VMEM((rows, depth), BF16),
                pltpu.VMEM((rows, cols), F32),
                pltpu.VMEM((nb * rank, rows), F32),
                pltpu.SemaphoreType.DMA((PARTS,)),
                pltpu.SemaphoreType.DMA((2 * nb,)),
                pltpu.SemaphoreType.DMA((2, 4 * nz)),
            ],
        ),
        compiler_params=PARAMS,
        cost_estimate=COST,
        name="forward",
    )(tenant, place, cot, weight, down, up, *pieces, *deps)


def shards(inputs, weight, adapter_down_factors, adapter_up_factors, magnitude, cotangent, tenant):
    col_count, row_count = lax.axis_size("col"), lax.axis_size("row")
    nz = col_count // 4
    down, up = adapter_down_factors, adapter_up_factors
    tenant_number, rank, depth = down.shape
    cols = weight.shape[1]
    tokens = tenant.shape[0]
    nblk = tokens // BLOCK
    rows_row = tokens // row_count
    blocks_mine = rows_row // BLOCK
    col, row = lax.axis_index("col"), lax.axis_index("row")
    z, x, core = col >> 2, (col >> 1) & 1, col & 1

    def move(value, dz, fx, fc):
        perm = []
        for source in range(col_count):
            sz, sx, sc = source // 4, (source // 2) % 2, source % 2
            perm.append((source, ((sz + dz) % nz) * 4 + (sx ^ fx) * 2 + (sc ^ fc)))
        return lax.ppermute(value, "col", perm)

    def swap(value):
        return lax.ppermute(value, "row", [(0, 1), (1, 0)])

    def place(*firsts):
        return jnp.stack([z, x, core, *firsts]).astype(jnp.int32)

    pair = row_count == 2

    def once(value, other):
        return lax.optimization_barrier((value, other))[0]

    along_z = [inputs] + [move(inputs, k, 0, 0) for k in range(1, nz)]
    along_x = {0: move(inputs, 0, 1, 0)}

    def other_x(k, after):
        along_z[k] = once(along_z[k], after)
        along_x[k] = move(along_z[k], 0, 1, 0)

    def other_core(part):
        return move(jnp.concatenate(part, axis=0), 0, 0, 1)

    nsq = partial_norms(tenant, weight, down, up)
    if pair:
        nsq_a, nsq_b = nsq, swap(once(nsq, along_x[0]))
        firsts = [row * blocks_mine, (1 - row) * blocks_mine]
        cots = [cotangent, swap(cotangent)]
    else:
        nsq_a, nsq_b = lax.psum(nsq, "row"), jnp.zeros_like(nsq)
        firsts = [0 * row]
        cots = [lax.all_gather(cotangent, "row", axis=0, tiled=True)]
    places = [place(first) for first in firsts]

    def gradient(g, add, deps):
        return input_gradient(
            tenant, places[g], cots[g], nsq_a, nsq_b, magnitude, weight, down, up, add, deps
        )

    def cross_core(made, deps):
        return add_core(made[2], move(made[3], 0, 0, 1), deps)

    def cross_x(pairs, deps):
        mine, *away = add_x(place(*firsts), pairs, nz, deps)
        return [mine] + [move(block, k + 1, 0, 0) for k, block in enumerate(away)]

    def across_x(made):
        return made[0], move(made[1], 0, 1, 0)

    if pair:
        ours = gradient(0, [], [cots[1]])
        for k in [nz - 1] + list(range(1, nz - 1)):
            other_x(k, ours[0])
        core_z = other_core(along_z)
        theirs = gradient(1, [ours[2], move(ours[3], 0, 0, 1)], [core_z])
        near = across_x(theirs[4:])
        along_x = [along_x[k] for k in range(nz)]
        along_x[nz - 2] = once(along_x[nz - 2], theirs[0])
        core_x = other_core(along_x)
        far = cross_core(theirs, [core_x])
        pieces = [piece for both in zip(along_z, along_x) for piece in both] + [core_z, core_x]

        def project(g, out_dtype, deps):
            return forward(
                tenant, places[g], weight, cots[g], down, up, pieces, nz, out_dtype, deps
            )

        away, dots_away, low_away = project(1, BF16, [far[0]])
        arrived = swap(away)
        finals = cross_x([near, across_x(far)], [dots_away])
        part, dots_here, low_here = project(0, F32, [finals[0]])
        dots = jnp.concatenate([dots_here, dots_away], axis=0)
        low = jnp.concatenate([low_here, low_away], axis=1)
        late = (finals[nz // 2], finals[nz - 1])
        dots = dots + jnp.roll(swap(once(dots, late)), blocks_mine, axis=0)
        low = low + jnp.roll(swap(once(low, late)), rows_row, axis=1)
        parts = [ours, theirs]
    else:
        ours = gradient(0, [], [])
        near = across_x(cross_core(ours, []))
        for k in range(1, nz):
            other_x(k, inputs)
        along_x = [along_x[k] for k in range(nz)]
        pieces = [piece for both in zip(along_z, along_x) for piece in both]
        pieces += [other_core(along_z), other_core(along_x)]
        part, dots, low = forward(
            tenant, places[0], weight, cots[0], down, up, pieces, nz, F32, []
        )
        finals = cross_x([near], [])
        low, dots = lax.psum((low, dots), "row")
        parts = [ours]

    scales = jnp.concatenate([group[0] for group in parts], axis=0)

    tenants = jnp.arange(tenant_number, dtype=jnp.int32)
    block_tenant = tenant.reshape(nblk, BLOCK)[:, 0]
    size = nblk // len(parts)
    owners = jnp.concatenate(
        [lax.dynamic_slice_in_dim(block_tenant, first, size, 0) for first in firsts]
    )
    low = low.astype(BF16)
    grad_b = 0.0
    for g, group in enumerate(parts):
        owner = jnp.repeat(owners[g * size : (g + 1) * size], BLOCK)
        mine = low[:, g * size * BLOCK : (g + 1) * size * BLOCK]
        wide = jnp.where((tenants[:, None] == owner[None, :])[:, None, :], mine[None], 0)
        wide = wide.reshape(tenant_number * rank, size * BLOCK)
        grad_b = grad_b + jnp.dot(wide, group[1], preferred_element_type=F32)
    grad_b = grad_b.reshape(tenant_number, rank, cols)
    hit = (tenants[:, None] == owners[None, :])[:, :, None]
    terms = jnp.where(hit, (dots * scales)[None], 0.0)
    grad_m = 0.0
    for g in range(len(parts)):
        group = terms[:, g * size : (g + 1) * size]
        grad_m = grad_m + functools.reduce(jnp.add, [group[:, i] for i in range(size)])
    grad_inputs = add_z([once(finals[0], grad_b)] + finals[1:])
    if pair:
        pre = part + arrived.astype(F32)
        scale_mine = parts[0][0]
    else:
        pre = lax.psum_scatter(part, "row", scatter_dimension=0, tiled=True)
        scale_mine = lax.dynamic_slice_in_dim(scales, row * blocks_mine, blocks_mine, 0)
    output = (pre.reshape(blocks_mine, BLOCK, cols) * scale_mine[:, None, :]).astype(BF16)
    output = output.reshape(rows_row, cols)
    return (output, grad_inputs, grad_b, grad_m / magnitude)


def solution(mesh):
    return jax.shard_map(
        shards,
        mesh=mesh,
        in_specs=(
            P("col", "row"),
            P("row", "col"),
            P(None, None, "row"),
            P(None, None, "col"),
            P(None, "col"),
            P("row", "col"),
            P(),
        ),
        out_specs=(P("row", "col"), P("col", "row"), P(None, None, "col"), P(None, "col")),
        check_vma=False,
    )
```

```python
import functools

import jax
import jax.numpy as jnp
from jax import lax
from jax.experimental import pallas as pl
from jax.experimental.pallas import tpu as pltpu
from jax.sharding import PartitionSpec as P

BLOCK = 128
EPS = 1e-06
HIGH = lax.Precision.HIGHEST
STEPS = 8
PARTS = 16
AHEAD = 6
F32 = jnp.float32
BF16 = jnp.bfloat16
COST = pl.CostEstimate(flops=1000, bytes_accessed=1000, transcendentals=0)
LAST = (((1,), (1,)), ((), ()))
PARAMS = pltpu.CompilerParams(vmem_limit_bytes=52 * 1024 * 1024)
SMALL = pltpu.CompilerParams(vmem_limit_bytes=12 * 1024 * 1024)
IN_HBM = pl.BlockSpec(memory_space=pltpu.HBM)


def order_specs(deps):
    return [pl.BlockSpec(memory_space=pl.ANY)] * len(deps)


def same_block(array):
    return pl.BlockSpec(array.shape, lambda *args: (0,) * array.ndim)


def hi_lo(value, axis):
    hi = value.astype(BF16)
    lo = (value - hi.astype(F32)).astype(BF16)
    return jnp.concatenate([hi, lo], axis=axis)


def weight_copy(w_hbm, w_ref, sem, i):
    size = w_ref.shape[0] // PARTS
    rows = pl.ds(pl.multiple_of(i * size, size), size)
    return pltpu.make_async_copy(w_hbm.at[rows, :], w_ref.at[rows, :], sem.at[i])


def weight_block(w_hbm, w_ref, sem, i, steps):
    count = PARTS // steps
    for n in range(count):
        weight_copy(w_hbm, w_ref, sem, i * count + n).wait()
    for n in range(count):
        later = i * count + n + AHEAD

        @pl.when(later < PARTS)
        def _():
            weight_copy(w_hbm, w_ref, sem, later).start(priority=(n + AHEAD) % 2)


def factor_copies(tenant_ref, first, hbm, ref, sem, at):
    rank, nblk = hbm.shape[1], tenant_ref.shape[0] // BLOCK
    copies = []
    for b in range(ref.shape[0] // rank):
        src = hbm.at[tenant_ref[lax.rem(first + b, nblk) * BLOCK]]
        dst = ref.at[pl.ds(b * rank, rank), :]
        copies.append(pltpu.make_async_copy(src, dst, sem.at[at + b]))
    return copies


def norm_body(nblk, rank, tenant_ref, w_hbm, a_hbm, up_hbm, nsq_ref, *refs):
    w_ref, a_ref, up_ref, cross_ref, square_ref, w_sem, sem = refs
    cols = w_ref.shape[1]
    db = w_ref.shape[0] // STEPS
    copies = factor_copies(tenant_ref, 0, a_hbm, a_ref, sem, 0)
    late = factor_copies(tenant_ref, 0, up_hbm, up_ref, sem, nblk)
    for copy in copies:
        copy.start()
    for i in range(AHEAD):
        weight_copy(w_hbm, w_ref, w_sem, i).start(priority=i % 2)
    for copy in late:
        copy.start()
    cross_ref[...] = jnp.zeros_like(cross_ref)
    square_ref[...] = jnp.zeros_like(square_ref)
    for copy in copies:
        copy.wait()
    step = min(db, 256)

    def block(i, carry):
        weight_block(w_hbm, w_ref, w_sem, i, STEPS)
        squares = square_ref[...]
        for start in range(0, db, step):
            rows = pl.ds(pl.multiple_of(i * db + start, step), step)
            w = w_ref[rows, :]
            cross_ref[...] += jnp.dot(a_ref[:, rows], w, preferred_element_type=F32)
            for at in range(0, step, 16):
                wf = w[at : at + 16, :].astype(F32)
                squares = squares + wf[:8] * wf[:8] + wf[8:] * wf[8:]
        square_ref[...] = squares
        return carry

    lax.fori_loop(0, STEPS, block, 0)
    for copy in late:
        copy.wait()
    gram = lax.dot_general(a_ref[...], a_ref[...], LAST, preferred_element_type=F32)
    row = lax.broadcasted_iota(jnp.int32, gram.shape, 0) // rank
    col = lax.broadcasted_iota(jnp.int32, gram.shape, 1) // rank
    gram = jnp.where(row == col, gram, 0.0)
    up = up_ref[...].astype(F32)
    quad = jnp.dot(gram, up, preferred_element_type=F32, precision=HIGH)
    mixed = (up * (2.0 * cross_ref[...] + quad)).reshape(nblk, rank, cols)
    nsq_ref[...] = jnp.sum(mixed, axis=1) + jnp.sum(square_ref[...], axis=0, keepdims=True)


def partial_norms(tenant, weight, down, up):
    depth, cols = weight.shape
    rank = down.shape[1]
    nblk = tenant.shape[0] // BLOCK
    shape = jax.ShapeDtypeStruct((nblk, cols), F32)
    return pl.pallas_call(
        functools.partial(norm_body, nblk, rank),
        out_shape=shape,
        grid_spec=pltpu.PrefetchScalarGridSpec(
            num_scalar_prefetch=1,
            grid=(1,),
            in_specs=[IN_HBM] * 3,
            out_specs=same_block(shape),
            scratch_shapes=[
                pltpu.VMEM((depth, cols), BF16),
                pltpu.VMEM((nblk * rank, depth), BF16),
                pltpu.VMEM((nblk * rank, cols), BF16),
                pltpu.VMEM((nblk * rank, cols), F32),
                pltpu.VMEM((8, cols), F32),
                pltpu.SemaphoreType.DMA((PARTS,)),
                pltpu.SemaphoreType.DMA((2 * nblk,)),
            ],
        ),
        compiler_params=PARAMS,
        cost_estimate=COST,
        name="partial_norms",
    )(tenant, weight, down, up)


def grad_body(nb, rank, adds, tenant_ref, place_ref, cot_ref, nsq_a, nsq_b, mag_ref, *refs):
    w_hbm, a_hbm, up_hbm = refs[:3]
    if adds:
        add_core_body(*refs[3:5], *refs[-9:-7])
        refs = refs[:-9] + refs[-7:]
    scale_ref, sg_ref, keep_ref, send_ref = refs[-11:-7]
    w_ref, a_ref, up_ref, sgp_ref, backp_ref, w_sem, sem = refs[-7:]
    rows, db = sg_ref.shape[0], keep_ref.shape[1]
    piece = BLOCK // 4
    half = rows // 2
    step = pl.program_id(0)
    x, core, first = place_ref[1], place_ref[2], place_ref[3]

    @pl.when(step == 0)
    def _():
        copies = factor_copies(tenant_ref, first, up_hbm, up_ref, sem, 0)
        copies += factor_copies(tenant_ref, first, a_hbm, a_ref, sem, nb)
        for copy in copies:
            copy.start()
        for i in range(AHEAD):
            weight_copy(w_hbm, w_ref, w_sem, i).start(priority=i % 2)
        for b in range(nb):
            at = first + b
            total = nsq_a[pl.ds(at, 1), :] + nsq_b[pl.ds(at, 1), :]
            scale = mag_ref[pl.ds(tenant_ref[at * BLOCK], 1), :] / jnp.sqrt(total + EPS)
            scale_ref[b : b + 1, :] = scale
            here = slice(b * BLOCK, (b + 1) * BLOCK)
            sg_ref[here, :] = (cot_ref[here, :].astype(F32) * scale).astype(BF16)
        for fc in range(2):
            for fx in range(2):
                for b in range(nb):
                    c = b * 4 + (x ^ fx) * 2 + (core ^ fc)
                    src = pl.ds(pl.multiple_of(c * piece, piece), piece)
                    at = ((fc * 2 + fx) * nb + b) * piece
                    sgp_ref[at : at + piece, :] = sg_ref[src, :]
        for copy in copies:
            copy.wait()
        back = lax.dot_general(sgp_ref[...], up_ref[...], LAST, preferred_element_type=F32)
        block = lax.broadcasted_iota(jnp.int32, back.shape, 0) // piece % nb
        owner = lax.broadcasted_iota(jnp.int32, back.shape, 1) // rank
        backp_ref[...] = hi_lo(jnp.where(owner == block, back, 0.0), 1)

    weight_block(w_hbm, w_ref, w_sem, step, w_ref.shape[0] // db)
    at = pl.ds(pl.multiple_of(step * db, db), db)
    down = a_ref[:, at]
    down = jnp.concatenate([down, down], axis=0)
    part = lax.dot_general(w_ref[at, :], sgp_ref[...], LAST, preferred_element_type=F32).T
    part = part + jnp.dot(backp_ref[...], down, preferred_element_type=F32)
    keep_ref[...] = part[:half, :]
    send_ref[...] = part[half:, :].astype(BF16)


def input_gradient(tenant, place, cot, nsq_a, nsq_b, magnitude, weight, down, up, add, deps):
    depth, cols = weight.shape
    rows = cot.shape[0]
    nb = rows // BLOCK
    rank = down.shape[1]
    steps = STEPS // 2
    db = depth // steps
    shapes = (
        jax.ShapeDtypeStruct((nb, cols), F32),
        jax.ShapeDtypeStruct((rows, cols), BF16),
        jax.ShapeDtypeStruct((rows // 2, depth), F32),
        jax.ShapeDtypeStruct((rows // 2, depth), BF16),
    )
    if add:
        shapes += tuple(jax.ShapeDtypeStruct((rows // 4, depth), t) for t in (F32, BF16))

    def columns(array):
        return pl.BlockSpec((array.shape[0], db), lambda i, t, p: (0, i))

    return pl.pallas_call(
        functools.partial(grad_body, nb, rank, len(add)),
        out_shape=shapes,
        grid_spec=pltpu.PrefetchScalarGridSpec(
            num_scalar_prefetch=2,
            grid=(steps,),
            in_specs=[same_block(a) for a in (cot, nsq_a, nsq_b, magnitude)]
            + [IN_HBM] * 3
            + [columns(a) for a in add]
            + order_specs(deps),
            out_specs=[same_block(s) for s in shapes[:2]] + [columns(s) for s in shapes[2:]],
            scratch_shapes=[
                pltpu.VMEM((depth, cols), BF16),
                pltpu.VMEM((nb * rank, depth), BF16),
                pltpu.VMEM((nb * rank, cols), BF16),
                pltpu.VMEM((rows, cols), BF16),
                pltpu.VMEM((rows, 2 * nb * rank), BF16),
                pltpu.SemaphoreType.DMA((PARTS,)),
                pltpu.SemaphoreType.DMA((2 * nb,)),
            ],
        ),
        compiler_params=PARAMS,
        cost_estimate=COST,
        name="input_gradient",
    )(tenant, place, cot, nsq_a, nsq_b, magnitude, weight, down, up, *add, *deps)


def add_core_body(keep_ref, recv_ref, *refs):
    mine_ref, send_ref = refs[-2:]
    half = mine_ref.shape[0]
    mine_ref[...] = keep_ref[:half, :] + recv_ref[:half, :].astype(F32)
    send_ref[...] = (keep_ref[half:, :] + recv_ref[half:, :].astype(F32)).astype(BF16)


def add_core(keep, recv, deps):
    rows, size = keep.shape
    block = size // 2
    return pl.pallas_call(
        add_core_body,
        out_shape=(
            jax.ShapeDtypeStruct((rows // 2, size), F32),
            jax.ShapeDtypeStruct((rows // 2, size), BF16),
        ),
        grid=(2,),
        in_specs=[pl.BlockSpec((rows, block), lambda i: (0, i))] * 2 + order_specs(deps),
        out_specs=[pl.BlockSpec((rows // 2, block), lambda i: (0, i))] * 2,
        compiler_params=SMALL,
        cost_estimate=COST,
        name="add_core",
    )(keep, recv, *deps)


def add_x_body(groups, nz, place_ref, *refs):
    outs, total_ref = refs[-nz - 1 : -1], refs[-1]
    piece = outs[0].shape[0]
    z = place_ref[0]
    for g in range(groups):
        keep_ref, recv_ref = refs[2 * g : 2 * g + 2]
        first = pl.multiple_of(place_ref[3 + g] * piece, piece)
        total = keep_ref[...] + recv_ref[...].astype(F32)
        total_ref[pl.ds(first, keep_ref.shape[0]), :] = total
    for k in range(nz):
        at = pl.multiple_of(lax.rem(z + k, nz) * piece, piece)
        outs[k][...] = total_ref[pl.ds(at, piece), :].astype(outs[k].dtype)


def add_x(place, pairs, nz, deps):
    piece = BLOCK // 4
    size = pairs[0][0].shape[1]
    block = size // 2
    operands = [array for pair in pairs for array in pair]

    def spec(array):
        return pl.BlockSpec((array.shape[0], block), lambda i, p: (0, i))

    shapes = tuple(jax.ShapeDtypeStruct((piece, size), BF16 if k else F32) for k in range(nz))
    return pl.pallas_call(
        functools.partial(add_x_body, len(pairs), nz),
        out_shape=shapes,
        grid_spec=pltpu.PrefetchScalarGridSpec(
            num_scalar_prefetch=1,
            grid=(2,),
            in_specs=[spec(a) for a in operands] + order_specs(deps),
            out_specs=[spec(s) for s in shapes],
            scratch_shapes=[pltpu.VMEM((nz * piece, block), F32)],
        ),
        compiler_params=SMALL,
        cost_estimate=COST,
        name="add_x",
    )(place, *operands, *deps)


def add_z_body(*refs):
    total = refs[0][...]
    for ref in refs[1:-1]:
        total = total + ref[...].astype(F32)
    refs[-1][...] = total.astype(BF16)


def add_z(parts):
    return pl.pallas_call(
        add_z_body,
        out_shape=jax.ShapeDtypeStruct(parts[0].shape, BF16),
        in_specs=[pl.BlockSpec(memory_space=pltpu.VMEM)] * len(parts),
        compiler_params=SMALL,
        cost_estimate=COST,
        name="add_z",
    )(*parts)


def forward_body(nb, rank, nz, tenant_ref, place_ref, cot_ref, w_hbm, a_hbm, up_hbm, *refs):
    pieces = refs[: 2 * nz + 2]
    part_ref, dot_ref, low_ref = refs[-12:-9]
    w_ref, a_ref, up_ref, x_ref, acc_ref, low_acc, w_sem, sem, x_sem = refs[-9:]
    rows, cols = acc_ref.shape
    piece = BLOCK // 4
    depth = w_ref.shape[0]
    steps = STEPS
    db = depth // steps
    z, x, core, first = place_ref[0], place_ref[1], place_ref[2], place_ref[3]

    def each(h, act):
        at = pl.ds(h * depth // 2, depth // 2)
        for n in range(4 * nz):
            k, fx, fc = n // 4, (n // 2) % 2, n % 2
            src = pieces[2 * nz + fx] if fc else pieces[2 * k + fx]
            src = src.at[pl.ds(k * piece if fc else 0, piece), at]
            b = lax.rem(z + (nz - k), nz) - first

            @pl.when(jnp.logical_and(b >= 0, b < nb))
            def _():
                row = (b * 4 + (x ^ fx) * 2 + (core ^ fc)) * piece
                dst = pl.ds(pl.multiple_of(row, piece), piece)
                act(pltpu.make_async_copy(src, x_ref.at[dst, at], x_sem.at[h, n]), n % 2)

    copies = factor_copies(tenant_ref, first, a_hbm, a_ref, sem, 0)
    late = factor_copies(tenant_ref, first, up_hbm, up_ref, sem, nb)
    each(0, lambda copy, queue: copy.start(priority=queue))
    for copy in copies:
        copy.start()
    for i in range(AHEAD):
        weight_copy(w_hbm, w_ref, w_sem, i).start(priority=i % 2)
    each(1, lambda copy, queue: copy.start(priority=queue))
    for copy in late:
        copy.start()
    acc_ref[...] = jnp.zeros_like(acc_ref)
    low_acc[...] = jnp.zeros_like(low_acc)
    for copy in copies:
        copy.wait()

    def block(i, carry):
        for h in range(2):

            @pl.when(i == h * (steps // 2))
            def _():
                each(h, lambda copy, queue: copy.wait())

        weight_block(w_hbm, w_ref, w_sem, i, steps)
        at = pl.ds(pl.multiple_of(i * db, db), db)
        xs = x_ref[:, at]
        acc_ref[...] += jnp.dot(xs, w_ref[at, :], preferred_element_type=F32)
        low_acc[...] += lax.dot_general(a_ref[:, at], xs, LAST, preferred_element_type=F32)
        return carry

    lax.fori_loop(0, steps, block, 0)
    low = low_acc[...]
    owner = lax.broadcasted_iota(jnp.int32, low.shape, 0) // rank
    block_of = lax.broadcasted_iota(jnp.int32, low.shape, 1) // BLOCK
    low = jnp.where(owner == block_of, low, 0.0)
    low_ref[...] = jnp.sum(low.reshape(nb, rank, rows), axis=0)
    hi = low.astype(BF16).astype(F32)
    lowcat = jnp.concatenate([hi, low - hi], axis=0).T.astype(BF16)
    for copy in late:
        copy.wait()
    up = up_ref[...]
    up = jnp.concatenate([up, up], axis=0)
    for i in range(nb):
        here = slice(i * BLOCK, (i + 1) * BLOCK)
        part = acc_ref[here, :] + jnp.dot(lowcat[here, :], up, preferred_element_type=F32)
        part_ref[here, :] = part.astype(part_ref.dtype)
        product = part * cot_ref[here, :].astype(F32)
        dot_ref[i : i + 1, :] = jnp.sum(product, axis=0, keepdims=True)


def forward(tenant, place, weight, cot, down, up, pieces, nz, out_dtype, deps):
    depth, cols = weight.shape
    rows = cot.shape[0]
    nb = rows // BLOCK
    rank = down.shape[1]
    shapes = (
        jax.ShapeDtypeStruct((rows, cols), out_dtype),
        jax.ShapeDtypeStruct((nb, cols), F32),
        jax.ShapeDtypeStruct((rank, rows), F32),
    )
    return pl.pallas_call(
        functools.partial(forward_body, nb, rank, nz),
        out_shape=shapes,
        grid_spec=pltpu.PrefetchScalarGridSpec(
            num_scalar_prefetch=2,
            grid=(1,),
            in_specs=[same_block(cot)] + [IN_HBM] * (3 + len(pieces)) + order_specs(deps),
            out_specs=[same_block(s) for s in shapes],
            scratch_shapes=[
                pltpu.VMEM((depth, cols), BF16),
                pltpu.VMEM((nb * rank, depth), BF16),
                pltpu.VMEM((nb * rank, cols), BF16),
                pltpu.VMEM((rows, depth), BF16),
                pltpu.VMEM((rows, cols), F32),
                pltpu.VMEM((nb * rank, rows), F32),
                pltpu.SemaphoreType.DMA((PARTS,)),
                pltpu.SemaphoreType.DMA((2 * nb,)),
                pltpu.SemaphoreType.DMA((2, 4 * nz)),
            ],
        ),
        compiler_params=PARAMS,
        cost_estimate=COST,
        name="forward",
    )(tenant, place, cot, weight, down, up, *pieces, *deps)


def shards(inputs, weight, adapter_down_factors, adapter_up_factors, magnitude, cotangent, tenant):
    col_count, row_count = lax.axis_size("col"), lax.axis_size("row")
    nz = col_count // 4
    down, up = adapter_down_factors, adapter_up_factors
    tenant_number, rank, depth = down.shape
    cols = weight.shape[1]
    tokens = tenant.shape[0]
    nblk = tokens // BLOCK
    rows_row = tokens // row_count
    blocks_mine = rows_row // BLOCK
    col, row = lax.axis_index("col"), lax.axis_index("row")
    z, x, core = col >> 2, (col >> 1) & 1, col & 1

    def move(value, dz, fx, fc):
        perm = []
        for source in range(col_count):
            sz, sx, sc = source // 4, (source // 2) % 2, source % 2
            perm.append((source, ((sz + dz) % nz) * 4 + (sx ^ fx) * 2 + (sc ^ fc)))
        return lax.ppermute(value, "col", perm)

    def swap(value):
        return lax.ppermute(value, "row", [(0, 1), (1, 0)])

    def place(*firsts):
        return jnp.stack([z, x, core, *firsts]).astype(jnp.int32)

    pair = row_count == 2

    def once(value, other):
        return lax.optimization_barrier((value, other))[0]

    along_z = [inputs] + [move(inputs, k, 0, 0) for k in range(1, nz)]
    along_x = {0: move(inputs, 0, 1, 0)}

    def other_x(k, after):
        along_z[k] = once(along_z[k], after)
        along_x[k] = move(along_z[k], 0, 1, 0)

    def other_core(part):
        return move(jnp.concatenate(part, axis=0), 0, 0, 1)

    nsq = partial_norms(tenant, weight, down, up)
    if pair:
        nsq_a, nsq_b = nsq, swap(once(nsq, along_x[0]))
        firsts = [row * blocks_mine, (1 - row) * blocks_mine]
        cots = [cotangent, swap(cotangent)]
    else:
        nsq_a, nsq_b = lax.psum(nsq, "row"), jnp.zeros_like(nsq)
        firsts = [0 * row]
        cots = [lax.all_gather(cotangent, "row", axis=0, tiled=True)]
    places = [place(first) for first in firsts]

    def gradient(g, add, deps):
        return input_gradient(
            tenant, places[g], cots[g], nsq_a, nsq_b, magnitude, weight, down, up, add, deps
        )

    def cross_core(made, deps):
        return add_core(made[2], move(made[3], 0, 0, 1), deps)

    def cross_x(pairs, deps):
        mine, *away = add_x(place(*firsts), pairs, nz, deps)
        return [mine] + [move(block, k + 1, 0, 0) for k, block in enumerate(away)]

    def across_x(made):
        return made[0], move(made[1], 0, 1, 0)

    if pair:
        ours = gradient(0, [], [cots[1]])
        for k in [nz - 1] + list(range(1, nz - 1)):
            other_x(k, ours[0])
        core_z = other_core(along_z)
        theirs = gradient(1, [ours[2], move(ours[3], 0, 0, 1)], [core_z])
        near = across_x(theirs[4:])
        along_x = [along_x[k] for k in range(nz)]
        along_x[nz - 2] = once(along_x[nz - 2], theirs[0])
        core_x = other_core(along_x)
        far = cross_core(theirs, [core_x])
        pieces = [piece for both in zip(along_z, along_x) for piece in both] + [core_z, core_x]

        def project(g, out_dtype, deps):
            return forward(
                tenant, places[g], weight, cots[g], down, up, pieces, nz, out_dtype, deps
            )

        away, dots_away, low_away = project(1, BF16, [far[0]])
        arrived = swap(away)
        finals = cross_x([near, across_x(far)], [dots_away])
        part, dots_here, low_here = project(0, F32, [finals[0]])
        dots = jnp.concatenate([dots_here, dots_away], axis=0)
        low = jnp.concatenate([low_here, low_away], axis=1)
        late = (finals[nz // 2], finals[nz - 1])
        dots = dots + jnp.roll(swap(once(dots, late)), blocks_mine, axis=0)
        low = low + jnp.roll(swap(once(low, late)), rows_row, axis=1)
        parts = [ours, theirs]
    else:
        ours = gradient(0, [], [])
        near = across_x(cross_core(ours, []))
        for k in range(1, nz):
            other_x(k, inputs)
        along_x = [along_x[k] for k in range(nz)]
        pieces = [piece for both in zip(along_z, along_x) for piece in both]
        pieces += [other_core(along_z), other_core(along_x)]
        part, dots, low = forward(
            tenant, places[0], weight, cots[0], down, up, pieces, nz, F32, []
        )
        finals = cross_x([near], [])
        low, dots = lax.psum((low, dots), "row")
        parts = [ours]

    scales = jnp.concatenate([group[0] for group in parts], axis=0)

    tenants = jnp.arange(tenant_number, dtype=jnp.int32)
    block_tenant = tenant.reshape(nblk, BLOCK)[:, 0]
    size = nblk // len(parts)
    owners = jnp.concatenate(
        [lax.dynamic_slice_in_dim(block_tenant, first, size, 0) for first in firsts]
    )
    low = low.astype(BF16)
    grad_b = 0.0
    for g, group in enumerate(parts):
        owner = jnp.repeat(owners[g * size : (g + 1) * size], BLOCK)
        mine = low[:, g * size * BLOCK : (g + 1) * size * BLOCK]
        wide = jnp.where((tenants[:, None] == owner[None, :])[:, None, :], mine[None], 0)
        wide = wide.reshape(tenant_number * rank, size * BLOCK)
        grad_b = grad_b + jnp.dot(wide, group[1], preferred_element_type=F32)
    grad_b = grad_b.reshape(tenant_number, rank, cols)
    hit = (tenants[:, None] == owners[None, :])[:, :, None]
    terms = jnp.where(hit, (dots * scales)[None], 0.0)
    grad_m = 0.0
    for g in range(len(parts)):
        group = terms[:, g * size : (g + 1) * size]
        grad_m = grad_m + functools.reduce(jnp.add, [group[:, i] for i in range(size)])
    grad_inputs = add_z([once(finals[0], grad_b)] + finals[1:])
    if pair:
        pre = part + arrived.astype(F32)
        scale_mine = parts[0][0]
    else:
        pre = lax.psum_scatter(part, "row", scatter_dimension=0, tiled=True)
        scale_mine = lax.dynamic_slice_in_dim(scales, row * blocks_mine, blocks_mine, 0)
    output = (pre.reshape(blocks_mine, BLOCK, cols) * scale_mine[:, None, :]).astype(BF16)
    output = output.reshape(rows_row, cols)
    return (output, grad_inputs, grad_b, grad_m / magnitude)


def solution(mesh):
    return jax.shard_map(
        shards,
        mesh=mesh,
        in_specs=(
            P("col", "row"),
            P("row", "col"),
            P(None, None, "row"),
            P(None, None, "col"),
            P(None, "col"),
            P("row", "col"),
            P(),
        ),
        out_specs=(P("row", "col"), P("col", "row"), P(None, None, "col"), P(None, "col")),
        check_vma=False,
    )
```

```python
import functools

import jax
import jax.numpy as jnp
from jax import lax
from jax.experimental import pallas as pl
from jax.experimental.pallas import tpu as pltpu
from jax.sharding import PartitionSpec as P

BLOCK = 128
EPS = 1e-06
HIGH = lax.Precision.HIGHEST
STEPS = 8
PARTS = 16
AHEAD = 6
F32 = jnp.float32
BF16 = jnp.bfloat16
COST = pl.CostEstimate(flops=1000, bytes_accessed=1000, transcendentals=0)
LAST = (((1,), (1,)), ((), ()))
PARAMS = pltpu.CompilerParams(vmem_limit_bytes=52 * 1024 * 1024)
SMALL = pltpu.CompilerParams(vmem_limit_bytes=12 * 1024 * 1024)
IN_HBM = pl.BlockSpec(memory_space=pltpu.HBM)


def order_specs(deps):
    return [pl.BlockSpec(memory_space=pl.ANY)] * len(deps)


def same_block(array):
    return pl.BlockSpec(array.shape, lambda *args: (0,) * array.ndim)


def hi_lo(value, axis):
    hi = value.astype(BF16)
    lo = (value - hi.astype(F32)).astype(BF16)
    return jnp.concatenate([hi, lo], axis=axis)


def weight_copy(w_hbm, w_ref, sem, i):
    size = w_ref.shape[0] // PARTS
    rows = pl.ds(pl.multiple_of(i * size, size), size)
    return pltpu.make_async_copy(w_hbm.at[rows, :], w_ref.at[rows, :], sem.at[i])


def weight_block(w_hbm, w_ref, sem, i, steps):
    count = PARTS // steps
    for n in range(count):
        weight_copy(w_hbm, w_ref, sem, i * count + n).wait()
    for n in range(count):
        later = i * count + n + AHEAD

        @pl.when(later < PARTS)
        def _():
            weight_copy(w_hbm, w_ref, sem, later).start(priority=(n + AHEAD) % 2)


def factor_copies(tenant_ref, first, hbm, ref, sem, at):
    rank, nblk = hbm.shape[1], tenant_ref.shape[0] // BLOCK
    copies = []
    for b in range(ref.shape[0] // rank):
        src = hbm.at[tenant_ref[lax.rem(first + b, nblk) * BLOCK]]
        dst = ref.at[pl.ds(b * rank, rank), :]
        copies.append(pltpu.make_async_copy(src, dst, sem.at[at + b]))
    return copies


def norm_body(nblk, rank, tenant_ref, w_hbm, a_hbm, up_hbm, nsq_ref, *refs):
    w_ref, a_ref, up_ref, cross_ref, square_ref, w_sem, sem = refs
    cols = w_ref.shape[1]
    db = w_ref.shape[0] // STEPS
    copies = factor_copies(tenant_ref, 0, a_hbm, a_ref, sem, 0)
    late = factor_copies(tenant_ref, 0, up_hbm, up_ref, sem, nblk)
    for copy in copies:
        copy.start()
    for i in range(AHEAD):
        weight_copy(w_hbm, w_ref, w_sem, i).start(priority=i % 2)
    for copy in late:
        copy.start()
    cross_ref[...] = jnp.zeros_like(cross_ref)
    square_ref[...] = jnp.zeros_like(square_ref)
    for copy in copies:
        copy.wait()
    step = min(db, 256)

    def block(i, carry):
        weight_block(w_hbm, w_ref, w_sem, i, STEPS)
        squares = square_ref[...]
        for start in range(0, db, step):
            rows = pl.ds(pl.multiple_of(i * db + start, step), step)
            w = w_ref[rows, :]
            cross_ref[...] += jnp.dot(a_ref[:, rows], w, preferred_element_type=F32)
            for at in range(0, step, 16):
                wf = w[at : at + 16, :].astype(F32)
                squares = squares + wf[:8] * wf[:8] + wf[8:] * wf[8:]
        square_ref[...] = squares
        return carry

    lax.fori_loop(0, STEPS, block, 0)
    for copy in late:
        copy.wait()
    gram = lax.dot_general(a_ref[...], a_ref[...], LAST, preferred_element_type=F32)
    row = lax.broadcasted_iota(jnp.int32, gram.shape, 0) // rank
    col = lax.broadcasted_iota(jnp.int32, gram.shape, 1) // rank
    gram = jnp.where(row == col, gram, 0.0)
    up = up_ref[...].astype(F32)
    quad = jnp.dot(gram, up, preferred_element_type=F32, precision=HIGH)
    mixed = (up * (2.0 * cross_ref[...] + quad)).reshape(nblk, rank, cols)
    nsq_ref[...] = jnp.sum(mixed, axis=1) + jnp.sum(square_ref[...], axis=0, keepdims=True)


def partial_norms(tenant, weight, down, up):
    depth, cols = weight.shape
    rank = down.shape[1]
    nblk = tenant.shape[0] // BLOCK
    shape = jax.ShapeDtypeStruct((nblk, cols), F32)
    return pl.pallas_call(
        functools.partial(norm_body, nblk, rank),
        out_shape=shape,
        grid_spec=pltpu.PrefetchScalarGridSpec(
            num_scalar_prefetch=1,
            grid=(1,),
            in_specs=[IN_HBM] * 3,
            out_specs=same_block(shape),
            scratch_shapes=[
                pltpu.VMEM((depth, cols), BF16),
                pltpu.VMEM((nblk * rank, depth), BF16),
                pltpu.VMEM((nblk * rank, cols), BF16),
                pltpu.VMEM((nblk * rank, cols), F32),
                pltpu.VMEM((8, cols), F32),
                pltpu.SemaphoreType.DMA((PARTS,)),
                pltpu.SemaphoreType.DMA((2 * nblk,)),
            ],
        ),
        compiler_params=PARAMS,
        cost_estimate=COST,
        name="partial_norms",
    )(tenant, weight, down, up)


def grad_body(nb, rank, adds, tenant_ref, place_ref, cot_ref, nsq_a, nsq_b, mag_ref, *refs):
    w_hbm, a_hbm, up_hbm = refs[:3]
    if adds:
        add_core_body(*refs[3:5], *refs[-9:-7])
        refs = refs[:-9] + refs[-7:]
    scale_ref, sg_ref, keep_ref, send_ref = refs[-11:-7]
    w_ref, a_ref, up_ref, sgp_ref, backp_ref, w_sem, sem = refs[-7:]
    rows, db = sg_ref.shape[0], keep_ref.shape[1]
    piece = BLOCK // 4
    half = rows // 2
    step = pl.program_id(0)
    x, core, first = place_ref[1], place_ref[2], place_ref[3]

    @pl.when(step == 0)
    def _():
        copies = factor_copies(tenant_ref, first, up_hbm, up_ref, sem, 0)
        copies += factor_copies(tenant_ref, first, a_hbm, a_ref, sem, nb)
        for copy in copies:
            copy.start()
        for i in range(AHEAD):
            weight_copy(w_hbm, w_ref, w_sem, i).start(priority=i % 2)
        for b in range(nb):
            at = first + b
            total = nsq_a[pl.ds(at, 1), :] + nsq_b[pl.ds(at, 1), :]
            scale = mag_ref[pl.ds(tenant_ref[at * BLOCK], 1), :] / jnp.sqrt(total + EPS)
            scale_ref[b : b + 1, :] = scale
            here = slice(b * BLOCK, (b + 1) * BLOCK)
            sg_ref[here, :] = (cot_ref[here, :].astype(F32) * scale).astype(BF16)
        for fc in range(2):
            for fx in range(2):
                for b in range(nb):
                    c = b * 4 + (x ^ fx) * 2 + (core ^ fc)
                    src = pl.ds(pl.multiple_of(c * piece, piece), piece)
                    at = ((fc * 2 + fx) * nb + b) * piece
                    sgp_ref[at : at + piece, :] = sg_ref[src, :]
        for copy in copies:
            copy.wait()
        back = lax.dot_general(sgp_ref[...], up_ref[...], LAST, preferred_element_type=F32)
        block = lax.broadcasted_iota(jnp.int32, back.shape, 0) // piece % nb
        owner = lax.broadcasted_iota(jnp.int32, back.shape, 1) // rank
        backp_ref[...] = hi_lo(jnp.where(owner == block, back, 0.0), 1)

    weight_block(w_hbm, w_ref, w_sem, step, STEPS)
    at = pl.ds(pl.multiple_of(step * db, db), db)
    down = a_ref[:, at]
    down = jnp.concatenate([down, down], axis=0)
    part = lax.dot_general(sgp_ref[...], w_ref[at, :], LAST, preferred_element_type=F32)
    part = part + jnp.dot(backp_ref[...], down, preferred_element_type=F32)
    keep_ref[...] = part[:half, :]
    send_ref[...] = part[half:, :].astype(BF16)


def input_gradient(tenant, place, cot, nsq_a, nsq_b, magnitude, weight, down, up, add, deps):
    depth, cols = weight.shape
    rows = cot.shape[0]
    nb = rows // BLOCK
    rank = down.shape[1]
    db = depth // STEPS
    shapes = (
        jax.ShapeDtypeStruct((nb, cols), F32),
        jax.ShapeDtypeStruct((rows, cols), BF16),
        jax.ShapeDtypeStruct((rows // 2, depth), F32),
        jax.ShapeDtypeStruct((rows // 2, depth), BF16),
    )
    if add:
        shapes += tuple(jax.ShapeDtypeStruct((rows // 4, depth), t) for t in (F32, BF16))

    def columns(array):
        return pl.BlockSpec((array.shape[0], db), lambda i, t, p: (0, i))

    return pl.pallas_call(
        functools.partial(grad_body, nb, rank, len(add)),
        out_shape=shapes,
        grid_spec=pltpu.PrefetchScalarGridSpec(
            num_scalar_prefetch=2,
            grid=(STEPS,),
            in_specs=[same_block(a) for a in (cot, nsq_a, nsq_b, magnitude)]
            + [IN_HBM] * 3
            + [columns(a) for a in add]
            + order_specs(deps),
            out_specs=[same_block(s) for s in shapes[:2]] + [columns(s) for s in shapes[2:]],
            scratch_shapes=[
                pltpu.VMEM((depth, cols), BF16),
                pltpu.VMEM((nb * rank, depth), BF16),
                pltpu.VMEM((nb * rank, cols), BF16),
                pltpu.VMEM((rows, cols), BF16),
                pltpu.VMEM((rows, 2 * nb * rank), BF16),
                pltpu.SemaphoreType.DMA((PARTS,)),
                pltpu.SemaphoreType.DMA((2 * nb,)),
            ],
        ),
        compiler_params=PARAMS,
        cost_estimate=COST,
        name="input_gradient",
    )(tenant, place, cot, nsq_a, nsq_b, magnitude, weight, down, up, *add, *deps)


def add_core_body(keep_ref, recv_ref, *refs):
    mine_ref, send_ref = refs[-2:]
    half = mine_ref.shape[0]
    mine_ref[...] = keep_ref[:half, :] + recv_ref[:half, :].astype(F32)
    send_ref[...] = (keep_ref[half:, :] + recv_ref[half:, :].astype(F32)).astype(BF16)


def add_core(keep, recv, deps):
    rows, size = keep.shape
    block = size // 2
    return pl.pallas_call(
        add_core_body,
        out_shape=(
            jax.ShapeDtypeStruct((rows // 2, size), F32),
            jax.ShapeDtypeStruct((rows // 2, size), BF16),
        ),
        grid=(2,),
        in_specs=[pl.BlockSpec((rows, block), lambda i: (0, i))] * 2 + order_specs(deps),
        out_specs=[pl.BlockSpec((rows // 2, block), lambda i: (0, i))] * 2,
        compiler_params=SMALL,
        cost_estimate=COST,
        name="add_core",
    )(keep, recv, *deps)


def add_x_body(groups, nz, place_ref, *refs):
    outs, total_ref = refs[-nz - 1 : -1], refs[-1]
    piece = outs[0].shape[0]
    z = place_ref[0]
    for g in range(groups):
        keep_ref, recv_ref = refs[2 * g : 2 * g + 2]
        first = pl.multiple_of(place_ref[3 + g] * piece, piece)
        total = keep_ref[...] + recv_ref[...].astype(F32)
        total_ref[pl.ds(first, keep_ref.shape[0]), :] = total
    for k in range(nz):
        at = pl.multiple_of(lax.rem(z + k, nz) * piece, piece)
        outs[k][...] = total_ref[pl.ds(at, piece), :].astype(outs[k].dtype)


def add_x(place, pairs, nz, deps):
    piece = BLOCK // 4
    size = pairs[0][0].shape[1]
    block = size // 2
    operands = [array for pair in pairs for array in pair]

    def spec(array):
        return pl.BlockSpec((array.shape[0], block), lambda i, p: (0, i))

    shapes = tuple(jax.ShapeDtypeStruct((piece, size), BF16 if k else F32) for k in range(nz))
    return pl.pallas_call(
        functools.partial(add_x_body, len(pairs), nz),
        out_shape=shapes,
        grid_spec=pltpu.PrefetchScalarGridSpec(
            num_scalar_prefetch=1,
            grid=(2,),
            in_specs=[spec(a) for a in operands] + order_specs(deps),
            out_specs=[spec(s) for s in shapes],
            scratch_shapes=[pltpu.VMEM((nz * piece, block), F32)],
        ),
        compiler_params=SMALL,
        cost_estimate=COST,
        name="add_x",
    )(place, *operands, *deps)


def add_z_body(*refs):
    total = refs[0][...]
    for ref in refs[1:-1]:
        total = total + ref[...].astype(F32)
    refs[-1][...] = total.astype(BF16)


def add_z(parts):
    return pl.pallas_call(
        add_z_body,
        out_shape=jax.ShapeDtypeStruct(parts[0].shape, BF16),
        in_specs=[pl.BlockSpec(memory_space=pltpu.VMEM)] * len(parts),
        compiler_params=SMALL,
        cost_estimate=COST,
        name="add_z",
    )(*parts)


def forward_body(nb, rank, nz, tenant_ref, place_ref, cot_ref, w_hbm, a_hbm, up_hbm, *refs):
    pieces = refs[: 2 * nz + 2]
    part_ref, dot_ref, low_ref = refs[-12:-9]
    w_ref, a_ref, up_ref, x_ref, acc_ref, low_acc, w_sem, sem, x_sem = refs[-9:]
    rows, cols = acc_ref.shape
    piece = BLOCK // 4
    depth = w_ref.shape[0]
    steps = STEPS
    db = depth // steps
    z, x, core, first = place_ref[0], place_ref[1], place_ref[2], place_ref[3]

    def each(h, act):
        at = pl.ds(h * depth // 2, depth // 2)
        for n in range(4 * nz):
            k, fx, fc = n // 4, (n // 2) % 2, n % 2
            src = pieces[2 * nz + fx] if fc else pieces[2 * k + fx]
            src = src.at[pl.ds(k * piece if fc else 0, piece), at]
            b = lax.rem(z + (nz - k), nz) - first

            @pl.when(jnp.logical_and(b >= 0, b < nb))
            def _():
                row = (b * 4 + (x ^ fx) * 2 + (core ^ fc)) * piece
                dst = pl.ds(pl.multiple_of(row, piece), piece)
                act(pltpu.make_async_copy(src, x_ref.at[dst, at], x_sem.at[h, n]), n % 2)

    copies = factor_copies(tenant_ref, first, a_hbm, a_ref, sem, 0)
    late = factor_copies(tenant_ref, first, up_hbm, up_ref, sem, nb)
    each(0, lambda copy, queue: copy.start(priority=queue))
    for copy in copies:
        copy.start()
    for i in range(AHEAD):
        weight_copy(w_hbm, w_ref, w_sem, i).start(priority=i % 2)
    each(1, lambda copy, queue: copy.start(priority=queue))
    for copy in late:
        copy.start()
    acc_ref[...] = jnp.zeros_like(acc_ref)
    low_acc[...] = jnp.zeros_like(low_acc)
    for copy in copies:
        copy.wait()

    def block(i, carry):
        for h in range(2):

            @pl.when(i == h * (steps // 2))
            def _():
                each(h, lambda copy, queue: copy.wait())

        weight_block(w_hbm, w_ref, w_sem, i, steps)
        at = pl.ds(pl.multiple_of(i * db, db), db)
        xs = x_ref[:, at]
        acc_ref[...] += jnp.dot(xs, w_ref[at, :], preferred_element_type=F32)
        low_acc[...] += lax.dot_general(a_ref[:, at], xs, LAST, preferred_element_type=F32)
        return carry

    lax.fori_loop(0, steps, block, 0)
    low = low_acc[...]
    owner = lax.broadcasted_iota(jnp.int32, low.shape, 0) // rank
    block_of = lax.broadcasted_iota(jnp.int32, low.shape, 1) // BLOCK
    low = jnp.where(owner == block_of, low, 0.0)
    low_ref[...] = jnp.sum(low.reshape(nb, rank, rows), axis=0)
    hi = low.astype(BF16).astype(F32)
    lowcat = jnp.concatenate([hi, low - hi], axis=0).T.astype(BF16)
    for copy in late:
        copy.wait()
    up = up_ref[...]
    up = jnp.concatenate([up, up], axis=0)
    for i in range(nb):
        here = slice(i * BLOCK, (i + 1) * BLOCK)
        part = acc_ref[here, :] + jnp.dot(lowcat[here, :], up, preferred_element_type=F32)
        part_ref[here, :] = part.astype(part_ref.dtype)
        product = part * cot_ref[here, :].astype(F32)
        dot_ref[i : i + 1, :] = jnp.sum(product, axis=0, keepdims=True)


def forward(tenant, place, weight, cot, down, up, pieces, nz, out_dtype, deps):
    depth, cols = weight.shape
    rows = cot.shape[0]
    nb = rows // BLOCK
    rank = down.shape[1]
    shapes = (
        jax.ShapeDtypeStruct((rows, cols), out_dtype),
        jax.ShapeDtypeStruct((nb, cols), F32),
        jax.ShapeDtypeStruct((rank, rows), F32),
    )
    return pl.pallas_call(
        functools.partial(forward_body, nb, rank, nz),
        out_shape=shapes,
        grid_spec=pltpu.PrefetchScalarGridSpec(
            num_scalar_prefetch=2,
            grid=(1,),
            in_specs=[same_block(cot)] + [IN_HBM] * (3 + len(pieces)) + order_specs(deps),
            out_specs=[same_block(s) for s in shapes],
            scratch_shapes=[
                pltpu.VMEM((depth, cols), BF16),
                pltpu.VMEM((nb * rank, depth), BF16),
                pltpu.VMEM((nb * rank, cols), BF16),
                pltpu.VMEM((rows, depth), BF16),
                pltpu.VMEM((rows, cols), F32),
                pltpu.VMEM((nb * rank, rows), F32),
                pltpu.SemaphoreType.DMA((PARTS,)),
                pltpu.SemaphoreType.DMA((2 * nb,)),
                pltpu.SemaphoreType.DMA((2, 4 * nz)),
            ],
        ),
        compiler_params=PARAMS,
        cost_estimate=COST,
        name="forward",
    )(tenant, place, cot, weight, down, up, *pieces, *deps)


def shards(inputs, weight, adapter_down_factors, adapter_up_factors, magnitude, cotangent, tenant):
    col_count, row_count = lax.axis_size("col"), lax.axis_size("row")
    nz = col_count // 4
    down, up = adapter_down_factors, adapter_up_factors
    tenant_number, rank, depth = down.shape
    cols = weight.shape[1]
    tokens = tenant.shape[0]
    nblk = tokens // BLOCK
    rows_row = tokens // row_count
    blocks_mine = rows_row // BLOCK
    col, row = lax.axis_index("col"), lax.axis_index("row")
    z, x, core = col >> 2, (col >> 1) & 1, col & 1

    def move(value, dz, fx, fc):
        perm = []
        for source in range(col_count):
            sz, sx, sc = source // 4, (source // 2) % 2, source % 2
            perm.append((source, ((sz + dz) % nz) * 4 + (sx ^ fx) * 2 + (sc ^ fc)))
        return lax.ppermute(value, "col", perm)

    def swap(value):
        return lax.ppermute(value, "row", [(0, 1), (1, 0)])

    def place(*firsts):
        return jnp.stack([z, x, core, *firsts]).astype(jnp.int32)

    pair = row_count == 2

    def once(value, other):
        return lax.optimization_barrier((value, other))[0]

    along_z = [inputs] + [move(inputs, k, 0, 0) for k in range(1, nz)]
    along_x = {0: move(inputs, 0, 1, 0)}

    def other_x(k, after):
        along_z[k] = once(along_z[k], after)
        along_x[k] = move(along_z[k], 0, 1, 0)

    def other_core(part):
        return move(jnp.concatenate(part, axis=0), 0, 0, 1)

    nsq = partial_norms(tenant, weight, down, up)
    if pair:
        nsq_a, nsq_b = nsq, swap(once(nsq, along_x[0]))
        firsts = [row * blocks_mine, (1 - row) * blocks_mine]
        cots = [cotangent, swap(cotangent)]
    else:
        nsq_a, nsq_b = lax.psum(nsq, "row"), jnp.zeros_like(nsq)
        firsts = [0 * row]
        cots = [lax.all_gather(cotangent, "row", axis=0, tiled=True)]
    places = [place(first) for first in firsts]

    def gradient(g, add, deps):
        return input_gradient(
            tenant, places[g], cots[g], nsq_a, nsq_b, magnitude, weight, down, up, add, deps
        )

    def cross_core(made, deps):
        return add_core(made[2], move(made[3], 0, 0, 1), deps)

    def cross_x(pairs, deps):
        mine, *away = add_x(place(*firsts), pairs, nz, deps)
        return [mine] + [move(block, k + 1, 0, 0) for k, block in enumerate(away)]

    def across_x(made):
        return made[0], move(made[1], 0, 1, 0)

    def scaled_output(pre, scale):
        out = pre.reshape(blocks_mine, BLOCK, cols) * scale[:, None, :]
        return out.astype(BF16).reshape(rows_row, cols)

    if pair:
        ours = gradient(0, [], [cots[1]])
        for k in [nz - 1] + list(range(1, nz - 1)):
            other_x(k, ours[0])
        core_z = other_core(along_z)
        theirs = gradient(1, [ours[2], move(ours[3], 0, 0, 1)], [core_z])
        near = across_x(theirs[4:])
        along_x = [along_x[k] for k in range(nz)]
        along_x[nz - 2] = once(along_x[nz - 2], theirs[0])
        core_x = other_core(along_x)
        far = cross_core(theirs, [core_x])
        pieces = [piece for both in zip(along_z, along_x) for piece in both] + [core_z, core_x]

        def project(g, out_dtype, deps):
            return forward(
                tenant, places[g], weight, cots[g], down, up, pieces, nz, out_dtype, deps
            )

        away, dots_away, low_away = project(1, BF16, [far[0]])
        arrived = swap(away)
        finals = cross_x([near, across_x(far)], [dots_away])
        part, dots_here, low_here = project(0, F32, [finals[0]])
        dots = jnp.concatenate([dots_here, dots_away], axis=0)
        low = jnp.concatenate([low_here, low_away], axis=1)
        output = scaled_output(part + arrived.astype(F32), ours[0])
        new_dots = swap(once(dots, finals[nz // 2]))
        new_low = once(swap(once(low, finals[nz - 1])), output)
        dots = dots + jnp.roll(new_dots, blocks_mine, axis=0)
        low = low + jnp.roll(new_low, rows_row, axis=1)
        parts = [ours, theirs]
    else:
        ours = gradient(0, [], [])
        near = across_x(cross_core(ours, []))
        for k in range(1, nz):
            other_x(k, inputs)
        along_x = [along_x[k] for k in range(nz)]
        pieces = [piece for both in zip(along_z, along_x) for piece in both]
        pieces += [other_core(along_z), other_core(along_x)]
        part, dots, low = forward(
            tenant, places[0], weight, cots[0], down, up, pieces, nz, F32, []
        )
        finals = cross_x([near], [])
        low, dots = lax.psum((low, dots), "row")
        parts = [ours]

    scales = jnp.concatenate([group[0] for group in parts], axis=0)

    tenants = jnp.arange(tenant_number, dtype=jnp.int32)
    block_tenant = tenant.reshape(nblk, BLOCK)[:, 0]
    size = nblk // len(parts)
    owners = jnp.concatenate(
        [lax.dynamic_slice_in_dim(block_tenant, first, size, 0) for first in firsts]
    )
    low = low.astype(BF16)
    grad_b = 0.0
    for g, group in enumerate(parts):
        owner = jnp.repeat(owners[g * size : (g + 1) * size], BLOCK)
        mine = low[:, g * size * BLOCK : (g + 1) * size * BLOCK]
        wide = jnp.where((tenants[:, None] == owner[None, :])[:, None, :], mine[None], 0)
        wide = wide.reshape(tenant_number * rank, size * BLOCK)
        grad_b = grad_b + jnp.dot(wide, group[1], preferred_element_type=F32)
    grad_b = grad_b.reshape(tenant_number, rank, cols)
    hit = (tenants[:, None] == owners[None, :])[:, :, None]
    terms = jnp.where(hit, (dots * scales)[None], 0.0)
    grad_m = 0.0
    for g in range(len(parts)):
        group = terms[:, g * size : (g + 1) * size]
        grad_m = grad_m + functools.reduce(jnp.add, [group[:, i] for i in range(size)])
    grad_inputs = add_z([once(finals[0], grad_b)] + finals[1:])
    if not pair:
        pre = lax.psum_scatter(part, "row", scatter_dimension=0, tiled=True)
        scale_mine = lax.dynamic_slice_in_dim(scales, row * blocks_mine, blocks_mine, 0)
        output = scaled_output(pre, scale_mine)
    return (output, grad_inputs, grad_b, grad_m / magnitude)


def solution(mesh):
    return jax.shard_map(
        shards,
        mesh=mesh,
        in_specs=(
            P("col", "row"),
            P("row", "col"),
            P(None, None, "row"),
            P(None, None, "col"),
            P(None, "col"),
            P("row", "col"),
            P(),
        ),
        out_specs=(P("row", "col"), P("col", "row"), P(None, None, "col"), P(None, "col")),
        check_vma=False,
    )
```

```python
import functools

import jax
import jax.numpy as jnp
from jax import lax
from jax.experimental import pallas as pl
from jax.experimental.pallas import tpu as pltpu
from jax.sharding import PartitionSpec as P

BLOCK = 128
EPS = 1e-06
HIGH = lax.Precision.HIGHEST
STEPS = 8
PARTS = 16
AHEAD = 6
F32 = jnp.float32
BF16 = jnp.bfloat16
COST = pl.CostEstimate(flops=1000, bytes_accessed=1000, transcendentals=0)
LAST = (((1,), (1,)), ((), ()))
PARAMS = pltpu.CompilerParams(vmem_limit_bytes=52 * 1024 * 1024)
LARGE = pltpu.CompilerParams(vmem_limit_bytes=62 * 1024 * 1024)
IN_HBM = pl.BlockSpec(memory_space=pltpu.HBM)


def order_specs(deps):
    return [pl.BlockSpec(memory_space=pl.ANY)] * len(deps)


def same_block(array):
    return pl.BlockSpec(array.shape, lambda *args: (0,) * array.ndim)


def hi_lo(value, axis):
    hi = value.astype(BF16)
    lo = (value - hi.astype(F32)).astype(BF16)
    return jnp.concatenate([hi, lo], axis=axis)


def weight_copy(w_hbm, w_ref, sem, i):
    size = w_ref.shape[0] // PARTS
    rows = pl.ds(pl.multiple_of(i * size, size), size)
    return pltpu.make_async_copy(w_hbm.at[rows, :], w_ref.at[rows, :], sem.at[i])


def weight_block(w_hbm, w_ref, sem, i, steps):
    count = PARTS // steps
    for n in range(count):
        weight_copy(w_hbm, w_ref, sem, i * count + n).wait()
    for n in range(count):
        later = i * count + n + AHEAD

        @pl.when(later < PARTS)
        def _():
            weight_copy(w_hbm, w_ref, sem, later).start()


def factor_copies(tenant_ref, first, hbm, ref, sem, at):
    rank, nblk = hbm.shape[1], tenant_ref.shape[0] // BLOCK
    copies = []
    for b in range(ref.shape[0] // rank):
        src = hbm.at[tenant_ref[lax.rem(first + b, nblk) * BLOCK]]
        dst = ref.at[pl.ds(b * rank, rank), :]
        copies.append(pltpu.make_async_copy(src, dst, sem.at[at + b]))
    return copies


def norm_body(nblk, rank, tenant_ref, w_hbm, a_hbm, up_hbm, nsq_ref, *refs):
    w_ref, a_ref, up_ref, cross_ref, square_ref, w_sem, sem = refs
    cols = w_ref.shape[1]
    db = w_ref.shape[0] // STEPS
    copies = factor_copies(tenant_ref, 0, a_hbm, a_ref, sem, 0)
    late = factor_copies(tenant_ref, 0, up_hbm, up_ref, sem, nblk)
    for copy in copies:
        copy.start()
    for i in range(AHEAD):
        weight_copy(w_hbm, w_ref, w_sem, i).start()
    for copy in late:
        copy.start()
    cross_ref[...] = jnp.zeros_like(cross_ref)
    square_ref[...] = jnp.zeros_like(square_ref)
    for copy in copies:
        copy.wait()
    step = min(db, 256)

    def block(i, carry):
        weight_block(w_hbm, w_ref, w_sem, i, STEPS)
        squares = square_ref[...]
        for start in range(0, db, step):
            rows = pl.ds(pl.multiple_of(i * db + start, step), step)
            w = w_ref[rows, :]
            cross_ref[...] += jnp.dot(a_ref[:, rows], w, preferred_element_type=F32)
            for at in range(0, step, 16):
                wf = w[at : at + 16, :].astype(F32)
                squares = squares + wf[:8] * wf[:8] + wf[8:] * wf[8:]
        square_ref[...] = squares
        return carry

    lax.fori_loop(0, STEPS, block, 0)
    for copy in late:
        copy.wait()
    gram = lax.dot_general(a_ref[...], a_ref[...], LAST, preferred_element_type=F32)
    row = lax.broadcasted_iota(jnp.int32, gram.shape, 0) // rank
    col = lax.broadcasted_iota(jnp.int32, gram.shape, 1) // rank
    gram = jnp.where(row == col, gram, 0.0)
    up = up_ref[...].astype(F32)
    quad = jnp.dot(gram, up, preferred_element_type=F32, precision=HIGH)
    mixed = (up * (2.0 * cross_ref[...] + quad)).reshape(nblk, rank, cols)
    nsq_ref[...] = jnp.sum(mixed, axis=1) + jnp.sum(square_ref[...], axis=0, keepdims=True)


def partial_norms(tenant, weight, down, up):
    depth, cols = weight.shape
    rank = down.shape[1]
    nblk = tenant.shape[0] // BLOCK
    shape = jax.ShapeDtypeStruct((nblk, cols), F32)
    return pl.pallas_call(
        functools.partial(norm_body, nblk, rank),
        out_shape=shape,
        grid_spec=pltpu.PrefetchScalarGridSpec(
            num_scalar_prefetch=1,
            grid=(1,),
            in_specs=[IN_HBM] * 3,
            out_specs=same_block(shape),
            scratch_shapes=[
                pltpu.VMEM((depth, cols), BF16),
                pltpu.VMEM((nblk * rank, depth), BF16),
                pltpu.VMEM((nblk * rank, cols), BF16),
                pltpu.VMEM((nblk * rank, cols), F32),
                pltpu.VMEM((8, cols), F32),
                pltpu.SemaphoreType.DMA((PARTS,)),
                pltpu.SemaphoreType.DMA((2 * nblk,)),
            ],
        ),
        compiler_params=LARGE,
        cost_estimate=COST,
        name="partial_norms",
    )(tenant, weight, down, up)


def grad_body(nb, rank, adds, tenant_ref, place_ref, cot_ref, nsq_a, nsq_b, mag_ref, *refs):
    w_hbm, a_hbm, up_hbm = refs[:3]
    if adds:
        add_core_body(*refs[3:5], *refs[-9:-7])
        refs = refs[:-9] + refs[-7:]
    scale_ref, sg_ref, keep_ref, send_ref = refs[-11:-7]
    w_ref, a_ref, up_ref, sgp_ref, backp_ref, w_sem, sem = refs[-7:]
    rows, db = sg_ref.shape[0], keep_ref.shape[1]
    piece = BLOCK // 4
    half = rows // 2
    step = pl.program_id(0)
    x, core, first = place_ref[1], place_ref[2], place_ref[3]

    @pl.when(step == 0)
    def _():
        copies = factor_copies(tenant_ref, first, up_hbm, up_ref, sem, 0)
        copies += factor_copies(tenant_ref, first, a_hbm, a_ref, sem, nb)
        for copy in copies:
            copy.start()
        for i in range(AHEAD):
            weight_copy(w_hbm, w_ref, w_sem, i).start()
        for b in range(nb):
            at = first + b
            total = nsq_a[pl.ds(at, 1), :] + nsq_b[pl.ds(at, 1), :]
            scale = mag_ref[pl.ds(tenant_ref[at * BLOCK], 1), :] / jnp.sqrt(total + EPS)
            scale_ref[b : b + 1, :] = scale
            here = slice(b * BLOCK, (b + 1) * BLOCK)
            sg_ref[here, :] = (cot_ref[here, :].astype(F32) * scale).astype(BF16)
        for fc in range(2):
            for fx in range(2):
                for b in range(nb):
                    c = b * 4 + (x ^ fx) * 2 + (core ^ fc)
                    src = pl.ds(pl.multiple_of(c * piece, piece), piece)
                    at = ((fc * 2 + fx) * nb + b) * piece
                    sgp_ref[at : at + piece, :] = sg_ref[src, :]
        for copy in copies:
            copy.wait()
        back = lax.dot_general(sgp_ref[...], up_ref[...], LAST, preferred_element_type=F32)
        block = lax.broadcasted_iota(jnp.int32, back.shape, 0) // piece % nb
        owner = lax.broadcasted_iota(jnp.int32, back.shape, 1) // rank
        backp_ref[...] = hi_lo(jnp.where(owner == block, back, 0.0), 1)

    weight_block(w_hbm, w_ref, w_sem, step, STEPS)
    at = pl.ds(pl.multiple_of(step * db, db), db)
    down = a_ref[:, at]
    down = jnp.concatenate([down, down], axis=0)
    part = lax.dot_general(sgp_ref[...], w_ref[at, :], LAST, preferred_element_type=F32)
    part = part + jnp.dot(backp_ref[...], down, preferred_element_type=F32)
    keep_ref[...] = part[:half, :]
    send_ref[...] = part[half:, :].astype(BF16)


def input_gradient(tenant, place, cot, nsq_a, nsq_b, magnitude, weight, down, up, add, deps):
    depth, cols = weight.shape
    rows = cot.shape[0]
    nb = rows // BLOCK
    rank = down.shape[1]
    db = depth // STEPS
    shapes = (
        jax.ShapeDtypeStruct((nb, cols), F32),
        jax.ShapeDtypeStruct((rows, cols), BF16),
        jax.ShapeDtypeStruct((rows // 2, depth), F32),
        jax.ShapeDtypeStruct((rows // 2, depth), BF16),
    )
    if add:
        shapes += tuple(jax.ShapeDtypeStruct((rows // 4, depth), t) for t in (F32, BF16))

    def columns(array):
        return pl.BlockSpec((array.shape[0], db), lambda i, t, p: (0, i))

    return pl.pallas_call(
        functools.partial(grad_body, nb, rank, len(add)),
        out_shape=shapes,
        grid_spec=pltpu.PrefetchScalarGridSpec(
            num_scalar_prefetch=2,
            grid=(STEPS,),
            in_specs=[same_block(a) for a in (cot, nsq_a, nsq_b, magnitude)]
            + [IN_HBM] * 3
            + [columns(a) for a in add]
            + order_specs(deps),
            out_specs=[same_block(s) for s in shapes[:2]] + [columns(s) for s in shapes[2:]],
            scratch_shapes=[
                pltpu.VMEM((depth, cols), BF16),
                pltpu.VMEM((nb * rank, depth), BF16),
                pltpu.VMEM((nb * rank, cols), BF16),
                pltpu.VMEM((rows, cols), BF16),
                pltpu.VMEM((rows, 2 * nb * rank), BF16),
                pltpu.SemaphoreType.DMA((PARTS,)),
                pltpu.SemaphoreType.DMA((2 * nb,)),
            ],
        ),
        compiler_params=PARAMS,
        cost_estimate=COST,
        name="input_gradient",
    )(tenant, place, cot, nsq_a, nsq_b, magnitude, weight, down, up, *add, *deps)


def add_core_body(keep_ref, recv_ref, *refs):
    mine_ref, send_ref = refs[-2:]
    half = mine_ref.shape[0]
    mine_ref[...] = keep_ref[:half, :] + recv_ref[:half, :].astype(F32)
    send_ref[...] = (keep_ref[half:, :] + recv_ref[half:, :].astype(F32)).astype(BF16)


def add_core(keep, recv, deps):
    rows, size = keep.shape
    block = size // 2
    return pl.pallas_call(
        add_core_body,
        out_shape=(
            jax.ShapeDtypeStruct((rows // 2, size), F32),
            jax.ShapeDtypeStruct((rows // 2, size), BF16),
        ),
        grid=(2,),
        in_specs=[pl.BlockSpec((rows, block), lambda i: (0, i))] * 2 + order_specs(deps),
        out_specs=[pl.BlockSpec((rows // 2, block), lambda i: (0, i))] * 2,
        compiler_params=PARAMS,
        cost_estimate=COST,
        name="add_core",
    )(keep, recv, *deps)


def add_x_body(groups, nz, place_ref, *refs):
    outs, total_ref = refs[-nz - 1 : -1], refs[-1]
    piece = outs[0].shape[0]
    z = place_ref[0]
    for g in range(groups):
        keep_ref, recv_ref = refs[2 * g : 2 * g + 2]
        first = pl.multiple_of(place_ref[3 + g] * piece, piece)
        total = keep_ref[...] + recv_ref[...].astype(F32)
        total_ref[pl.ds(first, keep_ref.shape[0]), :] = total
    for k in range(nz):
        at = pl.multiple_of(lax.rem(z + k, nz) * piece, piece)
        outs[k][...] = total_ref[pl.ds(at, piece), :].astype(outs[k].dtype)


def add_x(place, pairs, nz, deps):
    piece = BLOCK // 4
    size = pairs[0][0].shape[1]
    block = size // 2
    operands = [array for pair in pairs for array in pair]

    def spec(array):
        return pl.BlockSpec((array.shape[0], block), lambda i, p: (0, i))

    shapes = tuple(jax.ShapeDtypeStruct((piece, size), BF16 if k else F32) for k in range(nz))
    return pl.pallas_call(
        functools.partial(add_x_body, len(pairs), nz),
        out_shape=shapes,
        grid_spec=pltpu.PrefetchScalarGridSpec(
            num_scalar_prefetch=1,
            grid=(2,),
            in_specs=[spec(a) for a in operands] + order_specs(deps),
            out_specs=[spec(s) for s in shapes],
            scratch_shapes=[pltpu.VMEM((nz * piece, block), F32)],
        ),
        compiler_params=PARAMS,
        cost_estimate=COST,
        name="add_x",
    )(place, *operands, *deps)


def add_z_body(*refs):
    total = refs[0][...]
    for ref in refs[1:-1]:
        total = total + ref[...].astype(F32)
    refs[-1][...] = total.astype(BF16)


def add_z(parts):
    return pl.pallas_call(
        add_z_body,
        out_shape=jax.ShapeDtypeStruct(parts[0].shape, BF16),
        in_specs=[pl.BlockSpec(memory_space=pltpu.VMEM)] * len(parts),
        compiler_params=PARAMS,
        cost_estimate=COST,
        name="add_z",
    )(*parts)


def forward_body(nb, rank, nz, tenant_ref, place_ref, cot_ref, w_hbm, a_hbm, up_hbm, *refs):
    pieces = refs[: 2 * nz + 2]
    part_ref, dot_ref, low_ref = refs[-12:-9]
    w_ref, a_ref, up_ref, x_ref, acc_ref, low_acc, w_sem, sem, x_sem = refs[-9:]
    rows, cols = acc_ref.shape
    piece = BLOCK // 4
    depth = w_ref.shape[0]
    steps = STEPS
    db = depth // steps
    z, x, core, first = place_ref[0], place_ref[1], place_ref[2], place_ref[3]

    def each(h, act):
        at = pl.ds(h * depth // 2, depth // 2)
        for n in range(4 * nz):
            k, fx, fc = n // 4, (n // 2) % 2, n % 2
            src = pieces[2 * nz + fx] if fc else pieces[2 * k + fx]
            src = src.at[pl.ds(k * piece if fc else 0, piece), at]
            b = lax.rem(z + (nz - k), nz) - first

            @pl.when(jnp.logical_and(b >= 0, b < nb))
            def _():
                row = (b * 4 + (x ^ fx) * 2 + (core ^ fc)) * piece
                dst = pl.ds(pl.multiple_of(row, piece), piece)
                act(pltpu.make_async_copy(src, x_ref.at[dst, at], x_sem.at[h, n]))

    copies = factor_copies(tenant_ref, first, a_hbm, a_ref, sem, 0)
    late = factor_copies(tenant_ref, first, up_hbm, up_ref, sem, nb)
    each(0, lambda copy: copy.start())
    for copy in copies:
        copy.start()
    for i in range(AHEAD):
        weight_copy(w_hbm, w_ref, w_sem, i).start()
    each(1, lambda copy: copy.start())
    for copy in late:
        copy.start()
    acc_ref[...] = jnp.zeros_like(acc_ref)
    low_acc[...] = jnp.zeros_like(low_acc)
    for copy in copies:
        copy.wait()

    def block(i, carry):
        for h in range(2):

            @pl.when(i == h * (steps // 2))
            def _():
                each(h, lambda copy: copy.wait())

        weight_block(w_hbm, w_ref, w_sem, i, steps)
        at = pl.ds(pl.multiple_of(i * db, db), db)
        xs = x_ref[:, at]
        acc_ref[...] += jnp.dot(xs, w_ref[at, :], preferred_element_type=F32)
        low_acc[...] += lax.dot_general(a_ref[:, at], xs, LAST, preferred_element_type=F32)
        return carry

    lax.fori_loop(0, steps, block, 0)
    low = low_acc[...]
    owner = lax.broadcasted_iota(jnp.int32, low.shape, 0) // rank
    block_of = lax.broadcasted_iota(jnp.int32, low.shape, 1) // BLOCK
    low = jnp.where(owner == block_of, low, 0.0)
    low_ref[...] = jnp.sum(low.reshape(nb, rank, rows), axis=0)
    hi = low.astype(BF16).astype(F32)
    lowcat = jnp.concatenate([hi, low - hi], axis=0).T.astype(BF16)
    for copy in late:
        copy.wait()
    up = up_ref[...]
    up = jnp.concatenate([up, up], axis=0)
    for i in range(nb):
        here = slice(i * BLOCK, (i + 1) * BLOCK)
        part = acc_ref[here, :] + jnp.dot(lowcat[here, :], up, preferred_element_type=F32)
        part_ref[here, :] = part.astype(part_ref.dtype)
        product = part * cot_ref[here, :].astype(F32)
        dot_ref[i : i + 1, :] = jnp.sum(product, axis=0, keepdims=True)


def forward(tenant, place, weight, cot, down, up, pieces, nz, out_dtype, deps):
    depth, cols = weight.shape
    rows = cot.shape[0]
    nb = rows // BLOCK
    rank = down.shape[1]
    shapes = (
        jax.ShapeDtypeStruct((rows, cols), out_dtype),
        jax.ShapeDtypeStruct((nb, cols), F32),
        jax.ShapeDtypeStruct((rank, rows), F32),
    )
    return pl.pallas_call(
        functools.partial(forward_body, nb, rank, nz),
        out_shape=shapes,
        grid_spec=pltpu.PrefetchScalarGridSpec(
            num_scalar_prefetch=2,
            grid=(1,),
            in_specs=[same_block(cot)] + [IN_HBM] * (3 + len(pieces)) + order_specs(deps),
            out_specs=[same_block(s) for s in shapes],
            scratch_shapes=[
                pltpu.VMEM((depth, cols), BF16),
                pltpu.VMEM((nb * rank, depth), BF16),
                pltpu.VMEM((nb * rank, cols), BF16),
                pltpu.VMEM((rows, depth), BF16),
                pltpu.VMEM((rows, cols), F32),
                pltpu.VMEM((nb * rank, rows), F32),
                pltpu.SemaphoreType.DMA((PARTS,)),
                pltpu.SemaphoreType.DMA((2 * nb,)),
                pltpu.SemaphoreType.DMA((2, 4 * nz)),
            ],
        ),
        compiler_params=PARAMS,
        cost_estimate=COST,
        name="forward",
    )(tenant, place, cot, weight, down, up, *pieces, *deps)


def shards(inputs, weight, adapter_down_factors, adapter_up_factors, magnitude, cotangent, tenant):
    col_count, row_count = lax.axis_size("col"), lax.axis_size("row")
    nz = col_count // 4
    down, up = adapter_down_factors, adapter_up_factors
    tenant_number, rank, depth = down.shape
    cols = weight.shape[1]
    tokens = tenant.shape[0]
    nblk = tokens // BLOCK
    rows_row = tokens // row_count
    blocks_mine = rows_row // BLOCK
    col, row = lax.axis_index("col"), lax.axis_index("row")
    z, x, core = col >> 2, (col >> 1) & 1, col & 1

    def move(value, dz, fx, fc):
        perm = []
        for source in range(col_count):
            sz, sx, sc = source // 4, (source // 2) % 2, source % 2
            perm.append((source, ((sz + dz) % nz) * 4 + (sx ^ fx) * 2 + (sc ^ fc)))
        return lax.ppermute(value, "col", perm)

    def swap(value):
        return lax.ppermute(value, "row", [(0, 1), (1, 0)])

    def place(*firsts):
        return jnp.stack([z, x, core, *firsts]).astype(jnp.int32)

    pair = row_count == 2

    def once(value, other):
        return lax.optimization_barrier((value, other))[0]

    along_z = [inputs] + [move(inputs, k, 0, 0) for k in range(1, nz)]
    along_x = {0: move(inputs, 0, 1, 0)}

    def other_x(k, after):
        along_z[k] = once(along_z[k], after)
        along_x[k] = move(along_z[k], 0, 1, 0)

    def other_core(part):
        return move(jnp.concatenate(part, axis=0), 0, 0, 1)

    nsq = partial_norms(tenant, weight, down, up)
    if pair:
        nsq_a, nsq_b = nsq, swap(once(nsq, along_x[0]))
        firsts = [row * blocks_mine, (1 - row) * blocks_mine]
        cots = [cotangent, swap(cotangent)]
    else:
        nsq_a, nsq_b = lax.psum(nsq, "row"), jnp.zeros_like(nsq)
        firsts = [0 * row]
        cots = [lax.all_gather(cotangent, "row", axis=0, tiled=True)]
    places = [place(first) for first in firsts]

    def gradient(g, add, deps):
        return input_gradient(
            tenant, places[g], cots[g], nsq_a, nsq_b, magnitude, weight, down, up, add, deps
        )

    def cross_core(made, deps):
        return add_core(made[2], move(made[3], 0, 0, 1), deps)

    def cross_x(pairs, deps):
        mine, *away = add_x(place(*firsts), pairs, nz, deps)
        return [mine] + [move(block, k + 1, 0, 0) for k, block in enumerate(away)]

    def across_x(made):
        return made[0], move(made[1], 0, 1, 0)

    if pair:
        ours = gradient(0, [], [cots[1]])
        for k in [nz - 1] + list(range(1, nz - 1)):
            other_x(k, ours[0])
        core_z = other_core(along_z)
        theirs = gradient(1, [ours[2], move(ours[3], 0, 0, 1)], [core_z])
        near = across_x(theirs[4:])
        along_x = [along_x[k] for k in range(nz)]
        along_x[nz - 2] = once(along_x[nz - 2], theirs[0])
        core_x = other_core(along_x)
        far = cross_core(theirs, [core_x])
        pieces = [piece for both in zip(along_z, along_x) for piece in both] + [core_z, core_x]

        def project(g, out_dtype, deps):
            return forward(
                tenant, places[g], weight, cots[g], down, up, pieces, nz, out_dtype, deps
            )

        away, dots_away, low_away = project(1, BF16, [far[0]])
        arrived = swap(away)
        finals = cross_x([near, across_x(far)], [dots_away])
        part, dots_here, low_here = project(0, F32, [finals[0]])
        dots = jnp.concatenate([dots_here, dots_away], axis=0)
        low = jnp.concatenate([low_here, low_away], axis=1)
        new_dots = swap(once(dots, finals[nz // 2]))
        new_low = swap(once(low, finals[nz - 1]))
        dots = dots + jnp.roll(new_dots, blocks_mine, axis=0)
        low = low + jnp.roll(new_low, rows_row, axis=1)
        parts = [ours, theirs]
    else:
        ours = gradient(0, [], [])
        near = across_x(cross_core(ours, []))
        for k in range(1, nz):
            other_x(k, inputs)
        along_x = [along_x[k] for k in range(nz)]
        pieces = [piece for both in zip(along_z, along_x) for piece in both]
        pieces += [other_core(along_z), other_core(along_x)]
        part, dots, low = forward(
            tenant, places[0], weight, cots[0], down, up, pieces, nz, F32, []
        )
        finals = cross_x([near], [])
        low, dots = lax.psum((low, dots), "row")
        parts = [ours]

    scales = jnp.concatenate([group[0] for group in parts], axis=0)

    tenants = jnp.arange(tenant_number, dtype=jnp.int32)
    block_tenant = tenant.reshape(nblk, BLOCK)[:, 0]
    size = nblk // len(parts)
    owners = jnp.concatenate(
        [lax.dynamic_slice_in_dim(block_tenant, first, size, 0) for first in firsts]
    )
    low = low.astype(BF16)
    grad_b = 0.0
    for g, group in enumerate(parts):
        owner = jnp.repeat(owners[g * size : (g + 1) * size], BLOCK)
        mine = low[:, g * size * BLOCK : (g + 1) * size * BLOCK]
        wide = jnp.where((tenants[:, None] == owner[None, :])[:, None, :], mine[None], 0)
        wide = wide.reshape(tenant_number * rank, size * BLOCK)
        grad_b = grad_b + jnp.dot(wide, group[1], preferred_element_type=F32)
    grad_b = grad_b.reshape(tenant_number, rank, cols)
    hit = (tenants[:, None] == owners[None, :])[:, :, None]
    terms = jnp.where(hit, (dots * scales)[None], 0.0)
    grad_m = 0.0
    for g in range(len(parts)):
        group = terms[:, g * size : (g + 1) * size]
        grad_m = grad_m + functools.reduce(jnp.add, [group[:, i] for i in range(size)])
    grad_inputs = add_z([once(finals[0], grad_b)] + finals[1:])
    if pair:
        pre = part + arrived.astype(F32)
        scale_mine = parts[0][0]
    else:
        pre = lax.psum_scatter(part, "row", scatter_dimension=0, tiled=True)
        scale_mine = lax.dynamic_slice_in_dim(scales, row * blocks_mine, blocks_mine, 0)
    output = (pre.reshape(blocks_mine, BLOCK, cols) * scale_mine[:, None, :]).astype(BF16)
    output = output.reshape(rows_row, cols)
    return (output, grad_inputs, grad_b, grad_m / magnitude)


def solution(mesh):
    return jax.shard_map(
        shards,
        mesh=mesh,
        in_specs=(
            P("col", "row"),
            P("row", "col"),
            P(None, None, "row"),
            P(None, None, "col"),
            P(None, "col"),
            P("row", "col"),
            P(),
        ),
        out_specs=(P("row", "col"), P("col", "row"), P(None, None, "col"), P(None, "col")),
        check_vma=False,
    )
```

```python
import functools

import jax
import jax.numpy as jnp
from jax import lax
from jax.experimental import pallas as pl
from jax.experimental.pallas import tpu as pltpu
from jax.sharding import PartitionSpec as P

BLOCK = 128
EPS = 1e-06
HIGH = lax.Precision.HIGHEST
STEPS = 8
PARTS = 16
AHEAD = 6
F32 = jnp.float32
BF16 = jnp.bfloat16
COST = pl.CostEstimate(flops=1000, bytes_accessed=1000, transcendentals=0)
LAST = (((1,), (1,)), ((), ()))
PARAMS = pltpu.CompilerParams(vmem_limit_bytes=52 * 1024 * 1024)
SMALL = pltpu.CompilerParams(vmem_limit_bytes=12 * 1024 * 1024)
IN_HBM = pl.BlockSpec(memory_space=pltpu.HBM)


def order_specs(deps):
    return [pl.BlockSpec(memory_space=pl.ANY)] * len(deps)


def same_block(array):
    return pl.BlockSpec(array.shape, lambda *args: (0,) * array.ndim)


def hi_lo(value, axis):
    hi = value.astype(BF16)
    lo = (value - hi.astype(F32)).astype(BF16)
    return jnp.concatenate([hi, lo], axis=axis)


def weight_copy(w_hbm, w_ref, sem, i):
    size = w_ref.shape[0] // PARTS
    rows = pl.ds(pl.multiple_of(i * size, size), size)
    return pltpu.make_async_copy(w_hbm.at[rows, :], w_ref.at[rows, :], sem.at[i])


def weight_block(w_hbm, w_ref, sem, i, steps):
    count = PARTS // steps
    for n in range(count):
        weight_copy(w_hbm, w_ref, sem, i * count + n).wait()
    for n in range(count):
        later = i * count + n + AHEAD

        @pl.when(later < PARTS)
        def _():
            weight_copy(w_hbm, w_ref, sem, later).start()


def factor_copies(tenant_ref, first, hbm, ref, sem, at):
    rank, nblk = hbm.shape[1], tenant_ref.shape[0] // BLOCK
    copies = []
    for b in range(ref.shape[0] // rank):
        src = hbm.at[tenant_ref[lax.rem(first + b, nblk) * BLOCK]]
        dst = ref.at[pl.ds(b * rank, rank), :]
        copies.append(pltpu.make_async_copy(src, dst, sem.at[at + b]))
    return copies


def norm_body(nblk, rank, tenant_ref, w_hbm, a_hbm, up_hbm, nsq_ref, *refs):
    w_ref, a_ref, up_ref, cross_ref, square_ref, w_sem, sem = refs
    cols = w_ref.shape[1]
    db = w_ref.shape[0] // STEPS
    copies = factor_copies(tenant_ref, 0, a_hbm, a_ref, sem, 0)
    late = factor_copies(tenant_ref, 0, up_hbm, up_ref, sem, nblk)
    for copy in copies:
        copy.start()
    for i in range(AHEAD):
        weight_copy(w_hbm, w_ref, w_sem, i).start()
    for copy in late:
        copy.start()
    cross_ref[...] = jnp.zeros_like(cross_ref)
    square_ref[...] = jnp.zeros_like(square_ref)
    for copy in copies:
        copy.wait()
    step = min(db, 256)

    def block(i, carry):
        weight_block(w_hbm, w_ref, w_sem, i, STEPS)
        squares = square_ref[...]
        for start in range(0, db, step):
            rows = pl.ds(pl.multiple_of(i * db + start, step), step)
            w = w_ref[rows, :]
            cross_ref[...] += jnp.dot(a_ref[:, rows], w, preferred_element_type=F32)
            for at in range(0, step, 16):
                wf = w[at : at + 16, :].astype(F32)
                squares = squares + wf[:8] * wf[:8] + wf[8:] * wf[8:]
        square_ref[...] = squares
        return carry

    lax.fori_loop(0, STEPS, block, 0)
    for copy in late:
        copy.wait()
    gram = lax.dot_general(a_ref[...], a_ref[...], LAST, preferred_element_type=F32)
    row = lax.broadcasted_iota(jnp.int32, gram.shape, 0) // rank
    col = lax.broadcasted_iota(jnp.int32, gram.shape, 1) // rank
    gram = jnp.where(row == col, gram, 0.0)
    up = up_ref[...].astype(F32)
    quad = jnp.dot(gram, up, preferred_element_type=F32, precision=HIGH)
    mixed = (up * (2.0 * cross_ref[...] + quad)).reshape(nblk, rank, cols)
    nsq_ref[...] = jnp.sum(mixed, axis=1) + jnp.sum(square_ref[...], axis=0, keepdims=True)


def partial_norms(tenant, weight, down, up):
    depth, cols = weight.shape
    rank = down.shape[1]
    nblk = tenant.shape[0] // BLOCK
    shape = jax.ShapeDtypeStruct((nblk, cols), F32)
    return pl.pallas_call(
        functools.partial(norm_body, nblk, rank),
        out_shape=shape,
        grid_spec=pltpu.PrefetchScalarGridSpec(
            num_scalar_prefetch=1,
            grid=(1,),
            in_specs=[IN_HBM] * 3,
            out_specs=same_block(shape),
            scratch_shapes=[
                pltpu.VMEM((depth, cols), BF16),
                pltpu.VMEM((nblk * rank, depth), BF16),
                pltpu.VMEM((nblk * rank, cols), BF16),
                pltpu.VMEM((nblk * rank, cols), F32),
                pltpu.VMEM((8, cols), F32),
                pltpu.SemaphoreType.DMA((PARTS,)),
                pltpu.SemaphoreType.DMA((2 * nblk,)),
            ],
        ),
        compiler_params=PARAMS,
        cost_estimate=COST,
        name="partial_norms",
    )(tenant, weight, down, up)


def grad_body(nb, rank, adds, tenant_ref, place_ref, cot_ref, nsq_a, nsq_b, mag_ref, *refs):
    w_hbm, a_hbm, up_hbm = refs[:3]
    if adds:
        add_core_body(*refs[3:5], *refs[-9:-7])
        refs = refs[:-9] + refs[-7:]
    scale_ref, sg_ref, keep_ref, send_ref = refs[-11:-7]
    w_ref, a_ref, up_ref, sgp_ref, backp_ref, w_sem, sem = refs[-7:]
    rows, db = sg_ref.shape[0], keep_ref.shape[1]
    piece = BLOCK // 4
    half = rows // 2
    step = pl.program_id(0)
    x, core, first = place_ref[1], place_ref[2], place_ref[3]

    @pl.when(step == 0)
    def _():
        copies = factor_copies(tenant_ref, first, up_hbm, up_ref, sem, 0)
        copies += factor_copies(tenant_ref, first, a_hbm, a_ref, sem, nb)
        for copy in copies:
            copy.start()
        for i in range(AHEAD):
            weight_copy(w_hbm, w_ref, w_sem, i).start()
        for b in range(nb):
            at = first + b
            total = nsq_a[pl.ds(at, 1), :] + nsq_b[pl.ds(at, 1), :]
            scale = mag_ref[pl.ds(tenant_ref[at * BLOCK], 1), :] / jnp.sqrt(total + EPS)
            scale_ref[b : b + 1, :] = scale
            here = slice(b * BLOCK, (b + 1) * BLOCK)
            sg_ref[here, :] = (cot_ref[here, :].astype(F32) * scale).astype(BF16)
        for fc in range(2):
            for fx in range(2):
                for b in range(nb):
                    c = b * 4 + (x ^ fx) * 2 + (core ^ fc)
                    src = pl.ds(pl.multiple_of(c * piece, piece), piece)
                    at = ((fc * 2 + fx) * nb + b) * piece
                    sgp_ref[at : at + piece, :] = sg_ref[src, :]
        for copy in copies:
            copy.wait()
        back = lax.dot_general(sgp_ref[...], up_ref[...], LAST, preferred_element_type=F32)
        block = lax.broadcasted_iota(jnp.int32, back.shape, 0) // piece % nb
        owner = lax.broadcasted_iota(jnp.int32, back.shape, 1) // rank
        backp_ref[...] = hi_lo(jnp.where(owner == block, back, 0.0), 1)

    weight_block(w_hbm, w_ref, w_sem, step, STEPS)
    at = pl.ds(pl.multiple_of(step * db, db), db)
    down = a_ref[:, at]
    down = jnp.concatenate([down, down], axis=0)
    part = lax.dot_general(sgp_ref[...], w_ref[at, :], LAST, preferred_element_type=F32)
    part = part + jnp.dot(backp_ref[...], down, preferred_element_type=F32)
    keep_ref[...] = part[:half, :]
    send_ref[...] = part[half:, :].astype(BF16)


def input_gradient(tenant, place, cot, nsq_a, nsq_b, magnitude, weight, down, up, add, deps):
    depth, cols = weight.shape
    rows = cot.shape[0]
    nb = rows // BLOCK
    rank = down.shape[1]
    db = depth // STEPS
    shapes = (
        jax.ShapeDtypeStruct((nb, cols), F32),
        jax.ShapeDtypeStruct((rows, cols), BF16),
        jax.ShapeDtypeStruct((rows // 2, depth), F32),
        jax.ShapeDtypeStruct((rows // 2, depth), BF16),
    )
    if add:
        shapes += tuple(jax.ShapeDtypeStruct((rows // 4, depth), t) for t in (F32, BF16))

    def columns(array):
        return pl.BlockSpec((array.shape[0], db), lambda i, t, p: (0, i))

    return pl.pallas_call(
        functools.partial(grad_body, nb, rank, len(add)),
        out_shape=shapes,
        grid_spec=pltpu.PrefetchScalarGridSpec(
            num_scalar_prefetch=2,
            grid=(STEPS,),
            in_specs=[same_block(a) for a in (cot, nsq_a, nsq_b, magnitude)]
            + [IN_HBM] * 3
            + [columns(a) for a in add]
            + order_specs(deps),
            out_specs=[same_block(s) for s in shapes[:2]] + [columns(s) for s in shapes[2:]],
            scratch_shapes=[
                pltpu.VMEM((depth, cols), BF16),
                pltpu.VMEM((nb * rank, depth), BF16),
                pltpu.VMEM((nb * rank, cols), BF16),
                pltpu.VMEM((rows, cols), BF16),
                pltpu.VMEM((rows, 2 * nb * rank), BF16),
                pltpu.SemaphoreType.DMA((PARTS,)),
                pltpu.SemaphoreType.DMA((2 * nb,)),
            ],
        ),
        compiler_params=PARAMS,
        cost_estimate=COST,
        name="input_gradient",
    )(tenant, place, cot, nsq_a, nsq_b, magnitude, weight, down, up, *add, *deps)


def add_core_body(keep_ref, recv_ref, *refs):
    mine_ref, send_ref = refs[-2:]
    half = mine_ref.shape[0]
    mine_ref[...] = keep_ref[:half, :] + recv_ref[:half, :].astype(F32)
    send_ref[...] = (keep_ref[half:, :] + recv_ref[half:, :].astype(F32)).astype(BF16)


def add_core(keep, recv, deps):
    rows, size = keep.shape
    block = size // 2
    return pl.pallas_call(
        add_core_body,
        out_shape=(
            jax.ShapeDtypeStruct((rows // 2, size), F32),
            jax.ShapeDtypeStruct((rows // 2, size), BF16),
        ),
        grid=(2,),
        in_specs=[pl.BlockSpec((rows, block), lambda i: (0, i))] * 2 + order_specs(deps),
        out_specs=[pl.BlockSpec((rows // 2, block), lambda i: (0, i))] * 2,
        compiler_params=SMALL,
        cost_estimate=COST,
        name="add_core",
    )(keep, recv, *deps)


def add_x_body(groups, nz, place_ref, *refs):
    outs, total_ref = refs[-nz - 1 : -1], refs[-1]
    piece = outs[0].shape[0]
    z = place_ref[0]
    for g in range(groups):
        keep_ref, recv_ref = refs[2 * g : 2 * g + 2]
        first = pl.multiple_of(place_ref[3 + g] * piece, piece)
        total = keep_ref[...] + recv_ref[...].astype(F32)
        total_ref[pl.ds(first, keep_ref.shape[0]), :] = total
    for k in range(nz):
        at = pl.multiple_of(lax.rem(z + k, nz) * piece, piece)
        outs[k][...] = total_ref[pl.ds(at, piece), :].astype(outs[k].dtype)


def add_x(place, pairs, nz, deps):
    piece = BLOCK // 4
    size = pairs[0][0].shape[1]
    block = size // 2
    operands = [array for pair in pairs for array in pair]

    def spec(array):
        return pl.BlockSpec((array.shape[0], block), lambda i, p: (0, i))

    shapes = tuple(jax.ShapeDtypeStruct((piece, size), BF16 if k else F32) for k in range(nz))
    return pl.pallas_call(
        functools.partial(add_x_body, len(pairs), nz),
        out_shape=shapes,
        grid_spec=pltpu.PrefetchScalarGridSpec(
            num_scalar_prefetch=1,
            grid=(2,),
            in_specs=[spec(a) for a in operands] + order_specs(deps),
            out_specs=[spec(s) for s in shapes],
            scratch_shapes=[pltpu.VMEM((nz * piece, block), F32)],
        ),
        compiler_params=SMALL,
        cost_estimate=COST,
        name="add_x",
    )(place, *operands, *deps)


def add_z_body(*refs):
    total = refs[0][...]
    for ref in refs[1:-1]:
        total = total + ref[...].astype(F32)
    refs[-1][...] = total.astype(BF16)


def add_z(parts):
    return pl.pallas_call(
        add_z_body,
        out_shape=jax.ShapeDtypeStruct(parts[0].shape, BF16),
        in_specs=[pl.BlockSpec(memory_space=pltpu.VMEM)] * len(parts),
        compiler_params=SMALL,
        cost_estimate=COST,
        name="add_z",
    )(*parts)


def forward_body(nb, rank, nz, tenant_ref, place_ref, cot_ref, w_hbm, a_hbm, up_hbm, *refs):
    pieces = refs[: 2 * nz + 2]
    part_ref, dot_ref, low_ref = refs[-12:-9]
    w_ref, a_ref, up_ref, x_ref, acc_ref, low_acc, w_sem, sem, x_sem = refs[-9:]
    rows, cols = acc_ref.shape
    piece = BLOCK // 4
    depth = w_ref.shape[0]
    steps = STEPS
    db = depth // steps
    z, x, core, first = place_ref[0], place_ref[1], place_ref[2], place_ref[3]

    def each(h, act):
        at = pl.ds(h * depth // 2, depth // 2)
        for n in range(4 * nz):
            k, fx, fc = n // 4, (n // 2) % 2, n % 2
            src = pieces[2 * nz + fx] if fc else pieces[2 * k + fx]
            src = src.at[pl.ds(k * piece if fc else 0, piece), at]
            b = lax.rem(z + (nz - k), nz) - first

            @pl.when(jnp.logical_and(b >= 0, b < nb))
            def _():
                row = (b * 4 + (x ^ fx) * 2 + (core ^ fc)) * piece
                dst = pl.ds(pl.multiple_of(row, piece), piece)
                act(pltpu.make_async_copy(src, x_ref.at[dst, at], x_sem.at[h, n]))

    copies = factor_copies(tenant_ref, first, a_hbm, a_ref, sem, 0)
    late = factor_copies(tenant_ref, first, up_hbm, up_ref, sem, nb)
    each(0, lambda copy: copy.start())
    for copy in copies:
        copy.start()
    for i in range(AHEAD):
        weight_copy(w_hbm, w_ref, w_sem, i).start()
    each(1, lambda copy: copy.start())
    for copy in late:
        copy.start()
    acc_ref[...] = jnp.zeros_like(acc_ref)
    low_acc[...] = jnp.zeros_like(low_acc)
    for copy in copies:
        copy.wait()

    def block(i, carry):
        for h in range(2):

            @pl.when(i == h * (steps // 2))
            def _():
                each(h, lambda copy: copy.wait())

        weight_block(w_hbm, w_ref, w_sem, i, steps)
        at = pl.ds(pl.multiple_of(i * db, db), db)
        xs = x_ref[:, at]
        acc_ref[...] += jnp.dot(xs, w_ref[at, :], preferred_element_type=F32)
        low_acc[...] += lax.dot_general(a_ref[:, at], xs, LAST, preferred_element_type=F32)
        return carry

    lax.fori_loop(0, steps, block, 0)
    low = low_acc[...]
    owner = lax.broadcasted_iota(jnp.int32, low.shape, 0) // rank
    block_of = lax.broadcasted_iota(jnp.int32, low.shape, 1) // BLOCK
    low = jnp.where(owner == block_of, low, 0.0)
    low_ref[...] = jnp.sum(low.reshape(nb, rank, rows), axis=0)
    hi = low.astype(BF16).astype(F32)
    lowcat = jnp.concatenate([hi, low - hi], axis=0).T.astype(BF16)
    for copy in late:
        copy.wait()
    up = up_ref[...]
    up = jnp.concatenate([up, up], axis=0)
    for i in range(nb):
        here = slice(i * BLOCK, (i + 1) * BLOCK)
        part = acc_ref[here, :] + jnp.dot(lowcat[here, :], up, preferred_element_type=F32)
        part_ref[here, :] = part.astype(part_ref.dtype)
        product = part * cot_ref[here, :].astype(F32)
        dot_ref[i : i + 1, :] = jnp.sum(product, axis=0, keepdims=True)


def forward(tenant, place, weight, cot, down, up, pieces, nz, out_dtype, deps):
    depth, cols = weight.shape
    rows = cot.shape[0]
    nb = rows // BLOCK
    rank = down.shape[1]
    shapes = (
        jax.ShapeDtypeStruct((rows, cols), out_dtype),
        jax.ShapeDtypeStruct((nb, cols), F32),
        jax.ShapeDtypeStruct((rank, rows), F32),
    )
    return pl.pallas_call(
        functools.partial(forward_body, nb, rank, nz),
        out_shape=shapes,
        grid_spec=pltpu.PrefetchScalarGridSpec(
            num_scalar_prefetch=2,
            grid=(1,),
            in_specs=[same_block(cot)] + [IN_HBM] * (3 + len(pieces)) + order_specs(deps),
            out_specs=[same_block(s) for s in shapes],
            scratch_shapes=[
                pltpu.VMEM((depth, cols), BF16),
                pltpu.VMEM((nb * rank, depth), BF16),
                pltpu.VMEM((nb * rank, cols), BF16),
                pltpu.VMEM((rows, depth), BF16),
                pltpu.VMEM((rows, cols), F32),
                pltpu.VMEM((nb * rank, rows), F32),
                pltpu.SemaphoreType.DMA((PARTS,)),
                pltpu.SemaphoreType.DMA((2 * nb,)),
                pltpu.SemaphoreType.DMA((2, 4 * nz)),
            ],
        ),
        compiler_params=PARAMS,
        cost_estimate=COST,
        name="forward",
    )(tenant, place, cot, weight, down, up, *pieces, *deps)


def shards(inputs, weight, adapter_down_factors, adapter_up_factors, magnitude, cotangent, tenant):
    col_count, row_count = lax.axis_size("col"), lax.axis_size("row")
    nz = col_count // 4
    down, up = adapter_down_factors, adapter_up_factors
    tenant_number, rank, depth = down.shape
    cols = weight.shape[1]
    tokens = tenant.shape[0]
    nblk = tokens // BLOCK
    rows_row = tokens // row_count
    blocks_mine = rows_row // BLOCK
    col, row = lax.axis_index("col"), lax.axis_index("row")
    z, x, core = col >> 2, (col >> 1) & 1, col & 1

    def move(value, dz, fx, fc):
        perm = []
        for source in range(col_count):
            sz, sx, sc = source // 4, (source // 2) % 2, source % 2
            perm.append((source, ((sz + dz) % nz) * 4 + (sx ^ fx) * 2 + (sc ^ fc)))
        return lax.ppermute(value, "col", perm)

    def swap(value):
        return lax.ppermute(value, "row", [(0, 1), (1, 0)])

    def place(*firsts):
        return jnp.stack([z, x, core, *firsts]).astype(jnp.int32)

    pair = row_count == 2

    def once(value, other):
        return lax.optimization_barrier((value, other))[0]

    along_z = [inputs] + [move(inputs, k, 0, 0) for k in range(1, nz)]
    along_x = {0: move(inputs, 0, 1, 0)}

    def other_x(k, after):
        along_z[k] = once(along_z[k], after)
        along_x[k] = move(along_z[k], 0, 1, 0)

    def other_core(part):
        return move(jnp.concatenate(part, axis=0), 0, 0, 1)

    nsq = partial_norms(tenant, weight, down, up)
    if pair:
        nsq_a, nsq_b = nsq, swap(once(nsq, along_x[0]))
        firsts = [row * blocks_mine, (1 - row) * blocks_mine]
        cots = [cotangent, swap(cotangent)]
    else:
        nsq_a, nsq_b = lax.psum(nsq, "row"), jnp.zeros_like(nsq)
        firsts = [0 * row]
        cots = [lax.all_gather(cotangent, "row", axis=0, tiled=True)]
    places = [place(first) for first in firsts]

    def gradient(g, add, deps):
        return input_gradient(
            tenant, places[g], cots[g], nsq_a, nsq_b, magnitude, weight, down, up, add, deps
        )

    def cross_core(made, deps):
        return add_core(made[2], move(made[3], 0, 0, 1), deps)

    def cross_x(pairs, deps):
        mine, *away = add_x(place(*firsts), pairs, nz, deps)
        return [mine] + [move(block, k + 1, 0, 0) for k, block in enumerate(away)]

    def across_x(made):
        return made[0], move(made[1], 0, 1, 0)

    if pair:
        ours = gradient(0, [], [cots[1]])
        for k in [nz - 1] + list(range(1, nz - 1)):
            other_x(k, ours[0])
        core_z = other_core(along_z)
        theirs = gradient(1, [ours[2], move(ours[3], 0, 0, 1)], [core_z])
        near = across_x(theirs[4:])
        along_x = [along_x[k] for k in range(nz)]
        along_x[nz - 2] = once(along_x[nz - 2], theirs[0])
        core_x = other_core(along_x)
        far = cross_core(theirs, [core_x])
        pieces = [piece for both in zip(along_z, along_x) for piece in both] + [core_z, core_x]

        def project(g, out_dtype, deps):
            return forward(
                tenant, places[g], weight, cots[g], down, up, pieces, nz, out_dtype, deps
            )

        away, dots_away, low_away = project(1, BF16, [far[0]])
        arrived = swap(away)
        finals = cross_x([near, across_x(far)], [dots_away])
        part, dots_here, low_here = project(0, F32, [finals[0]])
        dots = jnp.concatenate([dots_here, dots_away], axis=0)
        low = jnp.concatenate([low_here, low_away], axis=1)
        new_dots = swap(once(dots, finals[nz // 2]))
        new_low = swap(once(low, finals[nz - 1]))
        dots = dots + jnp.roll(new_dots, blocks_mine, axis=0)
        low = low + jnp.roll(new_low, rows_row, axis=1)
        parts = [ours, theirs]
    else:
        ours = gradient(0, [], [])
        near = across_x(cross_core(ours, []))
        for k in range(1, nz):
            other_x(k, inputs)
        along_x = [along_x[k] for k in range(nz)]
        pieces = [piece for both in zip(along_z, along_x) for piece in both]
        pieces += [other_core(along_z), other_core(along_x)]
        part, dots, low = forward(
            tenant, places[0], weight, cots[0], down, up, pieces, nz, F32, []
        )
        finals = cross_x([near], [])
        low, dots = lax.psum((low, dots), "row")
        parts = [ours]

    scales = jnp.concatenate([group[0] for group in parts], axis=0)

    tenants = jnp.arange(tenant_number, dtype=jnp.int32)
    block_tenant = tenant.reshape(nblk, BLOCK)[:, 0]
    size = nblk // len(parts)
    owners = jnp.concatenate(
        [lax.dynamic_slice_in_dim(block_tenant, first, size, 0) for first in firsts]
    )
    low = low.astype(BF16)
    grad_b = 0.0
    for g, group in enumerate(parts):
        owner = jnp.repeat(owners[g * size : (g + 1) * size], BLOCK)
        mine = low[:, g * size * BLOCK : (g + 1) * size * BLOCK]
        wide = jnp.where((tenants[:, None] == owner[None, :])[:, None, :], mine[None], 0)
        wide = wide.reshape(tenant_number * rank, size * BLOCK)
        grad_b = grad_b + jnp.dot(wide, group[1], preferred_element_type=F32)
    grad_b = grad_b.reshape(tenant_number, rank, cols)
    hit = (tenants[:, None] == owners[None, :])[:, :, None]
    terms = jnp.where(hit, (dots * scales)[None], 0.0)
    grad_m = 0.0
    for g in range(len(parts)):
        group = terms[:, g * size : (g + 1) * size]
        grad_m = grad_m + functools.reduce(jnp.add, [group[:, i] for i in range(size)])
    grad_inputs = add_z([once(finals[0], grad_b)] + finals[1:])
    if pair:
        pre = part + arrived.astype(F32)
        scale_mine = parts[0][0]
    else:
        pre = lax.psum_scatter(part, "row", scatter_dimension=0, tiled=True)
        scale_mine = lax.dynamic_slice_in_dim(scales, row * blocks_mine, blocks_mine, 0)
    output = (pre.reshape(blocks_mine, BLOCK, cols) * scale_mine[:, None, :]).astype(BF16)
    output = output.reshape(rows_row, cols)
    return (output, grad_inputs, grad_b, grad_m / magnitude)


def solution(mesh):
    return jax.shard_map(
        shards,
        mesh=mesh,
        in_specs=(
            P("col", "row"),
            P("row", "col"),
            P(None, None, "row"),
            P(None, None, "col"),
            P(None, "col"),
            P("row", "col"),
            P(),
        ),
        out_specs=(P("row", "col"), P("col", "row"), P(None, None, "col"), P(None, "col")),
        check_vma=False,
    )
```
